256 devices in a mesh: section: 16 (over z, x_hi), dp: 16 (over y, x_lo, core).
Axes of the slice: x: 4 (x_hi: 2, x_lo: 2; x = x_hi * 2 + x_lo), y: 4, z: 8, core: 2. Of those that a mesh axis runs over, the one named last changes fastest.
Arguments:
- down_input: bfloat16 [2, 1024, 1024], P(None, 'dp')
- up_input: bfloat16 [2, 1024, 1024], P(None, 'dp')
- down_cot: bfloat16 [2, 1024, 1024], P(None, 'dp'), may hold values from -0.059814453 to 0.059814453
- up_cot: bfloat16 [2, 1024, 1024], P(None, 'dp'), may hold values from -0.059814453 to 0.059814453
- weight: bfloat16 [16, 1024, 1024], P('section', 'dp'), may hold values from -0.1875 to 0.1875
- gain: bfloat16 [16, 1024], P('section', 'dp'), may hold values from 0.5 to 2
Outputs:
- grad_weight: float32 [16, 1024, 1024], P('section', 'dp')
- grad_gain: float32 [16, 1024], P('section', 'dp')
The draws below stay inside these ranges and needn't reach their ends.
All inputs are finite; a program needn't handle non-finite values.
Results may differ from the reference program's by a relative error of at most 0.035.
Values may be sent and summed in bfloat16 or wider, within the bound.
A program may use at most 64 MiB of HBM per device.

```python
import math
import jax
import jax.numpy as jnp
from jax import lax

D = 1024
MB = 2
LAYERS = 16
ROWS = 1024


def scaled_rows(base_rows, key):
    row_key, column_key = jax.random.split(key)
    row_scale = jnp.exp(jax.random.uniform(row_key, (MB, ROWS, 1), jnp.float32, math.log(0.3), math.log(3.0)))
    column_scale = jnp.exp(jax.random.uniform(column_key, (1, 1, D), jnp.float32, math.log(0.5), math.log(2.0)))
    return (base_rows * row_scale * column_scale).astype(jnp.bfloat16)


def draw_down_input(key, part):
    key = jax.random.fold_in(key, 11)
    base_key, scale_key = jax.random.split(key)
    base_rows = jnp.clip(jax.random.normal(base_key, (MB, ROWS, D), jnp.float32), -6.0, 6.0)
    return scaled_rows(base_rows, scale_key)


def draw_up_input(key, part):
    key = jax.random.fold_in(key, 23)
    base_key, scale_key = jax.random.split(key)
    base_rows = jnp.clip(jax.random.normal(base_key, (MB, ROWS, D), jnp.float32), -6.0, 6.0)
    return scaled_rows(base_rows, scale_key)


def level_of(key, shape, cuts, least, top_value):
    loudness = 1.0
    for position, blocks in cuts:
        draws = jax.random.uniform(jax.random.fold_in(jax.random.fold_in(key, 6), position), (blocks,), jnp.float32, least / len(cuts), top_value / len(cuts))
        loudness = loudness * jnp.repeat(jnp.exp(draws), shape[position] // blocks).reshape((-1,) + (1,) * (len(shape) - 1 - position))
    return loudness


def gaussian(own_key, extent, spread, most, shards=(), dtype=jnp.bfloat16):
    result = jax.random.normal(own_key, extent, jnp.float32) * spread
    if len(shards) > 0:
        result = level_of(own_key, extent, shards, -0.22, 0.18) * result
    return jnp.clip(result, min=-most, max=most).astype(dtype)


def setup_inputs(seed: int = 0) -> dict:
    keys = jax.random.split(jax.random.key(seed), 7)
    return {
        "down_input": draw_down_input(jax.random.fold_in(keys[6], 71), 0),
        "up_input": draw_up_input(jax.random.fold_in(keys[6], 71), 0),
        "down_cot": gaussian(keys[2], (MB, ROWS, D), 0.01, 0.059814453, ((1, 16),)),
        "up_cot": gaussian(keys[3], (MB, ROWS, D), 0.01, 0.059814453, ((1, 16),)),
        "weight": gaussian(keys[4], (LAYERS, D, D), D ** -0.5, 0.1875, ((0, 16), (1, 16))),
        "gain": jnp.clip(jnp.exp(math.log(2.0) - 1.3862944 * jax.random.uniform(keys[5], (LAYERS, D), jnp.float32) ** level_of(keys[5], (LAYERS, D), ((0, 16), (1, 16)), -0.2, 0.2)), 0.5, 2.0).astype(jnp.bfloat16),
    }


EPSILON = 1e-05
CUBIC = 0.044715
SLOPE = math.sqrt(2.0 / math.pi)

def gelu_pair(projected):
    argument = SLOPE * (projected + CUBIC * projected * projected * projected)
    tangent = jnp.tanh(argument)
    gelu_value = 0.5 * projected * (1.0 + tangent)
    gelu_slope = 0.5 * (1.0 + tangent) + 0.5 * projected * (1.0 - tangent * tangent) * SLOPE * (1.0 + 3.0 * CUBIC * projected * projected)
    return (gelu_value, gelu_slope)

def layer_forward(layer_input, gain_row, weight_matrix):
    widened = layer_input.astype(jnp.float32)
    inverse = lax.rsqrt(lax.optimization_barrier(jnp.mean(widened * widened, axis=-1, keepdims=True)) + EPSILON)
    normed = (widened * inverse * gain_row.astype(jnp.float32)).astype(jnp.bfloat16)
    projected = jnp.dot(normed, weight_matrix, preferred_element_type=jnp.float32)
    gelu_value, _ = gelu_pair(projected)
    return ((widened + gelu_value).astype(jnp.bfloat16), normed, projected, inverse)

def layer_backward(cot_rows, layer_input, normed, projected, inverse, gain_row, weight_matrix):
    _, gelu_slope = gelu_pair(projected)
    grad_proj = (cot_rows.astype(jnp.float32) * gelu_slope).astype(jnp.bfloat16)
    weight_term = lax.dot_general(normed, grad_proj, (((0,), (0,)), ((), ())), preferred_element_type=jnp.float32)
    grad_normed = lax.dot_general(grad_proj, weight_matrix, (((1,), (1,)), ((), ())), preferred_element_type=jnp.float32)
    widened = layer_input.astype(jnp.float32)
    gain_term = lax.optimization_barrier(jnp.sum(grad_normed * widened * inverse, axis=0))
    scaled_grad = gain_row.astype(jnp.float32) * grad_normed
    grad_input = inverse * scaled_grad - widened * inverse * inverse * inverse * lax.optimization_barrier(jnp.mean(scaled_grad * widened, axis=-1, keepdims=True))
    return ((cot_rows.astype(jnp.float32) + grad_input).astype(jnp.bfloat16), weight_term, gain_term)

def reference(down_input, up_input, down_cot, up_cot, weight, gain):
    micro_inputs = jnp.concatenate([down_input, up_input], axis=0)
    micro_cots = jnp.concatenate([down_cot, up_cot], axis=0)

    def one_batch(running, batch_pair):
        inputs_one, cot_one = batch_pair

        def forward_step(layer_input, layer_params):
            weight_matrix, gain_row = layer_params
            output_rows, normed, projected, inverse = layer_forward(layer_input, gain_row, weight_matrix)
            return (output_rows, (layer_input, normed, projected, inverse))
        _, saved_rows = lax.scan(forward_step, inputs_one, (weight, gain))

        def backward_step(cot_rows, layer_items):
            weight_matrix, gain_row, layer_input, normed, projected, inverse = layer_items
            earlier, weight_term, gain_term = layer_backward(cot_rows, layer_input, normed, projected, inverse, gain_row, weight_matrix)
            return (earlier, (weight_term, gain_term))
        _, (weight_terms, gain_terms) = lax.scan(backward_step, cot_one, (weight, gain) + saved_rows, reverse=True)
        return ((running[0] + weight_terms, running[1] + gain_terms), None)
    initial = (jnp.zeros(weight.shape, jnp.float32), jnp.zeros(gain.shape, jnp.float32))
    (grad_weight, grad_gain), _ = lax.scan(one_batch, initial, (micro_inputs, micro_cots))
    return (grad_weight, grad_gain)
```

```python
import functools
import math

import jax
import jax.numpy as jnp
from jax import lax
from jax.experimental import pallas as pl
from jax.experimental.pallas import tpu as pltpu
from jax.sharding import PartitionSpec as P

EPSILON = 1e-05
CUBIC = 0.044715
SLOPE = math.sqrt(2.0 / math.pi)
MESH = pl.DeviceIdType.MESH
FIRST_PAIR = 8
D = 1024
HALF = D // 2
MB_ROWS = 32


def kernel(
    down_in, up_in, down_cot, up_cot, w_in, g_in, gw_out, gg_out,
    w, part, r0, r1a, r1b, s1a, s1b, r2a, r2b, zres, zsend, h, du, xs, sl, rinv, xo, do, cot,
    zx_s, zx_r, a1_s, a1_r, b1_s, b1_r, a2_s, a2_r, b2_s, b2_r, d_s, d_r,
    fx_s, fx_r, bx_s, bx_r, r0_s, r0_r, r1a_s, r1a_r, r1b_s, r1b_r, r2a_s, r2a_r, r2b_s, r2b_r,
    zr_s, zr_r,
):
    sec, dp = lax.axis_index("section"), lax.axis_index("dp")
    z, xh = sec // 2, sec % 2
    y, xl, c = dp // 4, (dp // 2) % 2, dp % 2
    x = xh * 2 + xl
    other = 1 - c

    def at(ax, ay, az, ac):
        return (az * 2 + ax // 2, ay * 4 + (ax % 2) * 2 + ac)

    def xdev(k):
        return at((x + k) % 4, y, z, c)

    def ydev(k):
        return at(x, (y + k) % 4, z, c)

    def zdev(k):
        return at(x, y, (z + 8 + k) % 8, c)

    sibling = at(x, y, z, other)
    pair = z >= FIRST_PAIR
    single = z < FIRST_PAIR
    ispair = pair.astype(jnp.int32) if FIRST_PAIR < 8 else 0
    odd = (z % 2) * ispair
    planes = 1 + ispair
    layers = 2 * planes
    slots = 4 // planes
    own_p = odd
    own_l = 2 * own_p + xh
    zpartner = at(x, y, z + 1 - 2 * (z % 2), c)

    barrier = pltpu.get_barrier_semaphore()
    peers = [sibling] + [xdev(k) for k in (1, 2, 3)] + [ydev(k) for k in (1, 2, 3)]
    peers += [zdev(1), zdev(-1)]
    if FIRST_PAIR < 8:
        peers += [zdev(2), zdev(-2)]
    for peer in peers:
        pl.semaphore_signal(barrier, inc=1, device_id=peer, device_id_type=MESH)

    def send(src, dst, ss, rs, to):
        return pltpu.make_async_remote_copy(
            src_ref=src, dst_ref=dst, send_sem=ss, recv_sem=rs, device_id=to, device_id_type=MESH
        )

    eye = lax.broadcasted_iota(jnp.int32, (64, 64), 0) == lax.broadcasted_iota(jnp.int32, (64, 64), 1)
    gain_col = jnp.sum(jnp.where(eye, g_in[...].astype(jnp.float32), 0.0), axis=1, keepdims=True)
    w[own_l, y, xl, c] = (w_in[0].astype(jnp.float32) * gain_col).astype(jnp.bfloat16)
    pl.semaphore_wait(barrier, len(peers))

    A, B, ALL = pl.ds(0, HALF), pl.ds(HALF, HALF), pl.ds(0, D)

    def blk(p, bx, by, cols):
        return w.at[2 * p + bx // 2, by, bx % 2, c, :, cols]

    def row_of(p, by):
        return w.at[pl.ds(2 * p, 2), by, :, c, :, A]

    def col_of(p, bx):
        return w.at[2 * p + bx // 2, :, bx % 2, c, :, B]

    def zx():
        ref = w.at[own_l, y, xl, c]
        return send(ref, ref, zx_s, zx_r, zpartner)

    def zx_other():
        ref = w.at[2 * (1 - own_p) + xh, y, xl, c]
        return send(ref, ref, zx_s, zx_r, zpartner)

    def a1(p, k):
        ref = blk(p, x, y, A)
        return send(ref, ref, a1_s.at[p, k - 1], a1_r.at[p, k - 1], xdev(k))

    def b1(p, k):
        ref = blk(p, x, y, B)
        return send(ref, ref, b1_s.at[p, k - 1], b1_r.at[p, k - 1], ydev(k))

    def a2(p, src, k):
        ref = blk(p, (x - src + 4) % 4, y, A)
        return send(ref, ref, a2_s.at[p, src, k - 1], a2_r.at[p, k - 1], ydev(k))

    def b2(p, src, k):
        ref = blk(p, x, (y - src + 4) % 4, B)
        return send(ref, ref, b2_s.at[p, src, k - 1], b2_r.at[p, k - 1], xdev(k))

    def a2_wait(p, k):
        ref = row_of(p, (y - k + 4) % 4)
        return send(ref, ref, a2_s.at[p, 0, 0], a2_r.at[p, k - 1], sibling)

    def b2_wait(p, k):
        ref = col_of(p, (x - k + 4) % 4)
        return send(ref, ref, b2_s.at[p, 0, 0], b2_r.at[p, k - 1], sibling)

    def d_own(p):
        ref = blk(p, x, y, ALL)
        return send(ref, ref, d_s.at[p, 0], d_r.at[p], sibling)

    def d_a1(p, k):
        ref = blk(p, (x - k + 4) % 4, y, A)
        return send(ref, ref, d_s.at[p, k], d_r.at[p], sibling)

    def d_b1(p, k):
        ref = blk(p, x, (y - k + 4) % 4, B)
        return send(ref, ref, d_s.at[p, 3 + k], d_r.at[p], sibling)

    def d_a2(p, k):
        ref = row_of(p, (y - k + 4) % 4)
        return send(ref, ref, d_s.at[p, 6 + k], d_r.at[p], sibling)

    def d_b2(p, k):
        ref = col_of(p, (x - k + 4) % 4)
        return send(ref, ref, d_s.at[p, 9 + k], d_r.at[p], sibling)

    def d_wait(p):
        ref = w.at[pl.ds(2 * p, 2), :, :, other]
        return send(ref, ref, d_s.at[p, 0], d_r.at[p], sibling)

    K = (1, 2, 3)
    if FIRST_PAIR < 8:

        @pl.when(pair)
        def _():
            zx().start()

    def gather_start(i, carry):
        p = (own_p + i) % planes

        @pl.when(i > 0)
        def _():
            zx_other().wait_recv()

        for k in K:
            a1(p, k).start()
            b1(p, k).start()
        for k in K:
            a2(p, 0, k).start()
            b2(p, 0, k).start()
        d_own(p).start()
        return carry

    def gather_mid(i, carry):
        p = (own_p + i) % planes
        for src in (1, 3, 2):
            a1(p, src).wait_recv()
            for k in K:
                a2(p, src, k).start()
            d_a1(p, src).start()
            b1(p, src).wait_recv()
            for k in K:
                b2(p, src, k).start()
            d_b1(p, src).start()
        return carry

    def gather_end(i, carry):
        p = (own_p + i) % planes
        for k in (1, 3, 2):
            a2_wait(p, k).wait_recv()
            d_a2(p, k).start()
            b2_wait(p, k).wait_recv()
            d_b2(p, k).start()
        return carry

    def gather_wait(i, carry):
        d_wait((own_p + i) % planes).wait_recv()
        return carry

    lax.fori_loop(0, planes, gather_start, 0)

    first = z < (2 if FIRST_PAIR == 0 else 1)
    last = z >= (7 if FIRST_PAIR == 8 else 6)

    def load_rows(dst, down, up):
        for slot in range(4):
            def take(j, slot=slot):
                b, half = j // 2, j % 2
                for ref, cond in ((down, xh == 0), (up, xh == 1)):

                    @pl.when(cond)
                    def _(ref=ref):
                        dst[slot] = ref[b, pl.ds(pl.multiple_of(half * MB_ROWS, MB_ROWS), MB_ROWS), :]

            if FIRST_PAIR == 8:
                take(slot)
            elif slot < 2:
                take((2 * slot + odd) if FIRST_PAIR == 0 else slot * planes + odd)
            else:

                @pl.when(single)
                def _(slot=slot):
                    take(slot)

    @pl.when(first)
    def _():
        load_rows(xs.at[0], down_in, up_in)

    @pl.when(last)
    def _():
        load_rows(cot, down_cot, up_cot)

    if FIRST_PAIR < 8:
        h[...] = jnp.zeros_like(h)
        du[...] = jnp.zeros_like(du)

    lax.fori_loop(0, planes, gather_mid, 0)
    lax.fori_loop(0, planes, gather_end, 0)
    lax.fori_loop(0, planes, gather_wait, 0)

    if FIRST_PAIR == 8:

        def f_route(j):
            return zdev(1), j

        def b_route(j):
            return zdev(-1), j

    else:
        to_pair = (z == FIRST_PAIR - 1).astype(jnp.int32)
        from_pair = ((z // 2) * 2 == FIRST_PAIR).astype(jnp.int32)

        def f_route(j):
            step = ispair * 2 + (1 - ispair) * (1 + to_pair * (j % 2))
            slot = j - to_pair * (j - j // 2)
            return zdev(step), slot

        def b_route(j):
            step = ispair * (2 + from_pair * (odd - 1)) + (1 - ispair)
            slot = j + from_pair * (j + odd)
            return zdev(-step), slot

    def fx(j):
        to, slot = f_route(j)
        return send(xo.at[j], xs.at[0, slot], fx_s.at[j], fx_r.at[slot], to)

    def fx_wait(j):
        return send(xo.at[j], xs.at[0, j], fx_s.at[j], fx_r.at[j], sibling)

    def bx(j):
        to, slot = b_route(j)
        return send(do.at[j], cot.at[slot], bx_s.at[j], bx_r.at[slot], to)

    def bx_wait(j):
        return send(do.at[j], cot.at[j], bx_s.at[j], bx_r.at[j], sibling)

    def forward(j, carry):
        @pl.when(jnp.logical_not(first))
        def _():
            fx_wait(j).wait_recv()

        rows = pl.ds(pl.multiple_of(j * MB_ROWS, MB_ROWS), MB_ROWS)

        def layer(l, carry):
            xf = xs[l, j].astype(jnp.float32)
            r = lax.rsqrt(jnp.mean(xf * xf, axis=-1, keepdims=True) + EPSILON)
            normed = (xf * r).astype(jnp.bfloat16)
            h[l, rows, :] = normed
            rinv[l, j] = jnp.broadcast_to(r, (MB_ROWS, 128))
            u = jnp.dot(normed, w[l].reshape(D, D), preferred_element_type=jnp.float32)
            u2 = u * u
            t = jnp.tanh(SLOPE * (u + CUBIC * u2 * u))
            nxt = (xf + 0.5 * u * (1.0 + t)).astype(jnp.bfloat16)

            @pl.when(l < layers - 1)
            def _():
                xs[l + 1, j] = nxt

            @pl.when(l == layers - 1)
            def _():
                xo[j] = nxt

                @pl.when(jnp.logical_not(last))
                def _():
                    fx(j).start()

            sl[l, j] = 0.5 * (1.0 + t) + 0.5 * u * (1.0 - t * t) * SLOPE * (1.0 + 3.0 * CUBIC * u2)
            return carry

        return lax.fori_loop(0, layers, layer, carry)

    lax.fori_loop(0, slots, forward, 0)

    def backward(j, carry):
        @pl.when(jnp.logical_not(last))
        def _():
            bx_wait(j).wait_recv()

        rows = pl.ds(pl.multiple_of(j * MB_ROWS, MB_ROWS), MB_ROWS)

        def layer(i, carry):
            l = layers - 1 - i
            df = cot[j].astype(jnp.float32)
            grad = (df * sl[l, j]).astype(jnp.bfloat16)
            du[l, rows, :] = grad

            @pl.when(jnp.logical_not(jnp.logical_and(first, l == 0)))
            def _():
                a = lax.dot_general(
                    grad, w[l].reshape(D, D), (((1,), (1,)), ((), ())), preferred_element_type=jnp.float32
                )
                r = rinv[l, j][:, 0:1]
                xr = xs[l, j].astype(jnp.float32) * r
                new = (df + r * (a - xr * jnp.mean(a * xr, axis=-1, keepdims=True))).astype(jnp.bfloat16)

                @pl.when(l > 0)
                def _():
                    cot[j] = new

                @pl.when(l == 0)
                def _():
                    do[j] = new
                    bx(j).start()

            return carry

        return lax.fori_loop(0, layers, layer, carry)

    lax.fori_loop(0, slots, backward, 0)

    def e0(l):
        return send(part.at[l, :, :, other], r0.at[l], r0_s.at[l], r0_r.at[l], sibling)

    def e1a(l, k):
        return send(
            r0.at[l, (y + k) % 4, :, :, A], r1a.at[l, k - 1], r1a_s.at[l, k - 1], r1a_r.at[l, k - 1], ydev(k)
        )

    def e1b(l, k):
        return send(
            r0.at[l, :, (x + k) % 2, :, B], r1b.at[l // 2, k - 1], r1b_s.at[l, k - 1], r1b_r.at[l // 2, k - 1], xdev(k)
        )

    def e2a(l, k):
        return send(
            s1a.at[l, (x + k) % 2], r2a.at[l // 2, k - 1], r2a_s.at[l, k - 1], r2a_r.at[l // 2, k - 1], xdev(k)
        )

    def e2b(l, k):
        p = l // 2
        return send(
            s1b.at[p, (y + k) % 4], r2b.at[p, k - 1], r2b_s.at[p, k - 1], r2b_r.at[p, k - 1], ydev(k)
        )

    def for_x(l, act):
        for k in K:

            @pl.when(((x + k) % 4) // 2 == l % 2)
            def _(k=k):
                act(k)

    def mine(l):
        return xh == l % 2

    def f32(v):
        return v.astype(jnp.float32)

    def reduce_a(i, carry):
        l = layers - 1 - i
        g = lax.dot_general(
            h[l], du[l], (((0,), (0,)), ((), ())), preferred_element_type=jnp.float32
        )
        part[l] = g.astype(jnp.bfloat16).reshape(4, 2, 2, 64, D)
        e0(l).start()
        return carry

    def reduce_b(i, carry):
        l = layers - 1 - i
        e0(l).wait_recv()
        r0[l] = (f32(r0[l]) + f32(part[l, :, :, c])).astype(jnp.bfloat16)
        for k in K:
            e1a(l, k).start()
        for_x(l, lambda k: e1b(l, k).start())
        return carry

    def reduce_c(i, carry):
        l = layers - 1 - i
        for k in K:
            e1a(l, k).wait_recv()
        s1a[l] = (f32(r0[l, y, :, :, 0:HALF]) + f32(r1a[l, 0]) + f32(r1a[l, 1]) + f32(r1a[l, 2])).astype(jnp.bfloat16)
        for_x(l, lambda k: e2a(l, k).start())

        @pl.when(mine(l))
        def _():
            p = l // 2
            for k in K:
                e1b(l, k).wait_recv()
            s1b[p] = (f32(r0[l, :, xl, :, HALF:D]) + f32(r1b[p, 0]) + f32(r1b[p, 1]) + f32(r1b[p, 2])).astype(jnp.bfloat16)
            for k in K:
                e2b(l, k).start()

        return carry

    def zr():
        return send(zsend, zres, zr_s, zr_r, zpartner)

    def total(l):
        p = l // 2
        for k in K:
            e2a(l, k).wait_recv()
            e2b(l, k).wait_recv()
        left = f32(s1a[l, xl]) + f32(r2a[p, 0]) + f32(r2a[p, 1]) + f32(r2a[p, 2])
        right = f32(s1b[p, y]) + f32(r2b[p, 0]) + f32(r2b[p, 1]) + f32(r2b[p, 2])
        return left, right

    lax.fori_loop(0, layers, reduce_a, 0)
    lax.fori_loop(0, layers, reduce_b, 0)
    lax.fori_loop(0, layers, reduce_c, 0)

    if FIRST_PAIR < 8:

        @pl.when(pair)
        def _():
            left, right = total(2 * (1 - own_p) + xh)
            zsend[:, 0:HALF] = left
            zsend[:, HALF:D] = right
            zr().start()

    left, right = total(own_l)
    gw_out[0, :, 0:HALF] = left
    gw_out[0, :, HALF:D] = right
    if FIRST_PAIR < 8:

        @pl.when(pair)
        def _():
            zr().wait_recv()
            gw_out[0] = gw_out[0] + zres[...]

    full = gw_out[0]
    per_row = jnp.sum(full * w_in[0].astype(jnp.float32), axis=1, keepdims=True)
    gg_out[...] = jnp.sum(jnp.where(eye, per_row, 0.0), axis=0, keepdims=True)
    gw_out[0] = full * gain_col

    if FIRST_PAIR < 8:

        @pl.when(pair)
        def _():
            zx().wait_send()
            zr().wait_send()

    def drain_gather(i, carry):
        p = (own_p + i) % planes
        for k in K:
            a1(p, k).wait_send()
            b1(p, k).wait_send()
            for src in range(4):
                a2(p, src, k).wait_send()
                b2(p, src, k).wait_send()
            d_a1(p, k).wait_send()
            d_b1(p, k).wait_send()
            d_a2(p, k).wait_send()
            d_b2(p, k).wait_send()
        d_own(p).wait_send()
        return carry

    lax.fori_loop(0, planes, drain_gather, 0)

    def drain_relay(j, carry):
        @pl.when(jnp.logical_not(last))
        def _():
            fx(j).wait_send()

        @pl.when(jnp.logical_not(first))
        def _():
            bx(j).wait_send()

        return carry

    lax.fori_loop(0, slots, drain_relay, 0)

    def drain_reduce(l, carry):
        e0(l).wait_send()
        for k in K:
            e1a(l, k).wait_send()
        for_x(l, lambda k: e1b(l, k).wait_send())
        for_x(l, lambda k: e2a(l, k).wait_send())

        @pl.when(mine(l))
        def _():
            for k in K:
                e2b(l, k).wait_send()

        return carry

    lax.fori_loop(0, layers, drain_reduce, 0)


def shards(down_input, up_input, down_cot, up_cot, weight, gain):
    nl = 2 if FIRST_PAIR == 8 else 4
    np_ = nl // 2
    bf, f4 = jnp.bfloat16, jnp.float32
    dma = pltpu.SemaphoreType.DMA
    scratch = [
        pltpu.VMEM((nl, 4, 2, 2, 64, D), bf),
        pltpu.VMEM((nl, 4, 2, 2, 64, D), bf),
        pltpu.VMEM((nl, 4, 2, 64, D), bf),
        pltpu.VMEM((nl, 3, 2, 64, HALF), bf),
        pltpu.VMEM((np_, 3, 4, 64, HALF), bf),
        pltpu.VMEM((nl, 2, 64, HALF), bf),
        pltpu.VMEM((np_, 4, 64, HALF), bf),
        pltpu.VMEM((np_, 3, 64, HALF), bf),
        pltpu.VMEM((np_, 3, 64, HALF), bf),
        pltpu.VMEM((64, D), f4),
        pltpu.VMEM((64, D), f4),
        pltpu.VMEM((nl, 4 * MB_ROWS, D), bf),
        pltpu.VMEM((nl, 4 * MB_ROWS, D), bf),
        pltpu.VMEM((nl, 4, MB_ROWS, D), bf),
        pltpu.VMEM((nl, 4, MB_ROWS, D), f4),
        pltpu.VMEM((nl, 4, MB_ROWS, 128), f4),
        pltpu.VMEM((4, MB_ROWS, D), bf),
        pltpu.VMEM((4, MB_ROWS, D), bf),
        pltpu.VMEM((4, MB_ROWS, D), bf),
        dma, dma,
        dma((np_, 3)), dma((np_, 3)), dma((np_, 3)), dma((np_, 3)),
        dma((np_, 4, 3)), dma((np_, 3)), dma((np_, 4, 3)), dma((np_, 3)),
        dma((np_, 13)), dma((np_,)),
        dma((4,)), dma((4,)), dma((4,)), dma((4,)),
        dma((nl,)), dma((nl,)),
        dma((nl, 3)), dma((nl, 3)), dma((nl, 3)), dma((np_, 3)),
        dma((nl, 3)), dma((np_, 3)), dma((np_, 3)), dma((np_, 3)),
        dma, dma,
    ]
    vmem = pl.BlockSpec(memory_space=pltpu.VMEM)
    return pl.pallas_call(
        kernel,
        out_shape=(
            jax.ShapeDtypeStruct((1, 64, D), f4),
            jax.ShapeDtypeStruct((1, 64), f4),
        ),
        in_specs=[vmem] * 6,
        out_specs=(vmem, vmem),
        scratch_shapes=scratch,
        compiler_params=pltpu.CompilerParams(
            collective_id=0, has_side_effects=True, vmem_limit_bytes=56 * 1024 * 1024
        ),
    )(down_input, up_input, down_cot, up_cot, weight, gain)


def solution(mesh):
    rows = P(None, "dp", None)
    return jax.shard_map(
        shards,
        mesh=mesh,
        in_specs=(rows, rows, rows, rows, P("section", "dp", None), P("section", "dp")),
        out_specs=(P("section", "dp", None), P("section", "dp")),
        check_vma=False,
    )
```

```python
import functools
import math

import jax
import jax.numpy as jnp
from jax import lax
from jax.experimental import pallas as pl
from jax.experimental.pallas import tpu as pltpu
from jax.sharding import PartitionSpec as P

EPSILON = 1e-05
CUBIC = 0.044715
SLOPE = math.sqrt(2.0 / math.pi)
MESH = pl.DeviceIdType.MESH
FIRST_PAIR = 2
D = 1024
HALF = D // 2
MB_ROWS = 32


def kernel(
    down_in, up_in, down_cot, up_cot, w_in, g_in, gw_out, gg_out,
    w, part, r0, r1a, r1b, s1a, s1b, r2a, r2b, zres, zsend, h, du, xs, sl, rinv, xo, do, cot,
    zx_s, zx_r, a1_s, a1_r, b1_s, b1_r, a2_s, a2_r, b2_s, b2_r, d_s, d_r,
    fx_s, fx_r, bx_s, bx_r, r0_s, r0_r, r1a_s, r1a_r, r1b_s, r1b_r, r2a_s, r2a_r, r2b_s, r2b_r,
    zr_s, zr_r,
):
    sec, dp = lax.axis_index("section"), lax.axis_index("dp")
    z, xh = sec // 2, sec % 2
    y, xl, c = dp // 4, (dp // 2) % 2, dp % 2
    x = xh * 2 + xl
    other = 1 - c

    def at(ax, ay, az, ac):
        return (az * 2 + ax // 2, ay * 4 + (ax % 2) * 2 + ac)

    def xdev(k):
        return at((x + k) % 4, y, z, c)

    def ydev(k):
        return at(x, (y + k) % 4, z, c)

    def zdev(k):
        return at(x, y, (z + 8 + k) % 8, c)

    sibling = at(x, y, z, other)
    pair = z >= FIRST_PAIR
    single = z < FIRST_PAIR
    ispair = pair.astype(jnp.int32) if FIRST_PAIR < 8 else 0
    odd = (z % 2) * ispair
    planes = 1 + ispair
    layers = 2 * planes
    slots = 4 // planes
    own_p = odd
    own_l = 2 * own_p + xh
    zpartner = at(x, y, z + 1 - 2 * (z % 2), c)

    barrier = pltpu.get_barrier_semaphore()
    peers = [sibling] + [xdev(k) for k in (1, 2, 3)] + [ydev(k) for k in (1, 2, 3)]
    peers += [zdev(1), zdev(-1)]
    if FIRST_PAIR < 8:
        peers += [zdev(2), zdev(-2)]
    for peer in peers:
        pl.semaphore_signal(barrier, inc=1, device_id=peer, device_id_type=MESH)

    def send(src, dst, ss, rs, to):
        return pltpu.make_async_remote_copy(
            src_ref=src, dst_ref=dst, send_sem=ss, recv_sem=rs, device_id=to, device_id_type=MESH
        )

    eye = lax.broadcasted_iota(jnp.int32, (64, 64), 0) == lax.broadcasted_iota(jnp.int32, (64, 64), 1)
    gain_col = jnp.sum(jnp.where(eye, g_in[...].astype(jnp.float32), 0.0), axis=1, keepdims=True)
    w[own_l, y, xl, c] = (w_in[0].astype(jnp.float32) * gain_col).astype(jnp.bfloat16)
    pl.semaphore_wait(barrier, len(peers))

    A, B, ALL = pl.ds(0, HALF), pl.ds(HALF, HALF), pl.ds(0, D)

    def blk(p, bx, by, cols):
        return w.at[2 * p + bx // 2, by, bx % 2, c, :, cols]

    def row_of(p, by):
        return w.at[pl.ds(2 * p, 2), by, :, c, :, A]

    def col_of(p, bx):
        return w.at[2 * p + bx // 2, :, bx % 2, c, :, B]

    def zx():
        ref = w.at[own_l, y, xl, c]
        return send(ref, ref, zx_s, zx_r, zpartner)

    def zx_other():
        ref = w.at[2 * (1 - own_p) + xh, y, xl, c]
        return send(ref, ref, zx_s, zx_r, zpartner)

    def a1(p, k):
        ref = blk(p, x, y, A)
        return send(ref, ref, a1_s.at[p, k - 1], a1_r.at[p, k - 1], xdev(k))

    def b1(p, k):
        ref = blk(p, x, y, B)
        return send(ref, ref, b1_s.at[p, k - 1], b1_r.at[p, k - 1], ydev(k))

    def a2(p, src, k):
        ref = blk(p, (x - src + 4) % 4, y, A)
        return send(ref, ref, a2_s.at[p, src, k - 1], a2_r.at[p, k - 1], ydev(k))

    def b2(p, src, k):
        ref = blk(p, x, (y - src + 4) % 4, B)
        return send(ref, ref, b2_s.at[p, src, k - 1], b2_r.at[p, k - 1], xdev(k))

    def a2_wait(p, k):
        ref = row_of(p, (y - k + 4) % 4)
        return send(ref, ref, a2_s.at[p, 0, 0], a2_r.at[p, k - 1], sibling)

    def b2_wait(p, k):
        ref = col_of(p, (x - k + 4) % 4)
        return send(ref, ref, b2_s.at[p, 0, 0], b2_r.at[p, k - 1], sibling)

    def d_own(p):
        ref = blk(p, x, y, ALL)
        return send(ref, ref, d_s.at[p, 0], d_r.at[p], sibling)

    def d_a1(p, k):
        ref = blk(p, (x - k + 4) % 4, y, A)
        return send(ref, ref, d_s.at[p, k], d_r.at[p], sibling)

    def d_b1(p, k):
        ref = blk(p, x, (y - k + 4) % 4, B)
        return send(ref, ref, d_s.at[p, 3 + k], d_r.at[p], sibling)

    def d_a2(p, k):
        ref = row_of(p, (y - k + 4) % 4)
        return send(ref, ref, d_s.at[p, 6 + k], d_r.at[p], sibling)

    def d_b2(p, k):
        ref = col_of(p, (x - k + 4) % 4)
        return send(ref, ref, d_s.at[p, 9 + k], d_r.at[p], sibling)

    def d_wait(p):
        ref = w.at[pl.ds(2 * p, 2), :, :, other]
        return send(ref, ref, d_s.at[p, 0], d_r.at[p], sibling)

    K = (1, 2, 3)
    if FIRST_PAIR < 8:

        @pl.when(pair)
        def _():
            zx().start()

    def gather_start(i, carry):
        p = (own_p + i) % planes

        @pl.when(i > 0)
        def _():
            zx_other().wait_recv()

        for k in K:
            a1(p, k).start()
            b1(p, k).start()
        for k in K:
            a2(p, 0, k).start()
            b2(p, 0, k).start()
        d_own(p).start()
        return carry

    def gather_mid(i, carry):
        p = (own_p + i) % planes
        for src in (1, 3, 2):
            a1(p, src).wait_recv()
            for k in K:
                a2(p, src, k).start()
            d_a1(p, src).start()
            b1(p, src).wait_recv()
            for k in K:
                b2(p, src, k).start()
            d_b1(p, src).start()
        return carry

    def gather_end(i, carry):
        p = (own_p + i) % planes
        for k in (1, 3, 2):
            a2_wait(p, k).wait_recv()
            d_a2(p, k).start()
            b2_wait(p, k).wait_recv()
            d_b2(p, k).start()
        return carry

    def gather_wait(i, carry):
        d_wait((own_p + i) % planes).wait_recv()
        return carry

    lax.fori_loop(0, planes, gather_start, 0)

    first = z < (2 if FIRST_PAIR == 0 else 1)
    last = z >= (7 if FIRST_PAIR == 8 else 6)

    def load_rows(dst, down, up):
        for slot in range(4):
            def take(j, slot=slot):
                b, half = j // 2, j % 2
                for ref, cond in ((down, xh == 0), (up, xh == 1)):

                    @pl.when(cond)
                    def _(ref=ref):
                        dst[slot] = ref[b, pl.ds(pl.multiple_of(half * MB_ROWS, MB_ROWS), MB_ROWS), :]

            if FIRST_PAIR == 8:
                take(slot)
            elif slot < 2:
                take((2 * slot + odd) if FIRST_PAIR == 0 else slot * planes + odd)
            else:

                @pl.when(single)
                def _(slot=slot):
                    take(slot)

    @pl.when(first)
    def _():
        load_rows(xs.at[0], down_in, up_in)

    @pl.when(last)
    def _():
        load_rows(cot, down_cot, up_cot)

    if FIRST_PAIR < 8:
        h[...] = jnp.zeros_like(h)
        du[...] = jnp.zeros_like(du)

    lax.fori_loop(0, planes, gather_mid, 0)
    lax.fori_loop(0, planes, gather_end, 0)
    lax.fori_loop(0, planes, gather_wait, 0)

    if FIRST_PAIR == 8:

        def f_route(j):
            return zdev(1), j

        def b_route(j):
            return zdev(-1), j

    else:
        to_pair = (z == FIRST_PAIR - 1).astype(jnp.int32)
        from_pair = ((z // 2) * 2 == FIRST_PAIR).astype(jnp.int32)

        def f_route(j):
            step = ispair * 2 + (1 - ispair) * (1 + to_pair * (j % 2))
            slot = j - to_pair * (j - j // 2)
            return zdev(step), slot

        def b_route(j):
            step = ispair * (2 + from_pair * (odd - 1)) + (1 - ispair)
            slot = j + from_pair * (j + odd)
            return zdev(-step), slot

    def fx(j):
        to, slot = f_route(j)
        return send(xo.at[j], xs.at[0, slot], fx_s.at[j], fx_r.at[slot], to)

    def fx_wait(j):
        return send(xo.at[j], xs.at[0, j], fx_s.at[j], fx_r.at[j], sibling)

    def bx(j):
        to, slot = b_route(j)
        return send(do.at[j], cot.at[slot], bx_s.at[j], bx_r.at[slot], to)

    def bx_wait(j):
        return send(do.at[j], cot.at[j], bx_s.at[j], bx_r.at[j], sibling)

    def forward(j, carry):
        @pl.when(jnp.logical_not(first))
        def _():
            fx_wait(j).wait_recv()

        rows = pl.ds(pl.multiple_of(j * MB_ROWS, MB_ROWS), MB_ROWS)

        def layer(l, carry):
            xf = xs[l, j].astype(jnp.float32)
            r = lax.rsqrt(jnp.mean(xf * xf, axis=-1, keepdims=True) + EPSILON)
            normed = (xf * r).astype(jnp.bfloat16)
            h[l, rows, :] = normed
            rinv[l, j] = jnp.broadcast_to(r, (MB_ROWS, 128))
            u = jnp.dot(normed, w[l].reshape(D, D), preferred_element_type=jnp.float32)
            u2 = u * u
            t = jnp.tanh(SLOPE * (u + CUBIC * u2 * u))
            nxt = (xf + 0.5 * u * (1.0 + t)).astype(jnp.bfloat16)

            @pl.when(l < layers - 1)
            def _():
                xs[l + 1, j] = nxt

            @pl.when(l == layers - 1)
            def _():
                xo[j] = nxt

                @pl.when(jnp.logical_not(last))
                def _():
                    fx(j).start()

            sl[l, j] = 0.5 * (1.0 + t) + 0.5 * u * (1.0 - t * t) * SLOPE * (1.0 + 3.0 * CUBIC * u2)
            return carry

        return lax.fori_loop(0, layers, layer, carry)

    lax.fori_loop(0, slots, forward, 0)

    def backward(j, carry):
        @pl.when(jnp.logical_not(last))
        def _():
            bx_wait(j).wait_recv()

        rows = pl.ds(pl.multiple_of(j * MB_ROWS, MB_ROWS), MB_ROWS)

        def layer(i, carry):
            l = layers - 1 - i
            df = cot[j].astype(jnp.float32)
            grad = (df * sl[l, j]).astype(jnp.bfloat16)
            du[l, rows, :] = grad

            @pl.when(jnp.logical_not(jnp.logical_and(first, l == 0)))
            def _():
                a = lax.dot_general(
                    grad, w[l].reshape(D, D), (((1,), (1,)), ((), ())), preferred_element_type=jnp.float32
                )
                r = rinv[l, j][:, 0:1]
                xr = xs[l, j].astype(jnp.float32) * r
                new = (df + r * (a - xr * jnp.mean(a * xr, axis=-1, keepdims=True))).astype(jnp.bfloat16)

                @pl.when(l > 0)
                def _():
                    cot[j] = new

                @pl.when(l == 0)
                def _():
                    do[j] = new
                    bx(j).start()

            return carry

        return lax.fori_loop(0, layers, layer, carry)

    lax.fori_loop(0, slots, backward, 0)

    def e0(l):
        return send(part.at[l, :, :, other], r0.at[l], r0_s.at[l], r0_r.at[l], sibling)

    def e1a(l, k):
        return send(
            r0.at[l, (y + k) % 4, :, :, A], r1a.at[l, k - 1], r1a_s.at[l, k - 1], r1a_r.at[l, k - 1], ydev(k)
        )

    def e1b(l, k):
        return send(
            r0.at[l, :, (x + k) % 2, :, B], r1b.at[l // 2, k - 1], r1b_s.at[l, k - 1], r1b_r.at[l // 2, k - 1], xdev(k)
        )

    def e2a(l, k):
        return send(
            s1a.at[l, (x + k) % 2], r2a.at[l // 2, k - 1], r2a_s.at[l, k - 1], r2a_r.at[l // 2, k - 1], xdev(k)
        )

    def e2b(l, k):
        p = l // 2
        return send(
            s1b.at[p, (y + k) % 4], r2b.at[p, k - 1], r2b_s.at[p, k - 1], r2b_r.at[p, k - 1], ydev(k)
        )

    def for_x(l, act):
        for k in K:

            @pl.when(((x + k) % 4) // 2 == l % 2)
            def _(k=k):
                act(k)

    def mine(l):
        return xh == l % 2

    def f32(v):
        return v.astype(jnp.float32)

    def reduce_a(i, carry):
        l = layers - 1 - i
        g = lax.dot_general(
            h[l], du[l], (((0,), (0,)), ((), ())), preferred_element_type=jnp.float32
        )
        part[l] = g.astype(jnp.bfloat16).reshape(4, 2, 2, 64, D)
        e0(l).start()
        return carry

    def reduce_b(i, carry):
        l = layers - 1 - i
        e0(l).wait_recv()
        r0[l] = (f32(r0[l]) + f32(part[l, :, :, c])).astype(jnp.bfloat16)
        for k in K:
            e1a(l, k).start()
        for_x(l, lambda k: e1b(l, k).start())
        return carry

    def reduce_c(i, carry):
        l = layers - 1 - i
        for k in K:
            e1a(l, k).wait_recv()
        s1a[l] = (f32(r0[l, y, :, :, 0:HALF]) + f32(r1a[l, 0]) + f32(r1a[l, 1]) + f32(r1a[l, 2])).astype(jnp.bfloat16)
        for_x(l, lambda k: e2a(l, k).start())

        @pl.when(mine(l))
        def _():
            p = l // 2
            for k in K:
                e1b(l, k).wait_recv()
            s1b[p] = (f32(r0[l, :, xl, :, HALF:D]) + f32(r1b[p, 0]) + f32(r1b[p, 1]) + f32(r1b[p, 2])).astype(jnp.bfloat16)
            for k in K:
                e2b(l, k).start()

        return carry

    def zr():
        return send(zsend, zres, zr_s, zr_r, zpartner)

    def total(l):
        p = l // 2
        for k in K:
            e2a(l, k).wait_recv()
            e2b(l, k).wait_recv()
        left = f32(s1a[l, xl]) + f32(r2a[p, 0]) + f32(r2a[p, 1]) + f32(r2a[p, 2])
        right = f32(s1b[p, y]) + f32(r2b[p, 0]) + f32(r2b[p, 1]) + f32(r2b[p, 2])
        return left, right

    lax.fori_loop(0, layers, reduce_a, 0)
    lax.fori_loop(0, layers, reduce_b, 0)
    lax.fori_loop(0, layers, reduce_c, 0)

    if FIRST_PAIR < 8:

        @pl.when(pair)
        def _():
            left, right = total(2 * (1 - own_p) + xh)
            zsend[:, 0:HALF] = left
            zsend[:, HALF:D] = right
            zr().start()

    left, right = total(own_l)
    gw_out[0, :, 0:HALF] = left
    gw_out[0, :, HALF:D] = right
    if FIRST_PAIR < 8:

        @pl.when(pair)
        def _():
            zr().wait_recv()
            gw_out[0] = gw_out[0] + zres[...]

    full = gw_out[0]
    per_row = jnp.sum(full * w_in[0].astype(jnp.float32), axis=1, keepdims=True)
    gg_out[...] = jnp.sum(jnp.where(eye, per_row, 0.0), axis=0, keepdims=True)
    gw_out[0] = full * gain_col

    if FIRST_PAIR < 8:

        @pl.when(pair)
        def _():
            zx().wait_send()
            zr().wait_send()

    def drain_gather(i, carry):
        p = (own_p + i) % planes
        for k in K:
            a1(p, k).wait_send()
            b1(p, k).wait_send()
            for src in range(4):
                a2(p, src, k).wait_send()
                b2(p, src, k).wait_send()
            d_a1(p, k).wait_send()
            d_b1(p, k).wait_send()
            d_a2(p, k).wait_send()
            d_b2(p, k).wait_send()
        d_own(p).wait_send()
        return carry

    lax.fori_loop(0, planes, drain_gather, 0)

    def drain_relay(j, carry):
        @pl.when(jnp.logical_not(last))
        def _():
            fx(j).wait_send()

        @pl.when(jnp.logical_not(first))
        def _():
            bx(j).wait_send()

        return carry

    lax.fori_loop(0, slots, drain_relay, 0)

    def drain_reduce(l, carry):
        e0(l).wait_send()
        for k in K:
            e1a(l, k).wait_send()
        for_x(l, lambda k: e1b(l, k).wait_send())
        for_x(l, lambda k: e2a(l, k).wait_send())

        @pl.when(mine(l))
        def _():
            for k in K:
                e2b(l, k).wait_send()

        return carry

    lax.fori_loop(0, layers, drain_reduce, 0)


def shards(down_input, up_input, down_cot, up_cot, weight, gain):
    nl = 2 if FIRST_PAIR == 8 else 4
    np_ = nl // 2
    bf, f4 = jnp.bfloat16, jnp.float32
    dma = pltpu.SemaphoreType.DMA
    scratch = [
        pltpu.VMEM((nl, 4, 2, 2, 64, D), bf),
        pltpu.VMEM((nl, 4, 2, 2, 64, D), bf),
        pltpu.VMEM((nl, 4, 2, 64, D), bf),
        pltpu.VMEM((nl, 3, 2, 64, HALF), bf),
        pltpu.VMEM((np_, 3, 4, 64, HALF), bf),
        pltpu.VMEM((nl, 2, 64, HALF), bf),
        pltpu.VMEM((np_, 4, 64, HALF), bf),
        pltpu.VMEM((np_, 3, 64, HALF), bf),
        pltpu.VMEM((np_, 3, 64, HALF), bf),
        pltpu.VMEM((64, D), f4),
        pltpu.VMEM((64, D), f4),
        pltpu.VMEM((nl, 4 * MB_ROWS, D), bf),
        pltpu.VMEM((nl, 4 * MB_ROWS, D), bf),
        pltpu.VMEM((nl, 4, MB_ROWS, D), bf),
        pltpu.VMEM((nl, 4, MB_ROWS, D), f4),
        pltpu.VMEM((nl, 4, MB_ROWS, 128), f4),
        pltpu.VMEM((4, MB_ROWS, D), bf),
        pltpu.VMEM((4, MB_ROWS, D), bf),
        pltpu.VMEM((4, MB_ROWS, D), bf),
        dma, dma,
        dma((np_, 3)), dma((np_, 3)), dma((np_, 3)), dma((np_, 3)),
        dma((np_, 4, 3)), dma((np_, 3)), dma((np_, 4, 3)), dma((np_, 3)),
        dma((np_, 13)), dma((np_,)),
        dma((4,)), dma((4,)), dma((4,)), dma((4,)),
        dma((nl,)), dma((nl,)),
        dma((nl, 3)), dma((nl, 3)), dma((nl, 3)), dma((np_, 3)),
        dma((nl, 3)), dma((np_, 3)), dma((np_, 3)), dma((np_, 3)),
        dma, dma,
    ]
    vmem = pl.BlockSpec(memory_space=pltpu.VMEM)
    return pl.pallas_call(
        kernel,
        out_shape=(
            jax.ShapeDtypeStruct((1, 64, D), f4),
            jax.ShapeDtypeStruct((1, 64), f4),
        ),
        in_specs=[vmem] * 6,
        out_specs=(vmem, vmem),
        scratch_shapes=scratch,
        compiler_params=pltpu.CompilerParams(
            collective_id=0, has_side_effects=True, vmem_limit_bytes=56 * 1024 * 1024
        ),
    )(down_input, up_input, down_cot, up_cot, weight, gain)


def solution(mesh):
    rows = P(None, "dp", None)
    return jax.shard_map(
        shards,
        mesh=mesh,
        in_specs=(rows, rows, rows, rows, P("section", "dp", None), P("section", "dp")),
        out_specs=(P("section", "dp", None), P("section", "dp")),
        check_vma=False,
    )
```

```python
import functools
import math

import jax
import jax.numpy as jnp
from jax import lax
from jax.experimental import pallas as pl
from jax.experimental.pallas import tpu as pltpu
from jax.sharding import PartitionSpec as P

EPSILON = 1e-05
CUBIC = 0.044715
SLOPE = math.sqrt(2.0 / math.pi)
MESH = pl.DeviceIdType.MESH
FIRST_PAIR = 4
D = 1024
HALF = D // 2
MB_ROWS = 32


def kernel(
    down_in, up_in, down_cot, up_cot, w_in, g_in, gw_out, gg_out,
    w, hs, ds, hx, dx, gs, gr, ft, fr, zres, zsend, xs, sl, rinv, xo, do, cot,
    zx_s, zx_r, a1_s, a1_r, b1_s, b1_r, a2_s, a2_r, b2_s, b2_r, d_s, d_r,
    fx_s, fx_r, bx_s, bx_r, h_s, h_r, u_s, u_r, g_s, g_r, f_s, f_r, zr_s, zr_r,
):
    sec, dp = lax.axis_index("section"), lax.axis_index("dp")
    z, xh = sec // 2, sec % 2
    y, xl, c = dp // 4, (dp // 2) % 2, dp % 2
    x = xh * 2 + xl
    other = 1 - c

    def at(ax, ay, az, ac):
        return (az * 2 + ax // 2, ay * 4 + (ax % 2) * 2 + ac)

    def xdev(k):
        return at((x + k) % 4, y, z, c)

    def ydev(k):
        return at(x, (y + k) % 4, z, c)

    def zdev(k):
        return at(x, y, (z + 8 + k) % 8, c)

    sibling = at(x, y, z, other)
    pair = z >= FIRST_PAIR
    single = z < FIRST_PAIR
    ispair = pair.astype(jnp.int32) if FIRST_PAIR < 8 else 0
    odd = (z % 2) * ispair
    planes = 1 + ispair
    layers = 2 * planes
    slots = 4 // planes
    own_p = odd
    own_l = 2 * own_p + xh
    zpartner = at(x, y, z + 1 - 2 * (z % 2), c)

    barrier = pltpu.get_barrier_semaphore()
    peers = [sibling] + [xdev(k) for k in (1, 2, 3)] + [ydev(k) for k in (1, 2, 3)]
    peers += [at((x + k) % 4, y, z, other) for k in (1, 2, 3)]
    peers += [zdev(1), zdev(-1)]
    if FIRST_PAIR < 8:
        peers += [zdev(2), zdev(-2)]
    for peer in peers:
        pl.semaphore_signal(barrier, inc=1, device_id=peer, device_id_type=MESH)

    def send(src, dst, ss, rs, to):
        return pltpu.make_async_remote_copy(
            src_ref=src, dst_ref=dst, send_sem=ss, recv_sem=rs, device_id=to, device_id_type=MESH
        )

    eye = lax.broadcasted_iota(jnp.int32, (64, 64), 0) == lax.broadcasted_iota(jnp.int32, (64, 64), 1)
    gain_col = jnp.sum(jnp.where(eye, g_in[...].astype(jnp.float32), 0.0), axis=1, keepdims=True)
    w[own_l, y, xl, c] = (w_in[0].astype(jnp.float32) * gain_col).astype(jnp.bfloat16)
    pl.semaphore_wait(barrier, len(peers))

    A, B, ALL = pl.ds(0, HALF), pl.ds(HALF, HALF), pl.ds(0, D)

    def blk(p, bx, by, cols):
        return w.at[2 * p + bx // 2, by, bx % 2, c, :, cols]

    def zx():
        ref = w.at[own_l, y, xl, c]
        return send(ref, ref, zx_s, zx_r, zpartner)

    def zx_other():
        ref = w.at[2 * (1 - own_p) + xh, y, xl, c]
        return send(ref, ref, zx_s, zx_r, zpartner)

    def a1(p, k):
        ref = blk(p, x, y, A)
        return send(ref, ref, a1_s.at[p, k - 1], a1_r.at[p, k - 1], xdev(k))

    def b1(p, k):
        ref = blk(p, x, y, B)
        return send(ref, ref, b1_s.at[p, k - 1], b1_r.at[p, k - 1], ydev(k))

    def a2(p, src, k):
        ref = blk(p, (x - src + 4) % 4, y, A)
        return send(ref, ref, a2_s.at[p, src, k - 1], a2_r.at[p, src, k - 1], ydev(k))

    def b2(p, src, k):
        ref = blk(p, x, (y - src + 4) % 4, B)
        return send(ref, ref, b2_s.at[p, src, k - 1], b2_r.at[p, src, k - 1], xdev(k))

    def d_a2(p, src, k):
        ref = blk(p, (x - src + 4) % 4, (y - k + 4) % 4, A)
        return send(ref, ref, d_s.at[p, 7 + 3 * src + k - 1], d_r.at[p], sibling)

    def d_b2(p, src, k):
        ref = blk(p, (x - k + 4) % 4, (y - src + 4) % 4, B)
        return send(ref, ref, d_s.at[p, 19 + 3 * src + k - 1], d_r.at[p], sibling)

    def a2_wait(p, src, k):
        ref = blk(p, (x - src + 4) % 4, (y - k + 4) % 4, A)
        return send(ref, ref, a2_s.at[p, src, k - 1], a2_r.at[p, src, k - 1], sibling)

    def b2_wait(p, src, k):
        ref = blk(p, (x - k + 4) % 4, (y - src + 4) % 4, B)
        return send(ref, ref, b2_s.at[p, src, k - 1], b2_r.at[p, src, k - 1], sibling)

    def d_own(p):
        ref = blk(p, x, y, ALL)
        return send(ref, ref, d_s.at[p, 0], d_r.at[p], sibling)

    def d_a1(p, k):
        ref = blk(p, (x - k + 4) % 4, y, A)
        return send(ref, ref, d_s.at[p, k], d_r.at[p], sibling)

    def d_b1(p, k):
        ref = blk(p, x, (y - k + 4) % 4, B)
        return send(ref, ref, d_s.at[p, 3 + k], d_r.at[p], sibling)

    def d_wait(p):
        ref = w.at[pl.ds(2 * p, 2), :, :, other]
        return send(ref, ref, d_s.at[p, 0], d_r.at[p], sibling)

    K = (1, 2, 3)
    if FIRST_PAIR < 8:

        @pl.when(pair)
        def _():
            zx().start()

    def gather_start(i, carry):
        p = (own_p + i) % planes

        @pl.when(i > 0)
        def _():
            zx_other().wait_recv()

        d_own(p).start()
        for k in (1, 3):
            a1(p, k).start()
            b1(p, k).start()
        a1(p, 2).start()
        b1(p, 2).start()
        for k in (1, 3, 2):
            a2(p, 0, k).start()
            b2(p, 0, k).start()
        return carry

    def gather_mid(i, carry):
        p = (own_p + i) % planes
        for src in (1, 3, 2):
            a1(p, src).wait_recv()
            for k in (1, 3, 2):
                a2(p, src, k).start()
            d_a1(p, src).start()
            b1(p, src).wait_recv()
            for k in (1, 3, 2):
                b2(p, src, k).start()
            d_b1(p, src).start()
        return carry

    def gather_end(i, carry):
        p = (own_p + i) % planes
        for src in (0, 1, 3, 2):
            for k in (1, 3, 2):
                a2_wait(p, src, k).wait_recv()
                d_a2(p, src, k).start()
                b2_wait(p, src, k).wait_recv()
                d_b2(p, src, k).start()
        return carry

    def gather_wait(i, carry):
        d_wait((own_p + i) % planes).wait_recv()
        return carry

    lax.fori_loop(0, planes, gather_start, 0)

    first = z < (2 if FIRST_PAIR == 0 else 1)
    last = z >= (7 if FIRST_PAIR == 8 else 6)

    def load_rows(dst, down, up):
        for slot in range(4):
            def take(j, slot=slot):
                b, half = j // 2, j % 2
                for ref, cond in ((down, xh == 0), (up, xh == 1)):

                    @pl.when(cond)
                    def _(ref=ref):
                        dst[slot] = ref[b, pl.ds(pl.multiple_of(half * MB_ROWS, MB_ROWS), MB_ROWS), :]

            if FIRST_PAIR == 8:
                take(slot)
            elif slot < 2:
                take((2 * slot + odd) if FIRST_PAIR == 0 else slot * planes + odd)
            else:

                @pl.when(single)
                def _(slot=slot):
                    take(slot)

    @pl.when(first)
    def _():
        load_rows(xs.at[0], down_in, up_in)

    @pl.when(last)
    def _():
        load_rows(cot, down_cot, up_cot)

    lax.fori_loop(0, planes, gather_mid, 0)
    lax.fori_loop(0, planes, gather_end, 0)
    lax.fori_loop(0, planes, gather_wait, 0)

    if FIRST_PAIR == 8:

        def f_route(j):
            return zdev(1), j

        def b_route(j):
            return zdev(-1), j

    else:
        to_pair = (z == FIRST_PAIR - 1).astype(jnp.int32)
        from_pair = ((z // 2) * 2 == FIRST_PAIR).astype(jnp.int32)

        def f_route(j):
            step = ispair * 2 + (1 - ispair) * (1 + to_pair * (j % 2))
            slot = j - to_pair * (j - j // 2)
            return zdev(step), slot

        def b_route(j):
            step = ispair * (2 + from_pair * (odd - 1)) + (1 - ispair)
            slot = j + from_pair * (j + odd)
            return zdev(-step), slot

    def fx(j):
        to, slot = f_route(j)
        return send(xo.at[j], xs.at[0, slot], fx_s.at[j], fx_r.at[slot], to)

    def fx_wait(j):
        return send(xo.at[j], xs.at[0, j], fx_s.at[j], fx_r.at[j], sibling)

    def bx(j):
        to, slot = b_route(j)
        return send(do.at[j], cot.at[slot], bx_s.at[j], bx_r.at[slot], to)

    def bx_wait(j):
        return send(do.at[j], cot.at[j], bx_s.at[j], bx_r.at[j], sibling)

    me8 = x * 2 + c

    def share(src, dst, ss, rs, l, j, t, cc):
        part = (t, cc)
        rows = pl.ds(pl.multiple_of(j * MB_ROWS, MB_ROWS), MB_ROWS)
        q = 2 * t + cc
        return send(
            src.at[l, part[0] if src is hs else part[1], rows, :],
            dst.at[l // 2, me8, rows, :],
            ss.at[l * slots + j, q],
            rs.at[l // 2, me8],
            at(2 * (l % 2) + t, y, z, cc),
        )

    def for_owners(l, act):
        for t in range(2):
            for cc in range(2):

                @pl.when(jnp.logical_or(2 * (l % 2) + t != x, cc != c))
                def _(t=t, cc=cc):
                    act(t, cc)

    def share_h(l, j, t, cc):
        return share(hs, hx, h_s, h_r, l, j, t, cc)

    def share_u(l, j, t, cc):
        return share(ds, dx, u_s, u_r, l, j, t, cc)

    def forward(j, carry):
        @pl.when(jnp.logical_not(first))
        def _():
            fx_wait(j).wait_recv()

        rows = pl.ds(pl.multiple_of(j * MB_ROWS, MB_ROWS), MB_ROWS)

        def layer(l, carry):
            xf = xs[l, j].astype(jnp.float32)
            r = lax.rsqrt(jnp.mean(xf * xf, axis=-1, keepdims=True) + EPSILON)
            normed = (xf * r).astype(jnp.bfloat16)
            for t in range(2):
                for b in range(4):
                    hs[l, t, rows, b * 128 : (b + 1) * 128] = normed[:, b * 256 + t * 128 : b * 256 + (t + 1) * 128]
            rinv[l, j] = jnp.broadcast_to(r, (MB_ROWS, 128))
            u = jnp.dot(normed, w[l].reshape(D, D), preferred_element_type=jnp.float32)
            u2 = u * u
            t = jnp.tanh(SLOPE * (u + CUBIC * u2 * u))
            nxt = (xf + 0.5 * u * (1.0 + t)).astype(jnp.bfloat16)

            @pl.when(l < layers - 1)
            def _():
                xs[l + 1, j] = nxt

            @pl.when(l == layers - 1)
            def _():
                xo[j] = nxt

                @pl.when(jnp.logical_not(last))
                def _():
                    fx(j).start()

            sl[l, j] = 0.5 * (1.0 + t) + 0.5 * u * (1.0 - t * t) * SLOPE * (1.0 + 3.0 * CUBIC * u2)
            for_owners(l, lambda t, cc: share_h(l, j, t, cc).start())
            return carry

        return lax.fori_loop(0, layers, layer, carry)

    lax.fori_loop(0, slots, forward, 0)

    def backward(j, carry):
        @pl.when(jnp.logical_not(last))
        def _():
            bx_wait(j).wait_recv()

        rows = pl.ds(pl.multiple_of(j * MB_ROWS, MB_ROWS), MB_ROWS)

        def layer(i, carry):
            l = layers - 1 - i
            df = cot[j].astype(jnp.float32)
            grad = (df * sl[l, j]).astype(jnp.bfloat16)
            ds[l, 0, rows, :] = grad[:, 0:HALF]
            ds[l, 1, rows, :] = grad[:, HALF:D]

            @pl.when(jnp.logical_not(jnp.logical_and(first, l == 0)))
            def _():
                a = lax.dot_general(
                    grad, w[l].reshape(D, D), (((1,), (1,)), ((), ())), preferred_element_type=jnp.float32
                )
                r = rinv[l, j][:, 0:1]
                xr = xs[l, j].astype(jnp.float32) * r
                new = (df + r * (a - xr * jnp.mean(a * xr, axis=-1, keepdims=True))).astype(jnp.bfloat16)

                @pl.when(l > 0)
                def _():
                    cot[j] = new

                @pl.when(l == 0)
                def _():
                    do[j] = new
                    bx(j).start()

            for_owners(l, lambda t, cc: share_u(l, j, t, cc).start())
            return carry

        return lax.fori_loop(0, layers, layer, carry)

    lax.fori_loop(0, slots, backward, 0)

    def f32(v):
        return v.astype(jnp.float32)

    def gy(p, k):
        return send(gs.at[p, (y + k) % 4], gr.at[p, k - 1], g_s.at[p, k - 1], g_r.at[p, k - 1], ydev(k))

    def swap(p):
        return send(ft.at[p, other], fr.at[p], f_s.at[p], f_r.at[p], sibling)

    def collect(p, count):
        for src in range(8):

            @pl.when(src != me8)
            def _(src=src):
                for ref, rs in ((hx, h_r), (dx, u_r)):
                    block = ref.at[p, src, pl.ds(0, count), :]
                    send(block, block, h_s.at[0, 0], rs.at[p, src], sibling).wait_recv()

        l = 2 * p + xh
        hx[p, me8, 0:count, :] = hs[l, xl, 0:count, :]
        dx[p, me8, 0:count, :] = ds[l, c, 0:count, :]
        g = lax.dot_general(
            hx[p, :, 0:count, :].reshape(8 * count, HALF),
            dx[p, :, 0:count, :].reshape(8 * count, HALF),
            (((0,), (0,)), ((), ())),
            preferred_element_type=jnp.float32,
        )
        gs[p] = g.astype(jnp.bfloat16).reshape(4, 128, HALF)
        for k in (1, 3, 2):
            gy(p, k).start()

    def add_up(p):
        for k in (1, 3, 2):
            gy(p, k).wait_recv()
        ft[p] = (f32(gs[p, y]) + f32(gr[p, 0]) + f32(gr[p, 1]) + f32(gr[p, 2])).reshape(2, 64, HALF)
        swap(p).start()

    here = pl.ds(pl.multiple_of(c * HALF, HALF), HALF)
    there = pl.ds(pl.multiple_of(other * HALF, HALF), HALF)

    def zr():
        return send(zsend, zres, zr_s, zr_r, zpartner)

    if FIRST_PAIR > 0:

        @pl.when(single)
        def _():
            collect(0, 4 * MB_ROWS)

    if FIRST_PAIR < 8:

        @pl.when(pair)
        def _():
            collect(1 - own_p, 2 * MB_ROWS)
            collect(own_p, 2 * MB_ROWS)
            add_up(1 - own_p)

    add_up(own_p)
    if FIRST_PAIR < 8:

        @pl.when(pair)
        def _():
            p = 1 - own_p
            swap(p).wait_recv()
            zsend[:, here] = ft[p, c]
            zsend[:, there] = fr[p]
            zr().start()

    swap(own_p).wait_recv()
    gw_out[0, :, here] = ft[own_p, c]
    gw_out[0, :, there] = fr[own_p]
    if FIRST_PAIR < 8:

        @pl.when(pair)
        def _():
            zr().wait_recv()
            gw_out[0] = gw_out[0] + zres[...]

    full = gw_out[0]
    per_row = jnp.sum(full * w_in[0].astype(jnp.float32), axis=1, keepdims=True)
    gg_out[...] = jnp.sum(jnp.where(eye, per_row, 0.0), axis=0, keepdims=True)
    gw_out[0] = full * gain_col

    if FIRST_PAIR < 8:

        @pl.when(pair)
        def _():
            zx().wait_send()
            zr().wait_send()

    def drain_gather(i, carry):
        p = (own_p + i) % planes
        for k in K:
            a1(p, k).wait_send()
            b1(p, k).wait_send()
            for src in range(4):
                a2(p, src, k).wait_send()
                b2(p, src, k).wait_send()
                d_a2(p, src, k).wait_send()
                d_b2(p, src, k).wait_send()
            d_a1(p, k).wait_send()
            d_b1(p, k).wait_send()
        d_own(p).wait_send()
        return carry

    lax.fori_loop(0, planes, drain_gather, 0)

    def drain_relay(j, carry):
        @pl.when(jnp.logical_not(last))
        def _():
            fx(j).wait_send()

        @pl.when(jnp.logical_not(first))
        def _():
            bx(j).wait_send()

        return carry

    lax.fori_loop(0, slots, drain_relay, 0)

    def drain_layers(l, carry):
        def drain_rows(j, carry):
            for_owners(l, lambda t, cc: share_h(l, j, t, cc).wait_send())
            for_owners(l, lambda t, cc: share_u(l, j, t, cc).wait_send())
            return carry

        return lax.fori_loop(0, slots, drain_rows, carry)

    lax.fori_loop(0, layers, drain_layers, 0)

    def drain_sums(p, carry):
        for k in K:
            gy(p, k).wait_send()
        swap(p).wait_send()
        return carry

    lax.fori_loop(0, planes, drain_sums, 0)


def shards(down_input, up_input, down_cot, up_cot, weight, gain):
    nl = 2 if FIRST_PAIR == 8 else 4
    np_ = nl // 2
    bf, f4 = jnp.bfloat16, jnp.float32
    dma = pltpu.SemaphoreType.DMA
    scratch = [
        pltpu.VMEM((nl, 4, 2, 2, 64, D), bf),
        pltpu.VMEM((nl, 2, 4 * MB_ROWS, HALF), bf),
        pltpu.VMEM((nl, 2, 4 * MB_ROWS, HALF), bf),
        pltpu.VMEM((np_, 8, 4 * MB_ROWS, HALF), bf),
        pltpu.VMEM((np_, 8, 4 * MB_ROWS, HALF), bf),
        pltpu.VMEM((np_, 4, 128, HALF), bf),
        pltpu.VMEM((np_, 3, 128, HALF), bf),
        pltpu.VMEM((np_, 2, 64, HALF), f4),
        pltpu.VMEM((np_, 64, HALF), f4),
        pltpu.VMEM((64, D), f4),
        pltpu.VMEM((64, D), f4),
        pltpu.VMEM((nl, 4, MB_ROWS, D), bf),
        pltpu.VMEM((nl, 4, MB_ROWS, D), f4),
        pltpu.VMEM((nl, 4, MB_ROWS, 128), f4),
        pltpu.VMEM((4, MB_ROWS, D), bf),
        pltpu.VMEM((4, MB_ROWS, D), bf),
        pltpu.VMEM((4, MB_ROWS, D), bf),
        dma, dma,
        dma((np_, 3)), dma((np_, 3)), dma((np_, 3)), dma((np_, 3)),
        dma((np_, 4, 3)), dma((np_, 4, 3)), dma((np_, 4, 3)), dma((np_, 4, 3)),
        dma((np_, 31)), dma((np_,)),
        dma((4,)), dma((4,)), dma((4,)), dma((4,)),
        dma((8, 4)), dma((np_, 8)), dma((8, 4)), dma((np_, 8)),
        dma((np_, 3)), dma((np_, 3)), dma((np_,)), dma((np_,)),
        dma, dma,
    ]
    vmem = pl.BlockSpec(memory_space=pltpu.VMEM)
    return pl.pallas_call(
        kernel,
        out_shape=(
            jax.ShapeDtypeStruct((1, 64, D), f4),
            jax.ShapeDtypeStruct((1, 64), f4),
        ),
        in_specs=[vmem] * 6,
        out_specs=(vmem, vmem),
        scratch_shapes=scratch,
        compiler_params=pltpu.CompilerParams(
            collective_id=0, has_side_effects=True, vmem_limit_bytes=56 * 1024 * 1024
        ),
    )(down_input, up_input, down_cot, up_cot, weight, gain)


def solution(mesh):
    rows = P(None, "dp", None)
    return jax.shard_map(
        shards,
        mesh=mesh,
        in_specs=(rows, rows, rows, rows, P("section", "dp", None), P("section", "dp")),
        out_specs=(P("section", "dp", None), P("section", "dp")),
        check_vma=False,
    )
```

```python
import functools
import math

import jax
import jax.numpy as jnp
from jax import lax
from jax.experimental import pallas as pl
from jax.experimental.pallas import tpu as pltpu
from jax.sharding import PartitionSpec as P

EPSILON = 1e-05
CUBIC = 0.044715
SLOPE = math.sqrt(2.0 / math.pi)
MESH = pl.DeviceIdType.MESH
FIRST_PAIR = 4
D = 1024
HALF = D // 2
MB_ROWS = 32


def kernel(
    down_in, up_in, down_cot, up_cot, w_in, g_in, gw_out, gg_out,
    w, wt, hs, ds, hx, dx, acc, gs, gr, ft, fr, zres, zsend, xs, sl, rinv, xo, do, cot,
    zx_s, zx_r, a1_s, a1_r, b1_s, b1_r, a2_s, a2_r, b2_s, b2_r, d_s, d_r,
    fx_s, fx_r, bx_s, bx_r, h_s, h_r, u_s, u_r, g_s, g_r, f_s, f_r, zr_s, zr_r, above,
):
    sec, dp = lax.axis_index("section"), lax.axis_index("dp")
    z, xh = sec // 2, sec % 2
    y, xl, c = dp // 4, (dp // 2) % 2, dp % 2
    x = xh * 2 + xl
    other = 1 - c

    def at(ax, ay, az, ac):
        return (az * 2 + ax // 2, ay * 4 + (ax % 2) * 2 + ac)

    def xdev(k):
        return at((x + k) % 4, y, z, c)

    def ydev(k):
        return at(x, (y + k) % 4, z, c)

    def zdev(k):
        return at(x, y, (z + 8 + k) % 8, c)

    sibling = at(x, y, z, other)
    pair = z >= FIRST_PAIR
    single = z < FIRST_PAIR
    ispair = pair.astype(jnp.int32) if FIRST_PAIR < 8 else 0
    odd = (z % 2) * ispair
    planes = 1 + ispair
    layers = 2 * planes
    slots = 4 // planes
    own_p = odd
    own_l = 2 * own_p + xh
    zpartner = at(x, y, z + 1 - 2 * (z % 2), c)

    barrier = pltpu.get_barrier_semaphore()
    peers = [sibling] + [xdev(k) for k in (1, 2, 3)] + [ydev(k) for k in (1, 2, 3)]
    peers += [at((x + k) % 4, y, z, other) for k in (1, 2, 3)]
    for peer in peers:
        pl.semaphore_signal(barrier, inc=1, device_id=peer, device_id_type=MESH)
    for k in (1, 2):

        @pl.when(z + k < 8)
        def _(k=k):
            pl.semaphore_signal(barrier, inc=1, device_id=zdev(k), device_id_type=MESH)

    def wait_above():
        for k in (1, 2):

            @pl.when(z + k < 8)
            def _(k=k):
                pl.semaphore_wait(above.at[k - 1], 1)

    def send(src, dst, ss, rs, to):
        return pltpu.make_async_remote_copy(
            src_ref=src, dst_ref=dst, send_sem=ss, recv_sem=rs, device_id=to, device_id_type=MESH
        )

    eye = lax.broadcasted_iota(jnp.int32, (64, 64), 0) == lax.broadcasted_iota(jnp.int32, (64, 64), 1)
    gain_col = jnp.sum(jnp.where(eye, g_in[...].astype(jnp.float32), 0.0), axis=1, keepdims=True)
    w[own_l, y, xl, c] = (w_in[0].astype(jnp.float32) * gain_col).astype(jnp.bfloat16)
    pl.semaphore_wait(barrier, len(peers) + jnp.minimum(z, 2))
    for k in (1, 2):

        @pl.when(z >= k)
        def _(k=k):
            pl.semaphore_signal(above.at[k - 1], inc=1, device_id=zdev(-k), device_id_type=MESH)


    A, B, ALL = pl.ds(0, HALF), pl.ds(HALF, HALF), pl.ds(0, D)

    def blk(p, bx, by, cols):
        return w.at[2 * p + bx // 2, by, bx % 2, c, :, cols]

    def zx():
        ref = w.at[own_l, y, xl, c]
        return send(ref, ref, zx_s, zx_r, zpartner)

    def zx_other():
        ref = w.at[2 * (1 - own_p) + xh, y, xl, c]
        return send(ref, ref, zx_s, zx_r, zpartner)

    def a1(p, k):
        ref = blk(p, x, y, A)
        return send(ref, ref, a1_s.at[p, k - 1], a1_r.at[p, k - 1], xdev(k))

    def b1(p, k):
        ref = blk(p, x, y, B)
        return send(ref, ref, b1_s.at[p, k - 1], b1_r.at[p, k - 1], ydev(k))

    def a2(p, src, k):
        ref = blk(p, (x - src + 4) % 4, y, A)
        return send(ref, ref, a2_s.at[p, src, k - 1], a2_r.at[p, src, k - 1], ydev(k))

    def b2(p, src, k):
        ref = blk(p, x, (y - src + 4) % 4, B)
        return send(ref, ref, b2_s.at[p, src, k - 1], b2_r.at[p, src, k - 1], xdev(k))

    def d_a2(p, src, k):
        ref = blk(p, (x - src + 4) % 4, (y - k + 4) % 4, A)
        return send(ref, ref, d_s.at[p, 7 + 3 * src + k - 1], d_r.at[p], sibling)

    def d_b2(p, src, k):
        ref = blk(p, (x - k + 4) % 4, (y - src + 4) % 4, B)
        return send(ref, ref, d_s.at[p, 19 + 3 * src + k - 1], d_r.at[p], sibling)

    def a2_wait(p, src, k):
        ref = blk(p, (x - src + 4) % 4, (y - k + 4) % 4, A)
        return send(ref, ref, a2_s.at[p, src, k - 1], a2_r.at[p, src, k - 1], sibling)

    def b2_wait(p, src, k):
        ref = blk(p, (x - k + 4) % 4, (y - src + 4) % 4, B)
        return send(ref, ref, b2_s.at[p, src, k - 1], b2_r.at[p, src, k - 1], sibling)

    def d_own(p):
        ref = blk(p, x, y, ALL)
        return send(ref, ref, d_s.at[p, 0], d_r.at[p], sibling)

    def d_a1(p, k):
        ref = blk(p, (x - k + 4) % 4, y, A)
        return send(ref, ref, d_s.at[p, k], d_r.at[p], sibling)

    def d_b1(p, k):
        ref = blk(p, x, (y - k + 4) % 4, B)
        return send(ref, ref, d_s.at[p, 3 + k], d_r.at[p], sibling)

    def d_wait(p):
        ref = w.at[pl.ds(2 * p, 2), :, :, other]
        return send(ref, ref, d_s.at[p, 0], d_r.at[p], sibling)

    K = (1, 2, 3)
    if FIRST_PAIR < 8:

        @pl.when(pair)
        def _():
            wait_above()
            zx().start()

    def gather_start(i, carry):
        p = (own_p + i) % planes

        @pl.when(i > 0)
        def _():
            zx_other().wait_recv()

        d_own(p).start()
        for k in (1, 3):
            a1(p, k).start()
            b1(p, k).start()
        a1(p, 2).start()
        b1(p, 2).start()
        for k in (1, 3, 2):
            a2(p, 0, k).start()
            b2(p, 0, k).start()
        return carry

    def gather_mid(i, carry):
        p = (own_p + i) % planes
        for src in (1, 3, 2):
            a1(p, src).wait_recv()
            for k in (1, 3, 2):
                a2(p, src, k).start()
            d_a1(p, src).start()
            b1(p, src).wait_recv()
            for k in (1, 3, 2):
                b2(p, src, k).start()
            d_b1(p, src).start()
        return carry

    def gather_end(i, carry):
        p = (own_p + i) % planes
        for src in (0, 1, 3, 2):
            for k in (1, 3, 2):
                a2_wait(p, src, k).wait_recv()
                d_a2(p, src, k).start()
                b2_wait(p, src, k).wait_recv()
                d_b2(p, src, k).start()
        return carry

    def gather_wait(i, carry):
        d_wait((own_p + i) % planes).wait_recv()
        return carry

    lax.fori_loop(0, planes, gather_start, 0)

    first = z < (2 if FIRST_PAIR == 0 else 1)
    last = z >= (7 if FIRST_PAIR == 8 else 6)

    def load_rows(dst, down, up):
        for slot in range(4):
            def take(j, slot=slot):
                b, half = j // 2, j % 2
                for ref, cond in ((down, xh == 0), (up, xh == 1)):

                    @pl.when(cond)
                    def _(ref=ref):
                        dst[slot] = ref[b, pl.ds(pl.multiple_of(half * MB_ROWS, MB_ROWS), MB_ROWS), :]

            if FIRST_PAIR == 8:
                take(slot)
            elif slot < 2:
                take((2 * slot + odd) if FIRST_PAIR == 0 else slot * planes + odd)
            else:

                @pl.when(single)
                def _(slot=slot):
                    take(slot)

    @pl.when(first)
    def _():
        load_rows(xs.at[0], down_in, up_in)

    @pl.when(last)
    def _():
        load_rows(cot, down_cot, up_cot)

    lax.fori_loop(0, planes, gather_mid, 0)
    lax.fori_loop(0, planes, gather_end, 0)
    lax.fori_loop(0, planes, gather_wait, 0)

    if FIRST_PAIR == 8:

        def f_route(j):
            return zdev(1), j

        def b_route(j):
            return zdev(-1), j

    else:
        to_pair = (z == FIRST_PAIR - 1).astype(jnp.int32)
        from_pair = ((z // 2) * 2 == FIRST_PAIR).astype(jnp.int32)

        def f_route(j):
            step = ispair * 2 + (1 - ispair) * (1 + to_pair * (j % 2))
            slot = j - to_pair * (j - j // 2)
            return zdev(step), slot

        def b_route(j):
            step = ispair * (2 + from_pair * (odd - 1)) + (1 - ispair)
            slot = j + from_pair * (j + odd)
            return zdev(-step), slot

    def fx(j):
        to, slot = f_route(j)
        return send(xo.at[j], xs.at[0, slot], fx_s.at[j], fx_r.at[slot], to)

    def fx_wait(j):
        return send(xo.at[j], xs.at[0, j], fx_s.at[j], fx_r.at[j], sibling)

    def bx(j):
        to, slot = b_route(j)
        return send(do.at[j], cot.at[slot], bx_s.at[j], bx_r.at[slot], to)

    def bx_wait(j):
        return send(do.at[j], cot.at[j], bx_s.at[j], bx_r.at[j], sibling)

    me8 = x * 2 + c

    def share(src, dst, ss, rs, l, j, t, cc):
        part = (t, cc)
        rows = pl.ds(pl.multiple_of(j * MB_ROWS, MB_ROWS), MB_ROWS)
        q = 2 * t + cc
        return send(
            src.at[l, part[0] if src is hs else part[1], rows, :],
            dst.at[l // 2, j, me8],
            ss.at[l * slots + j, q],
            rs.at[l // 2, j, me8],
            at(2 * (l % 2) + t, y, z, cc),
        )

    def for_owners(l, act):
        for t in range(2):
            for cc in range(2):

                @pl.when(jnp.logical_or(2 * (l % 2) + t != x, cc != c))
                def _(t=t, cc=cc):
                    act(t, cc)

    def share_h(l, j, t, cc):
        return share(hs, hx, h_s, h_r, l, j, t, cc)

    def share_u(l, j, t, cc):
        return share(ds, dx, u_s, u_r, l, j, t, cc)

    def forward(j, carry):
        @pl.when(jnp.logical_not(first))
        def _():
            fx_wait(j).wait_recv()

        rows = pl.ds(pl.multiple_of(j * MB_ROWS, MB_ROWS), MB_ROWS)

        def layer(l, carry):
            xf = xs[l, j].astype(jnp.float32)
            r = lax.rsqrt(jnp.mean(xf * xf, axis=-1, keepdims=True) + EPSILON)
            normed = (xf * r).astype(jnp.bfloat16)
            for t in range(2):
                for b in range(4):
                    hs[l, t, rows, b * 128 : (b + 1) * 128] = normed[:, b * 256 + t * 128 : b * 256 + (t + 1) * 128]
            rinv[l, j] = jnp.broadcast_to(r, (MB_ROWS, 128))
            u = jnp.dot(normed, w[l].reshape(D, D), preferred_element_type=jnp.float32)
            u2 = u * u
            t = jnp.tanh(SLOPE * (u + CUBIC * u2 * u))
            nxt = (xf + 0.5 * u * (1.0 + t)).astype(jnp.bfloat16)

            @pl.when(l < layers - 1)
            def _():
                xs[l + 1, j] = nxt

            @pl.when(l == layers - 1)
            def _():
                xo[j] = nxt

                @pl.when(jnp.logical_not(last))
                def _():
                    fx(j).start()

            sl[l, j] = 0.5 * (1.0 + t) + 0.5 * u * (1.0 - t * t) * SLOPE * (1.0 + 3.0 * CUBIC * u2)
            for_owners(l, lambda t, cc: share_h(l, j, t, cc).start())
            return carry

        return lax.fori_loop(0, layers, layer, carry)

    def turn(l, carry):
        wt[l] = w[l].reshape(D, D).T
        return carry

    @pl.when(last)
    def _():
        lax.fori_loop(0, layers, turn, 0)

    if FIRST_PAIR > 0:

        @pl.when(single)
        def _():
            wait_above()

    lax.fori_loop(0, slots, forward, 0)

    @pl.when(jnp.logical_not(last))
    def _():
        lax.fori_loop(0, layers, turn, 0)


    def backward(j, carry):
        @pl.when(jnp.logical_not(last))
        def _():
            bx_wait(j).wait_recv()

        rows = pl.ds(pl.multiple_of(j * MB_ROWS, MB_ROWS), MB_ROWS)

        def layer(i, carry):
            l = layers - 1 - i
            df = cot[j].astype(jnp.float32)
            grad = (df * sl[l, j]).astype(jnp.bfloat16)
            ds[l, 0, rows, :] = grad[:, 0:HALF]
            ds[l, 1, rows, :] = grad[:, HALF:D]

            @pl.when(jnp.logical_not(jnp.logical_and(first, l == 0)))
            def _():
                a = jnp.dot(grad, wt[l], preferred_element_type=jnp.float32)
                r = rinv[l, j][:, 0:1]
                xr = xs[l, j].astype(jnp.float32) * r
                new = (df + r * (a - xr * jnp.mean(a * xr, axis=-1, keepdims=True))).astype(jnp.bfloat16)

                @pl.when(l > 0)
                def _():
                    cot[j] = new

                @pl.when(l == 0)
                def _():
                    do[j] = new
                    bx(j).start()

            for_owners(l, lambda t, cc: share_u(l, j, t, cc).start())
            return carry

        return lax.fori_loop(0, layers, layer, carry)

    lax.fori_loop(0, slots, backward, 0)

    def f32(v):
        return v.astype(jnp.float32)

    def gy(p, k):
        return send(gs.at[p, (y + k) % 4], gr.at[p, k - 1], g_s.at[p, k - 1], g_r.at[p, k - 1], ydev(k))

    def swap(p):
        return send(ft.at[p, other], fr.at[p], f_s.at[p], f_r.at[p], sibling)

    def collect(p):
        l = 2 * p + xh
        acc[...] = jnp.zeros_like(acc)

        def one(j, carry):
            rows = pl.ds(pl.multiple_of(j * MB_ROWS, MB_ROWS), MB_ROWS)
            hx[p, j, me8] = hs[l, xl, rows, :]
            dx[p, j, me8] = ds[l, c, rows, :]
            for src in range(8):

                @pl.when(src != me8)
                def _(src=src):
                    for ref, rs in ((hx, h_r), (dx, u_r)):
                        block = ref.at[p, j, src]
                        send(block, block, h_s.at[0, 0], rs.at[p, j, src], sibling).wait_recv()

            acc[...] += lax.dot_general(
                hx[p, j].reshape(8 * MB_ROWS, HALF),
                dx[p, j].reshape(8 * MB_ROWS, HALF),
                (((0,), (0,)), ((), ())),
                preferred_element_type=jnp.float32,
            )
            return carry

        lax.fori_loop(0, slots, one, 0)
        gs[p] = acc[...].astype(jnp.bfloat16).reshape(4, 128, HALF)
        for k in (1, 3, 2):
            gy(p, k).start()

    def add_up(p):
        for k in (1, 3, 2):
            gy(p, k).wait_recv()
        ft[p] = (f32(gs[p, y]) + f32(gr[p, 0]) + f32(gr[p, 1]) + f32(gr[p, 2])).reshape(2, 64, HALF)
        swap(p).start()

    here = pl.ds(pl.multiple_of(c * HALF, HALF), HALF)
    there = pl.ds(pl.multiple_of(other * HALF, HALF), HALF)

    def zr():
        return send(zsend, zres, zr_s, zr_r, zpartner)

    if FIRST_PAIR < 8:

        @pl.when(pair)
        def _():
            collect(1 - own_p)

    collect(own_p)
    if FIRST_PAIR < 8:

        @pl.when(pair)
        def _():
            add_up(1 - own_p)

    add_up(own_p)
    if FIRST_PAIR < 8:

        @pl.when(pair)
        def _():
            p = 1 - own_p
            swap(p).wait_recv()
            zsend[:, here] = ft[p, c]
            zsend[:, there] = fr[p]
            zr().start()

    swap(own_p).wait_recv()
    gw_out[0, :, here] = ft[own_p, c]
    gw_out[0, :, there] = fr[own_p]
    if FIRST_PAIR < 8:

        @pl.when(pair)
        def _():
            zr().wait_recv()
            gw_out[0] = gw_out[0] + zres[...]

    full = gw_out[0]
    per_row = jnp.sum(full * w_in[0].astype(jnp.float32), axis=1, keepdims=True)
    gg_out[...] = jnp.sum(jnp.where(eye, per_row, 0.0), axis=0, keepdims=True)
    gw_out[0] = full * gain_col

    if FIRST_PAIR < 8:

        @pl.when(pair)
        def _():
            zx().wait_send()
            zr().wait_send()

    def drain_gather(i, carry):
        p = (own_p + i) % planes
        for k in K:
            a1(p, k).wait_send()
            b1(p, k).wait_send()
            for src in range(4):
                a2(p, src, k).wait_send()
                b2(p, src, k).wait_send()
                d_a2(p, src, k).wait_send()
                d_b2(p, src, k).wait_send()
            d_a1(p, k).wait_send()
            d_b1(p, k).wait_send()
        d_own(p).wait_send()
        return carry

    lax.fori_loop(0, planes, drain_gather, 0)

    def drain_relay(j, carry):
        @pl.when(jnp.logical_not(last))
        def _():
            fx(j).wait_send()

        @pl.when(jnp.logical_not(first))
        def _():
            bx(j).wait_send()

        return carry

    lax.fori_loop(0, slots, drain_relay, 0)

    def drain_layers(l, carry):
        def drain_rows(j, carry):
            for_owners(l, lambda t, cc: share_h(l, j, t, cc).wait_send())
            for_owners(l, lambda t, cc: share_u(l, j, t, cc).wait_send())
            return carry

        return lax.fori_loop(0, slots, drain_rows, carry)

    lax.fori_loop(0, layers, drain_layers, 0)

    def drain_sums(p, carry):
        for k in K:
            gy(p, k).wait_send()
        swap(p).wait_send()
        return carry

    lax.fori_loop(0, planes, drain_sums, 0)


def shards(down_input, up_input, down_cot, up_cot, weight, gain):
    nl = 2 if FIRST_PAIR == 8 else 4
    np_ = nl // 2
    bf, f4 = jnp.bfloat16, jnp.float32
    dma = pltpu.SemaphoreType.DMA
    scratch = [
        pltpu.VMEM((nl, 4, 2, 2, 64, D), bf),
        pltpu.VMEM((nl, D, D), bf),
        pltpu.VMEM((nl, 2, 4 * MB_ROWS, HALF), bf),
        pltpu.VMEM((nl, 2, 4 * MB_ROWS, HALF), bf),
        pltpu.VMEM((np_, 4, 8, MB_ROWS, HALF), bf),
        pltpu.VMEM((np_, 4, 8, MB_ROWS, HALF), bf),
        pltpu.VMEM((HALF, HALF), f4),
        pltpu.VMEM((np_, 4, 128, HALF), bf),
        pltpu.VMEM((np_, 3, 128, HALF), bf),
        pltpu.VMEM((np_, 2, 64, HALF), f4),
        pltpu.VMEM((np_, 64, HALF), f4),
        pltpu.VMEM((64, D), f4),
        pltpu.VMEM((64, D), f4),
        pltpu.VMEM((nl, 4, MB_ROWS, D), bf),
        pltpu.VMEM((nl, 4, MB_ROWS, D), f4),
        pltpu.VMEM((nl, 4, MB_ROWS, 128), f4),
        pltpu.VMEM((4, MB_ROWS, D), bf),
        pltpu.VMEM((4, MB_ROWS, D), bf),
        pltpu.VMEM((4, MB_ROWS, D), bf),
        dma, dma,
        dma((np_, 3)), dma((np_, 3)), dma((np_, 3)), dma((np_, 3)),
        dma((np_, 4, 3)), dma((np_, 4, 3)), dma((np_, 4, 3)), dma((np_, 4, 3)),
        dma((np_, 31)), dma((np_,)),
        dma((4,)), dma((4,)), dma((4,)), dma((4,)),
        dma((8, 4)), dma((np_, 4, 8)), dma((8, 4)), dma((np_, 4, 8)),
        dma((np_, 3)), dma((np_, 3)), dma((np_,)), dma((np_,)),
        dma, dma,
        pltpu.SemaphoreType.REGULAR((2,)),
    ]
    vmem = pl.BlockSpec(memory_space=pltpu.VMEM)
    return pl.pallas_call(
        kernel,
        out_shape=(
            jax.ShapeDtypeStruct((1, 64, D), f4),
            jax.ShapeDtypeStruct((1, 64), f4),
        ),
        in_specs=[vmem] * 6,
        out_specs=(vmem, vmem),
        scratch_shapes=scratch,
        compiler_params=pltpu.CompilerParams(
            collective_id=0, has_side_effects=True, vmem_limit_bytes=56 * 1024 * 1024
        ),
    )(down_input, up_input, down_cot, up_cot, weight, gain)


def solution(mesh):
    rows = P(None, "dp", None)
    return jax.shard_map(
        shards,
        mesh=mesh,
        in_specs=(rows, rows, rows, rows, P("section", "dp", None), P("section", "dp")),
        out_specs=(P("section", "dp", None), P("section", "dp")),
        check_vma=False,
    )
```

```python
import functools
import math

import jax
import jax.numpy as jnp
from jax import lax
from jax.experimental import pallas as pl
from jax.experimental.pallas import tpu as pltpu
from jax.sharding import PartitionSpec as P

EPSILON = 1e-05
CUBIC = 0.044715
SLOPE = math.sqrt(2.0 / math.pi)
MESH = pl.DeviceIdType.MESH
FIRST_PAIR = 2
D = 1024
HALF = D // 2
MB_ROWS = 32


def kernel(
    down_in, up_in, down_cot, up_cot, w_in, g_in, gw_out, gg_out,
    wv, w, wt, hs, ds, hx, dx, acc, gs, gr, zres, zsend, xs, sl, rinv, xo, do, cot,
    zx_s, zx_r, a1_s, a1_r, b1_s, b1_r, a2_s, a2_r, b2_s, b2_r, a3_s, a3_r, b3_s, b3_r, d_s, d_r,
    fx_s, fx_r, bx_s, bx_r, h_s, h_r, u_s, u_r, g_s, g_r, zr_s, zr_r, above, w_sem, in_sem,
):
    sec, dp = lax.axis_index("section"), lax.axis_index("dp")
    z, xh = sec // 2, sec % 2
    y, xl, c = dp // 4, (dp // 2) % 2, dp % 2
    x = xh * 2 + xl
    other = 1 - c

    def at(ax, ay, az, ac):
        return (az * 2 + ax // 2, ay * 4 + (ax % 2) * 2 + ac)

    def xdev(k):
        return at((x + k) % 4, y, z, c)

    def ydev(k):
        return at(x, (y + k) % 4, z, c)

    def zdev(k):
        return at(x, y, (z + 8 + k) % 8, c)

    sibling = at(x, y, z, other)
    pair = z >= FIRST_PAIR
    single = z < FIRST_PAIR
    ispair = pair.astype(jnp.int32) if FIRST_PAIR < 8 else 0
    odd = (z % 2) * ispair
    planes = 1 + ispair
    layers = 2 * planes
    slots = 4 // planes
    own_p = odd
    own_l = 2 * own_p + xh
    zpartner = at(x, y, z + 1 - 2 * (z % 2), c)

    load_w = pltpu.make_async_copy(w_in.at[0], wv, w_sem)
    load_w.start()
    barrier = pltpu.get_barrier_semaphore()
    peers = [sibling] + [xdev(k) for k in (1, 2, 3)] + [ydev(k) for k in (1, 2, 3)]
    peers += [at((x + k) % 4, y, z, other) for k in (1, 2, 3)]
    peers += [at(x, (y + k) % 4, z, other) for k in (1, 2, 3)]
    for peer in peers:
        pl.semaphore_signal(barrier, inc=1, device_id=peer, device_id_type=MESH)
    for k in (1, 2):

        @pl.when(z + k < 8)
        def _(k=k):
            pl.semaphore_signal(barrier, inc=1, device_id=zdev(k), device_id_type=MESH)

    if FIRST_PAIR < 8:

        @pl.when(odd == 1)
        def _():
            pl.semaphore_signal(barrier, inc=1, device_id=zpartner, device_id_type=MESH)

    def wait_above():
        for k in (1, 2):

            @pl.when(z + k < 8)
            def _(k=k):
                pl.semaphore_wait(above.at[k - 1], 1)

    def send(src, dst, ss, rs, to):
        return pltpu.make_async_remote_copy(
            src_ref=src, dst_ref=dst, send_sem=ss, recv_sem=rs, device_id=to, device_id_type=MESH
        )

    eye = lax.broadcasted_iota(jnp.int32, (64, 64), 0) == lax.broadcasted_iota(jnp.int32, (64, 64), 1)
    gain_col = jnp.sum(jnp.where(eye, g_in[...].astype(jnp.float32), 0.0), axis=1, keepdims=True)
    load_w.wait()
    w[own_l, y, xl, c] = (wv[...].astype(jnp.float32) * gain_col).astype(jnp.bfloat16)
    pl.semaphore_wait(barrier, len(peers) + jnp.minimum(z, 2) + (ispair - odd))
    for k in (1, 2):

        @pl.when(z >= k)
        def _(k=k):
            pl.semaphore_signal(above.at[k - 1], inc=1, device_id=zdev(-k), device_id_type=MESH)


    A, B, ALL = pl.ds(0, HALF), pl.ds(HALF, HALF), pl.ds(0, D)

    def blk(p, bx, by, cols):
        return w.at[2 * p + bx // 2, by, bx % 2, c, :, cols]

    def zx():
        ref = w.at[own_l, y, xl, c]
        return send(ref, ref, zx_s, zx_r, zpartner)

    def zx_other():
        ref = w.at[2 * (1 - own_p) + xh, y, xl, c]
        return send(ref, ref, zx_s, zx_r, zpartner)

    def a1(p, k):
        ref = blk(p, x, y, A)
        return send(ref, ref, a1_s.at[p, k - 1], a1_r.at[p, k - 1], xdev(k))

    def b1(p, k):
        ref = blk(p, x, y, B)
        return send(ref, ref, b1_s.at[p, k - 1], b1_r.at[p, k - 1], ydev(k))

    def a2(p, src, k):
        ref = blk(p, (x - src + 4) % 4, y, A)
        return send(ref, ref, a2_s.at[p, src, k // 2], a2_r.at[p, src, k // 2], ydev(k))

    def b2(p, src, k):
        ref = blk(p, x, (y - src + 4) % 4, B)
        return send(ref, ref, b2_s.at[p, src, k // 2], b2_r.at[p, src, k // 2], xdev(k))

    def half_blk(p, bx, by, cols, k):
        return w.at[2 * p + bx // 2, by, bx % 2, c, pl.ds(32 * (k // 2), 32), cols]

    def a3(p, src, k):
        ref = half_blk(p, (x - src + 4) % 4, (y - k + 4) % 4, A, k)
        return send(ref, ref, a3_s.at[p, src, k // 2], a3_r.at[p, src, k // 2], ydev(k))

    def b3(p, src, k):
        ref = half_blk(p, (x - k + 4) % 4, (y - src + 4) % 4, B, k)
        return send(ref, ref, b3_s.at[p, src, k // 2], b3_r.at[p, src, k // 2], xdev(k))

    def a3_wait(p, src, k):
        ref = half_blk(p, (x - src + 4) % 4, (y + 2) % 4, A, k)
        return send(ref, ref, a3_s.at[p, src, k // 2], a3_r.at[p, src, k // 2], sibling)

    def b3_wait(p, src, k):
        ref = half_blk(p, (x + 2) % 4, (y - src + 4) % 4, B, k)
        return send(ref, ref, b3_s.at[p, src, k // 2], b3_r.at[p, src, k // 2], sibling)

    def d_a2(p, src, k):
        ref = blk(p, (x - src + 4) % 4, (y - k + 4) % 4, A)
        return send(ref, ref, d_s.at[p, 7 + 2 * src + k // 2], d_r.at[p], sibling)

    def d_b2(p, src, k):
        ref = blk(p, (x - k + 4) % 4, (y - src + 4) % 4, B)
        return send(ref, ref, d_s.at[p, 15 + 2 * src + k // 2], d_r.at[p], sibling)

    def d_a3(p, src, k):
        ref = half_blk(p, (x - src + 4) % 4, (y + 2) % 4, A, k)
        return send(ref, ref, d_s.at[p, 23 + 2 * src + k // 2], d_r.at[p], sibling)

    def d_b3(p, src, k):
        ref = half_blk(p, (x + 2) % 4, (y - src + 4) % 4, B, k)
        return send(ref, ref, d_s.at[p, 31 + 2 * src + k // 2], d_r.at[p], sibling)

    def a2_wait(p, src, k):
        ref = blk(p, (x - src + 4) % 4, (y - k + 4) % 4, A)
        return send(ref, ref, a2_s.at[p, src, k // 2], a2_r.at[p, src, k // 2], sibling)

    def b2_wait(p, src, k):
        ref = blk(p, (x - k + 4) % 4, (y - src + 4) % 4, B)
        return send(ref, ref, b2_s.at[p, src, k // 2], b2_r.at[p, src, k // 2], sibling)

    def d_own(p):
        ref = blk(p, x, y, ALL)
        return send(ref, ref, d_s.at[p, 0], d_r.at[p], sibling)

    def d_a1(p, k):
        ref = blk(p, (x - k + 4) % 4, y, A)
        return send(ref, ref, d_s.at[p, k], d_r.at[p], sibling)

    def d_b1(p, k):
        ref = blk(p, x, (y - k + 4) % 4, B)
        return send(ref, ref, d_s.at[p, 3 + k], d_r.at[p], sibling)

    def d_wait(p):
        ref = w.at[pl.ds(2 * p, 2), :, :, other]
        return send(ref, ref, d_s.at[p, 0], d_r.at[p], sibling)

    K, N = (1, 2, 3), (1, 3)
    if FIRST_PAIR < 8:

        @pl.when(pair)
        def _():
            zx().start()

    def gather_start(i, carry):
        p = (own_p + i) % planes

        @pl.when(i > 0)
        def _():
            zx_other().wait_recv()

        d_own(p).start()
        for k in (1, 3):
            a1(p, k).start()
            b1(p, k).start()
        a1(p, 2).start()
        b1(p, 2).start()
        for k in N:
            a2(p, 0, k).start()
            b2(p, 0, k).start()
        return carry

    def onward(p, src):
        a1(p, src).wait_recv()
        for k in N:
            a2(p, src, k).start()
        d_a1(p, src).start()
        b1(p, src).wait_recv()
        for k in N:
            b2(p, src, k).start()
        d_b1(p, src).start()

    def arrived(p, src):
        for k in N:
            a2_wait(p, src, k).wait_recv()
            a3(p, src, k).start()
            d_a2(p, src, k).start()
            b2_wait(p, src, k).wait_recv()
            b3(p, src, k).start()
            d_b2(p, src, k).start()

    def far_side(p, src):
        for k in N:
            a3_wait(p, src, k).wait_recv()
            d_a3(p, src, k).start()
            b3_wait(p, src, k).wait_recv()
            d_b3(p, src, k).start()

    def gather_mid(i, carry):
        p = (own_p + i) % planes
        for src in (1, 3, 2):
            onward(p, src)
        arrived(p, 0)
        return carry

    def gather_end(i, carry):
        p = (own_p + i) % planes
        arrived(p, 1)
        arrived(p, 3)
        far_side(p, 0)
        arrived(p, 2)
        far_side(p, 1)
        far_side(p, 3)
        far_side(p, 2)
        return carry

    def gather_wait(i, carry):
        d_wait((own_p + i) % planes).wait_recv()
        return carry

    lax.fori_loop(0, planes, gather_start, 0)

    first = z < (2 if FIRST_PAIR == 0 else 1)
    last = z >= (7 if FIRST_PAIR == 8 else 6)

    def rows_in(ref, dst, slot, j):
        rows = pl.ds(pl.multiple_of((j % 2) * MB_ROWS, MB_ROWS), MB_ROWS)
        return pltpu.make_async_copy(ref.at[j // 2, rows, :], dst.at[slot], in_sem.at[slot])

    def load_rows(dst, down, up):
        def one(slot, carry):
            j = slot * planes + odd
            for ref, cond in ((down, xh == 0), (up, xh == 1)):

                @pl.when(cond)
                def _(ref=ref):
                    rows_in(ref, dst, slot, j).start()

            return carry

        lax.fori_loop(0, slots, one, 0)

    @pl.when(first)
    def _():
        load_rows(xs.at[0], down_in, up_in)

    @pl.when(last)
    def _():
        load_rows(cot, down_cot, up_cot)

    lax.fori_loop(0, planes, gather_mid, 0)
    lax.fori_loop(0, planes, gather_end, 0)
    lax.fori_loop(0, planes, gather_wait, 0)

    if FIRST_PAIR == 8:

        def f_route(j):
            return zdev(1), j

        def b_route(j):
            return zdev(-1), j

    else:
        to_pair = (z == FIRST_PAIR - 1).astype(jnp.int32)
        from_pair = ((z // 2) * 2 == FIRST_PAIR).astype(jnp.int32)

        def f_route(j):
            step = ispair * 2 + (1 - ispair) * (1 + to_pair * (j % 2))
            slot = j - to_pair * (j - j // 2)
            return zdev(step), slot

        def b_route(j):
            step = ispair * (2 + from_pair * (odd - 1)) + (1 - ispair)
            slot = j + from_pair * (j + odd)
            return zdev(-step), slot

    def fx(j):
        to, slot = f_route(j)
        return send(xo.at[j], xs.at[0, slot], fx_s.at[j], fx_r.at[slot], to)

    def fx_wait(j):
        return send(xo.at[j], xs.at[0, j], fx_s.at[j], fx_r.at[j], sibling)

    def bx(j):
        to, slot = b_route(j)
        return send(do.at[j], cot.at[slot], bx_s.at[j], bx_r.at[slot], to)

    def bx_wait(j):
        return send(do.at[j], cot.at[j], bx_s.at[j], bx_r.at[j], sibling)

    me8 = x * 2 + c

    def share(src, dst, ss, rs, l, j, t, cc):
        part = (t, cc)
        rows = pl.ds(pl.multiple_of(j * MB_ROWS, MB_ROWS), MB_ROWS)
        q = 2 * t + cc
        return send(
            src.at[l, part[0] if src is hs else part[1], rows, :],
            dst.at[l // 2, j, me8],
            ss.at[l * slots + j, q],
            rs.at[l // 2, j, me8],
            at(2 * (l % 2) + t, y, z, cc),
        )

    def for_owners(l, act):
        for t in range(2):
            for cc in range(2):

                @pl.when(jnp.logical_or(2 * (l % 2) + t != x, cc != c))
                def _(t=t, cc=cc):
                    act(t, cc)

    def share_h(l, j, t, cc):
        return share(hs, hx, h_s, h_r, l, j, t, cc)

    def share_u(l, j, t, cc):
        return share(ds, dx, u_s, u_r, l, j, t, cc)

    def forward(j, carry):
        @pl.when(first)
        def _():
            rows_in(down_in, xs.at[0], j, 0).wait()

        @pl.when(jnp.logical_not(first))
        def _():
            fx_wait(j).wait_recv()

        rows = pl.ds(pl.multiple_of(j * MB_ROWS, MB_ROWS), MB_ROWS)

        def layer(l, carry):
            xf = xs[l, j].astype(jnp.float32)
            r = lax.rsqrt(jnp.mean(xf * xf, axis=-1, keepdims=True) + EPSILON)
            normed = (xf * r).astype(jnp.bfloat16)
            for t in range(2):
                for b in range(4):
                    hs[l, t, rows, b * 128 : (b + 1) * 128] = normed[:, b * 256 + t * 128 : b * 256 + (t + 1) * 128]
            rinv[l, j] = jnp.broadcast_to(r, (MB_ROWS, 128))
            u = jnp.dot(normed, w[l].reshape(D, D), preferred_element_type=jnp.float32)
            u2 = u * u
            t = jnp.tanh(SLOPE * (u + CUBIC * u2 * u))
            nxt = (xf + 0.5 * u * (1.0 + t)).astype(jnp.bfloat16)

            @pl.when(l < layers - 1)
            def _():
                xs[l + 1, j] = nxt

            @pl.when(l == layers - 1)
            def _():
                xo[j] = nxt

                @pl.when(jnp.logical_not(last))
                def _():
                    fx(j).start()

            sl[l, j] = 0.5 * (1.0 + t) + 0.5 * u * (1.0 - t * t) * SLOPE * (1.0 + 3.0 * CUBIC * u2)
            for_owners(l, lambda t, cc: share_h(l, j, t, cc).start())
            return carry

        return lax.fori_loop(0, layers, layer, carry)

    def turn(l, carry):
        wt[l] = w[l].reshape(D, D).T
        return carry

    @pl.when(last)
    def _():
        lax.fori_loop(0, layers, turn, 0)

    wait_above()
    lax.fori_loop(0, slots, forward, 0)

    @pl.when(jnp.logical_not(last))
    def _():
        lax.fori_loop(0, layers, turn, 0)


    def backward(j, carry):
        @pl.when(last)
        def _():
            rows_in(down_cot, cot, j, 0).wait()

        @pl.when(jnp.logical_not(last))
        def _():
            bx_wait(j).wait_recv()

        rows = pl.ds(pl.multiple_of(j * MB_ROWS, MB_ROWS), MB_ROWS)

        def layer(i, carry):
            l = layers - 1 - i
            df = cot[j].astype(jnp.float32)
            grad = (df * sl[l, j]).astype(jnp.bfloat16)
            ds[l, 0, rows, :] = grad[:, 0:HALF]
            ds[l, 1, rows, :] = grad[:, HALF:D]

            @pl.when(jnp.logical_not(jnp.logical_and(first, l == 0)))
            def _():
                a = jnp.dot(grad, wt[l], preferred_element_type=jnp.float32)
                r = rinv[l, j][:, 0:1]
                xr = xs[l, j].astype(jnp.float32) * r
                new = (df + r * (a - xr * jnp.mean(a * xr, axis=-1, keepdims=True))).astype(jnp.bfloat16)

                @pl.when(l > 0)
                def _():
                    cot[j] = new

                @pl.when(l == 0)
                def _():
                    do[j] = new
                    bx(j).start()

            for_owners(l, lambda t, cc: share_u(l, j, t, cc).start())
            return carry

        return lax.fori_loop(0, layers, layer, carry)

    lax.fori_loop(0, slots, backward, 0)

    def f32(v):
        return v.astype(jnp.float32)

    def gy(p, k, cc):
        to_y = (y + k) % 4
        return send(gs.at[p, to_y, cc], gr.at[p, c, k], g_s.at[p, k, cc], g_r.at[p, c, k], at(x, to_y, z, cc))

    def for_sums(p, act):
        for k in (1, 3, 2, 0):
            for cc in range(2):
                if k == 0:

                    @pl.when(cc != c)
                    def _(k=k, cc=cc):
                        act(p, k, cc)

                else:
                    act(p, k, cc)

    def sum_wait(p, k, cs):
        return send(gr.at[p, cs, k], gr.at[p, cs, k], g_s.at[p, k, cs], g_r.at[p, cs, k], sibling)

    def collect(p):
        l = 2 * p + xh
        acc[...] = jnp.zeros_like(acc)

        def one(j, carry):
            rows = pl.ds(pl.multiple_of(j * MB_ROWS, MB_ROWS), MB_ROWS)
            hx[p, j, me8] = hs[l, xl, rows, :]
            dx[p, j, me8] = ds[l, c, rows, :]
            for src in range(8):

                @pl.when(src != me8)
                def _(src=src):
                    for ref, rs in ((hx, h_r), (dx, u_r)):
                        block = ref.at[p, j, src]
                        send(block, block, h_s.at[0, 0], rs.at[p, j, src], sibling).wait_recv()

            acc[...] += lax.dot_general(
                hx[p, j].reshape(8 * MB_ROWS, HALF),
                dx[p, j].reshape(8 * MB_ROWS, HALF),
                (((0,), (0,)), ((), ())),
                preferred_element_type=jnp.float32,
            )
            return carry

        lax.fori_loop(0, slots, one, 0)
        gs[p] = acc[...].astype(jnp.bfloat16).reshape(4, 2, 64, HALF)
        for_sums(p, lambda p, k, cc: gy(p, k, cc).start())
        gr[p, c, 0] = gs[p, y, c]

    def add_up(p, out):
        for cs in range(2):

            @pl.when(cs != c)
            def _(cs=cs):
                sum_wait(p, 0, cs).wait_recv()

            for k in (1, 3, 2):
                sum_wait(p, k, cs).wait_recv()
            out[:, cs * HALF : (cs + 1) * HALF] = (
                f32(gr[p, cs, 0]) + f32(gr[p, cs, 1]) + f32(gr[p, cs, 2]) + f32(gr[p, cs, 3])
            )

    def zr():
        return send(zsend, zres, zr_s, zr_r, zpartner)

    if FIRST_PAIR < 8:

        @pl.when(pair)
        def _():
            collect(1 - own_p)

    collect(own_p)
    if FIRST_PAIR < 8:

        @pl.when(pair)
        def _():
            add_up(1 - own_p, zsend)
            zr().start()

    add_up(own_p, gw_out.at[0])
    if FIRST_PAIR < 8:

        @pl.when(pair)
        def _():
            zr().wait_recv()
            gw_out[0] = gw_out[0] + zres[...]

    full = gw_out[0]
    per_row = jnp.sum(full * wv[...].astype(jnp.float32), axis=1, keepdims=True)
    gg_out[...] = jnp.sum(jnp.where(eye, per_row, 0.0), axis=0, keepdims=True)
    gw_out[0] = full * gain_col

    if FIRST_PAIR < 8:

        @pl.when(pair)
        def _():
            zx().wait_send()
            zr().wait_send()

    def drain_gather(i, carry):
        p = (own_p + i) % planes
        for k in K:
            a1(p, k).wait_send()
            b1(p, k).wait_send()
            d_a1(p, k).wait_send()
            d_b1(p, k).wait_send()
        for src in range(4):
            for k in N:
                for copy in (a2, b2, a3, b3, d_a2, d_b2, d_a3, d_b3):
                    copy(p, src, k).wait_send()
        d_own(p).wait_send()
        return carry

    lax.fori_loop(0, planes, drain_gather, 0)

    def drain_relay(j, carry):
        @pl.when(jnp.logical_not(last))
        def _():
            fx(j).wait_send()

        @pl.when(jnp.logical_not(first))
        def _():
            bx(j).wait_send()

        return carry

    lax.fori_loop(0, slots, drain_relay, 0)

    def drain_layers(l, carry):
        def drain_rows(j, carry):
            for_owners(l, lambda t, cc: share_h(l, j, t, cc).wait_send())
            for_owners(l, lambda t, cc: share_u(l, j, t, cc).wait_send())
            return carry

        return lax.fori_loop(0, slots, drain_rows, carry)

    lax.fori_loop(0, layers, drain_layers, 0)

    def drain_sums(p, carry):
        for_sums(p, lambda p, k, cc: gy(p, k, cc).wait_send())
        return carry

    lax.fori_loop(0, planes, drain_sums, 0)


def shards(down_input, up_input, down_cot, up_cot, weight, gain):
    nl = 2 if FIRST_PAIR == 8 else 4
    np_ = nl // 2
    bf, f4 = jnp.bfloat16, jnp.float32
    dma = pltpu.SemaphoreType.DMA
    scratch = [
        pltpu.VMEM((64, D), bf),
        pltpu.VMEM((nl, 4, 2, 2, 64, D), bf),
        pltpu.VMEM((nl, D, D), bf),
        pltpu.VMEM((nl, 2, 4 * MB_ROWS, HALF), bf),
        pltpu.VMEM((nl, 2, 4 * MB_ROWS, HALF), bf),
        pltpu.VMEM((np_, 4, 8, MB_ROWS, HALF), bf),
        pltpu.VMEM((np_, 4, 8, MB_ROWS, HALF), bf),
        pltpu.VMEM((HALF, HALF), f4),
        pltpu.VMEM((np_, 4, 2, 64, HALF), bf),
        pltpu.VMEM((np_, 2, 4, 64, HALF), bf),
        pltpu.VMEM((64, D), f4),
        pltpu.VMEM((64, D), f4),
        pltpu.VMEM((nl, 4, MB_ROWS, D), bf),
        pltpu.VMEM((nl, 4, MB_ROWS, D), f4),
        pltpu.VMEM((nl, 4, MB_ROWS, 128), f4),
        pltpu.VMEM((4, MB_ROWS, D), bf),
        pltpu.VMEM((4, MB_ROWS, D), bf),
        pltpu.VMEM((4, MB_ROWS, D), bf),
        dma, dma,
        dma((np_, 3)), dma((np_, 3)), dma((np_, 3)), dma((np_, 3)),
        dma((np_, 4, 2)), dma((np_, 4, 2)), dma((np_, 4, 2)), dma((np_, 4, 2)),
        dma((np_, 4, 2)), dma((np_, 4, 2)), dma((np_, 4, 2)), dma((np_, 4, 2)),
        dma((np_, 39)), dma((np_,)),
        dma((4,)), dma((4,)), dma((4,)), dma((4,)),
        dma((8, 4)), dma((np_, 4, 8)), dma((8, 4)), dma((np_, 4, 8)),
        dma((np_, 4, 2)), dma((np_, 2, 4)),
        dma, dma,
        pltpu.SemaphoreType.REGULAR((2,)),
        dma, dma((4,)),
    ]
    vmem = pl.BlockSpec(memory_space=pltpu.VMEM)
    return pl.pallas_call(
        kernel,
        out_shape=(
            jax.ShapeDtypeStruct((1, 64, D), f4),
            jax.ShapeDtypeStruct((1, 64), f4),
        ),
        in_specs=[pl.BlockSpec(memory_space=pl.ANY)] * 5 + [vmem],
        out_specs=(vmem, vmem),
        scratch_shapes=scratch,
        compiler_params=pltpu.CompilerParams(
            collective_id=0, has_side_effects=True, vmem_limit_bytes=56 * 1024 * 1024
        ),
    )(down_input, up_input, down_cot, up_cot, weight, gain)


def solution(mesh):
    rows = P(None, "dp", None)
    return jax.shard_map(
        shards,
        mesh=mesh,
        in_specs=(rows, rows, rows, rows, P("section", "dp", None), P("section", "dp")),
        out_specs=(P("section", "dp", None), P("section", "dp")),
        check_vma=False,
    )
```

```python
import functools
import math

import jax
import jax.numpy as jnp
from jax import lax
from jax.experimental import pallas as pl
from jax.experimental.pallas import tpu as pltpu
from jax.sharding import PartitionSpec as P

EPSILON = 1e-05
CUBIC = 0.044715
SLOPE = math.sqrt(2.0 / math.pi)
MESH = pl.DeviceIdType.MESH
FIRST_PAIR = 2
D = 1024
HALF = D // 2
MB_ROWS = 32


def kernel(
    down_in, up_in, down_cot, up_cot, w_in, g_in, gw_out, gg_out,
    wv, w, wt, hs, ds, hx, dx, acc, gs, gr, zres, zsend, xs, sl, rinv, do, cot,
    zx_s, zx_r, a1_s, a1_r, b1_s, b1_r, a2_s, a2_r, b2_s, b2_r, a3_s, a3_r, b3_s, b3_r, d_s, d_r,
    fx_s, fx_r, bx_s, bx_r, h_s, h_r, hf_s, u_s, u_r, g_s, g_r, zr_s, zr_r, above, w_sem, in_sem,
):
    sec, dp = lax.axis_index("section"), lax.axis_index("dp")
    z, xh = sec // 2, sec % 2
    y, xl, c = dp // 4, (dp // 2) % 2, dp % 2
    x = xh * 2 + xl
    other = 1 - c

    def at(ax, ay, az, ac):
        return (az * 2 + ax // 2, ay * 4 + (ax % 2) * 2 + ac)

    def xdev(k):
        return at((x + k) % 4, y, z, c)

    def ydev(k):
        return at(x, (y + k) % 4, z, c)

    def zdev(k):
        return at(x, y, (z + 8 + k) % 8, other)

    sibling = at(x, y, z, other)
    pair = z >= FIRST_PAIR
    single = z < FIRST_PAIR
    ispair = pair.astype(jnp.int32) if FIRST_PAIR < 8 else 0
    odd = (z % 2) * ispair
    planes = 1 + ispair
    layers = 2 * planes
    slots = 4 // planes
    own_p = odd
    own_l = 2 * own_p + xh
    zpartner = at(x, y, z + 1 - 2 * (z % 2), c)

    load_w = pltpu.make_async_copy(w_in.at[0], wv, w_sem)
    load_w.start()
    barrier = pltpu.get_barrier_semaphore()
    peers = [sibling] + [xdev(k) for k in (1, 2, 3)] + [ydev(k) for k in (1, 2, 3)]
    peers += [at((x + k) % 4, y, z, other) for k in (1, 2, 3)]
    peers += [at(x, (y + k) % 4, z, other) for k in (1, 2, 3)]
    beside = x + 1 - 2 * xl
    peers += [at(beside, (y + k) % 4, z, ac) for k in (1, 2, 3) for ac in (0, 1)]
    for peer in peers:
        pl.semaphore_signal(barrier, inc=1, device_id=peer, device_id_type=MESH)
    for k in (1, 2):

        @pl.when(z + k < 8)
        def _(k=k):
            pl.semaphore_signal(barrier, inc=1, device_id=zdev(k), device_id_type=MESH)

    if FIRST_PAIR < 8:

        @pl.when(pair)
        def _():
            pl.semaphore_signal(barrier, inc=1, device_id=zpartner, device_id_type=MESH)

    def wait_above():
        for k in (1, 2):

            @pl.when(z + k < 8)
            def _(k=k):
                pl.semaphore_wait(above.at[k - 1], 1)

    def send(src, dst, ss, rs, to):
        return pltpu.make_async_remote_copy(
            src_ref=src, dst_ref=dst, send_sem=ss, recv_sem=rs, device_id=to, device_id_type=MESH
        )

    eye = lax.broadcasted_iota(jnp.int32, (64, 64), 0) == lax.broadcasted_iota(jnp.int32, (64, 64), 1)
    gain_col = jnp.sum(jnp.where(eye, g_in[...].astype(jnp.float32), 0.0), axis=1, keepdims=True)
    load_w.wait()
    w[own_l, y, xl, c] = (wv[...].astype(jnp.float32) * gain_col).astype(jnp.bfloat16)
    pl.semaphore_wait(barrier, len(peers) + jnp.minimum(z, 2) + ispair)
    for k in (1, 2):

        @pl.when(z >= k)
        def _(k=k):
            pl.semaphore_signal(above.at[k - 1], inc=1, device_id=zdev(-k), device_id_type=MESH)


    A, B, ALL = pl.ds(0, HALF), pl.ds(HALF, HALF), pl.ds(0, D)

    def blk(p, bx, by, cols):
        return w.at[2 * p + bx // 2, by, bx % 2, c, :, cols]

    def zx():
        ref = w.at[own_l, y, xl, c]
        return send(ref, ref, zx_s, zx_r, zpartner)

    def zx_other():
        ref = w.at[2 * (1 - own_p) + xh, y, xl, c]
        return send(ref, ref, zx_s, zx_r, zpartner)

    def a1(p, k):
        ref = blk(p, x, y, A)
        return send(ref, ref, a1_s.at[p, k - 1], a1_r.at[p, k - 1], xdev(k))

    def b1(p, k):
        ref = blk(p, x, y, B)
        return send(ref, ref, b1_s.at[p, k - 1], b1_r.at[p, k - 1], ydev(k))

    def a2(p, src, k):
        ref = blk(p, (x - src + 4) % 4, y, A)
        return send(ref, ref, a2_s.at[p, src, k // 2], a2_r.at[p, src, k // 2], ydev(k))

    def b2(p, src, k):
        ref = blk(p, x, (y - src + 4) % 4, B)
        return send(ref, ref, b2_s.at[p, src, k // 2], b2_r.at[p, src, k // 2], xdev(k))

    def half_blk(p, bx, by, cols, k):
        return w.at[2 * p + bx // 2, by, bx % 2, c, pl.ds(32 * (k // 2), 32), cols]

    def a3(p, src, k):
        ref = half_blk(p, (x - src + 4) % 4, (y - k + 4) % 4, A, k)
        return send(ref, ref, a3_s.at[p, src, k // 2], a3_r.at[p, src, k // 2], ydev(k))

    def b3(p, src, k):
        ref = half_blk(p, (x - k + 4) % 4, (y - src + 4) % 4, B, k)
        return send(ref, ref, b3_s.at[p, src, k // 2], b3_r.at[p, src, k // 2], xdev(k))

    def a3_wait(p, src, k):
        ref = half_blk(p, (x - src + 4) % 4, (y + 2) % 4, A, k)
        return send(ref, ref, a3_s.at[p, src, k // 2], a3_r.at[p, src, k // 2], sibling)

    def b3_wait(p, src, k):
        ref = half_blk(p, (x + 2) % 4, (y - src + 4) % 4, B, k)
        return send(ref, ref, b3_s.at[p, src, k // 2], b3_r.at[p, src, k // 2], sibling)

    def d_a2(p, src, k):
        ref = blk(p, (x - src + 4) % 4, (y - k + 4) % 4, A)
        return send(ref, ref, d_s.at[p, 7 + 2 * src + k // 2], d_r.at[p], sibling)

    def d_b2(p, src, k):
        ref = blk(p, (x - k + 4) % 4, (y - src + 4) % 4, B)
        return send(ref, ref, d_s.at[p, 15 + 2 * src + k // 2], d_r.at[p], sibling)

    def d_a3(p, src, k):
        ref = half_blk(p, (x - src + 4) % 4, (y + 2) % 4, A, k)
        return send(ref, ref, d_s.at[p, 23 + 2 * src + k // 2], d_r.at[p], sibling)

    def d_b3(p, src, k):
        ref = half_blk(p, (x + 2) % 4, (y - src + 4) % 4, B, k)
        return send(ref, ref, d_s.at[p, 31 + 2 * src + k // 2], d_r.at[p], sibling)

    def a2_wait(p, src, k):
        ref = blk(p, (x - src + 4) % 4, (y - k + 4) % 4, A)
        return send(ref, ref, a2_s.at[p, src, k // 2], a2_r.at[p, src, k // 2], sibling)

    def b2_wait(p, src, k):
        ref = blk(p, (x - k + 4) % 4, (y - src + 4) % 4, B)
        return send(ref, ref, b2_s.at[p, src, k // 2], b2_r.at[p, src, k // 2], sibling)

    def d_own(p):
        ref = blk(p, x, y, ALL)
        return send(ref, ref, d_s.at[p, 0], d_r.at[p], sibling)

    def d_a1(p, k):
        ref = blk(p, (x - k + 4) % 4, y, A)
        return send(ref, ref, d_s.at[p, k], d_r.at[p], sibling)

    def d_b1(p, k):
        ref = blk(p, x, (y - k + 4) % 4, B)
        return send(ref, ref, d_s.at[p, 3 + k], d_r.at[p], sibling)

    def d_wait(p):
        ref = w.at[pl.ds(2 * p, 2), :, :, other]
        return send(ref, ref, d_s.at[p, 0], d_r.at[p], sibling)

    K, N = (1, 2, 3), (1, 3)
    if FIRST_PAIR < 8:

        @pl.when(pair)
        def _():
            zx().start()

    def gather_start(i, carry):
        p = (own_p + i) % planes

        @pl.when(i > 0)
        def _():
            zx_other().wait_recv()

        d_own(p).start()
        for k in (1, 3):
            a1(p, k).start()
            b1(p, k).start()
        a1(p, 2).start()
        b1(p, 2).start()
        for k in N:
            a2(p, 0, k).start()
            b2(p, 0, k).start()
        return carry

    def onward(p, src):
        a1(p, src).wait_recv()
        for k in N:
            a2(p, src, k).start()
        d_a1(p, src).start()
        b1(p, src).wait_recv()
        for k in N:
            b2(p, src, k).start()
        d_b1(p, src).start()

    def arrived(p, src):
        for k in N:
            a2_wait(p, src, k).wait_recv()
            a3(p, src, k).start()
            d_a2(p, src, k).start()
            b2_wait(p, src, k).wait_recv()
            b3(p, src, k).start()
            d_b2(p, src, k).start()

    def far_side(p, src):
        for k in N:
            a3_wait(p, src, k).wait_recv()
            d_a3(p, src, k).start()
            b3_wait(p, src, k).wait_recv()
            d_b3(p, src, k).start()

    def gather_mid(i, carry):
        p = (own_p + i) % planes
        for src in (1, 3, 2):
            onward(p, src)
        arrived(p, 0)
        return carry

    def gather_end(i, carry):
        p = (own_p + i) % planes
        arrived(p, 1)
        arrived(p, 3)
        far_side(p, 0)
        arrived(p, 2)
        far_side(p, 1)
        far_side(p, 3)
        far_side(p, 2)
        return carry

    def gather_wait(i, carry):
        d_wait((own_p + i) % planes).wait_recv()
        return carry

    lax.fori_loop(0, planes, gather_start, 0)

    first = z < (2 if FIRST_PAIR == 0 else 1)
    last = z >= (7 if FIRST_PAIR == 8 else 6)

    def rows_in(ref, dst, slot, j):
        rows = pl.ds(pl.multiple_of((j % 2) * MB_ROWS, MB_ROWS), MB_ROWS)
        return pltpu.make_async_copy(ref.at[j // 2, rows, :], dst.at[slot], in_sem.at[slot])

    def load_rows(dst, down, up):
        def one(slot, carry):
            j = slot * planes + odd
            for ref, cond in ((down, xh == 0), (up, xh == 1)):

                @pl.when(cond)
                def _(ref=ref):
                    rows_in(ref, dst, slot, j).start()

            return carry

        lax.fori_loop(0, slots, one, 0)

    @pl.when(first)
    def _():
        load_rows(xs.at[0], down_in, up_in)

    @pl.when(last)
    def _():
        load_rows(cot, down_cot, up_cot)

    lax.fori_loop(0, planes, gather_mid, 0)
    lax.fori_loop(0, planes, gather_end, 0)
    lax.fori_loop(0, planes, gather_wait, 0)

    if FIRST_PAIR == 8:

        def f_route(j):
            return zdev(1), j

        def b_route(j):
            return zdev(-1), j

    else:
        to_pair = (z == FIRST_PAIR - 1).astype(jnp.int32)
        from_pair = ((z // 2) * 2 == FIRST_PAIR).astype(jnp.int32)

        def f_route(j):
            step = ispair * 2 + (1 - ispair) * (1 + to_pair * (j % 2))
            slot = j - to_pair * (j - j // 2)
            return zdev(step), slot

        def b_route(j):
            step = ispair * (2 + from_pair * (odd - 1)) + (1 - ispair)
            slot = j + from_pair * (j + odd)
            return zdev(-step), slot

    def fx(j):
        to, slot = f_route(j)
        return send(xs.at[layers, j], xs.at[0, slot], fx_s.at[j], fx_r.at[slot], to)

    def fx_wait(j):
        return send(xs.at[layers, j], xs.at[0, j], fx_s.at[j], fx_r.at[j], sibling)

    def bx(j):
        to, slot = b_route(j)
        return send(do.at[j], cot.at[slot], bx_s.at[j], bx_r.at[slot], to)

    def bx_wait(j):
        return send(do.at[j], cot.at[j], bx_s.at[j], bx_r.at[j], sibling)

    me8 = x * 2 + c

    quarter = 2 * xl + c
    WIDE = D // 4

    def mb_rows(j):
        return pl.ds(pl.multiple_of(j * MB_ROWS, MB_ROWS), MB_ROWS)

    def share_h(l, j, t):
        to_x = 2 * (l % 2) + t
        near = (to_x == x).astype(jnp.int32)
        core = c + near * (1 - 2 * c)
        return send(
            hs.at[l, mb_rows(j), :], hx.at[l // 2, j, me8], h_s.at[l * slots + j, t], h_r.at[l // 2, j, me8],
            at(to_x, y, z, core),
        )

    def hand_h(p, j, k):
        src = ((x + k) % 4) * 2 + c
        ref = hx.at[p, j, src]
        return send(ref, ref, hf_s.at[p, j, k - 1], h_r.at[p, j, src], sibling)

    def hand_over(p):
        def one(j, carry):
            for k in K:
                hand_h(p, j, k).wait_recv()
                hand_h(p, j, k).start()
            return carry

        lax.fori_loop(0, slots, one, 0)

    def share_u(l, j, t, cc):
        return send(
            ds.at[l, 2 * t + cc, mb_rows(j), :], dx.at[l // 2, j, me8], u_s.at[l * slots + j, 2 * t + cc],
            u_r.at[l // 2, j, me8], at(2 * (l % 2) + t, y, z, cc),
        )

    def for_owners(l, act):
        for t in range(2):
            for cc in range(2):

                @pl.when(jnp.logical_or(2 * (l % 2) + t != x, cc != c))
                def _(t=t, cc=cc):
                    act(t, cc)

    def f32(v):
        return v.astype(jnp.float32)

    def forward_layers(j, count):
        rows = pl.ds(pl.multiple_of(j * MB_ROWS, MB_ROWS), MB_ROWS)
        xf = f32(xs[0, j])
        for l in range(count):
            r = lax.rsqrt(jnp.mean(xf * xf, axis=-1, keepdims=True) + EPSILON)
            normed = (xf * r).astype(jnp.bfloat16)
            u = jnp.dot(normed, w[l].reshape(D, D), preferred_element_type=jnp.float32)
            t = jnp.tanh(SLOPE * (u + CUBIC * (u * u) * u))
            nxt = (xf + 0.5 * u * (1.0 + t)).astype(jnp.bfloat16)
            xs[l + 1, j] = nxt
            xf = f32(nxt)
            sl[l, j] = u
            rinv[l, j] = jnp.broadcast_to(r, (MB_ROWS, 128))
            hs[l, rows, :] = normed

    def forward(j, carry):
        @pl.when(first)
        def _():
            rows_in(down_in, xs.at[0], j, 0).wait()

        @pl.when(jnp.logical_not(first))
        def _():
            fx_wait(j).wait_recv()

        if FIRST_PAIR > 0:

            @pl.when(single)
            def _():
                forward_layers(j, 2)

        if FIRST_PAIR < 8:

            @pl.when(pair)
            def _():
                forward_layers(j, 4)

        @pl.when(jnp.logical_not(last))
        def _():
            fx(j).start()

        return carry

    def slopes(l, carry):
        def one(j, carry):
            u = sl[l, j]
            u2 = u * u
            t = jnp.tanh(SLOPE * (u + CUBIC * u2 * u))
            sl[l, j] = 0.5 * (1.0 + t) + 0.5 * u * (1.0 - t * t) * SLOPE * (1.0 + 3.0 * CUBIC * u2)
            return carry

        return lax.fori_loop(0, slots, one, carry)

    def turn(l, carry):
        wt[l] = w[l].reshape(D, D).T
        return carry

    def share_all_h(l, carry):
        def one(j, carry):
            for t in range(2):
                share_h(l, j, t).start()
            return carry

        return lax.fori_loop(0, slots, one, carry)

    def drain_gather(i, carry):
        p = (own_p + i) % planes
        for k in K:
            a1(p, k).wait_send()
            b1(p, k).wait_send()
            d_a1(p, k).wait_send()
            d_b1(p, k).wait_send()
        for src in range(4):
            for k in N:
                for copy in (a2, b2, a3, b3, d_a2, d_b2, d_a3, d_b3):
                    copy(p, src, k).wait_send()
        d_own(p).wait_send()
        return carry

    @pl.when(last)
    def _():
        lax.fori_loop(0, layers, turn, 0)

    wait_above()
    lax.fori_loop(0, slots, forward, 0)

    @pl.when(jnp.logical_not(last))
    def _():
        lax.fori_loop(0, layers, share_all_h, 0)
        lax.fori_loop(0, layers, turn, 0)

    lax.fori_loop(0, layers, slopes, 0)

    @pl.when(jnp.logical_not(last))
    def _():
        lax.fori_loop(0, planes, drain_gather, 0)

    if FIRST_PAIR > 0:

        @pl.when(single)
        def _():
            hand_over(0)

    def backward_layers(j, top, bottom):
        rows = pl.ds(pl.multiple_of(j * MB_ROWS, MB_ROWS), MB_ROWS)
        delta = cot[j]
        for l in range(top, bottom - 1, -1):
            df = f32(delta)
            grad = (df * sl[l, j]).astype(jnp.bfloat16)
            for q in range(4):
                ds[l, q, rows, :] = grad[:, q * WIDE : (q + 1) * WIDE]
            a = jnp.dot(grad, wt[l], preferred_element_type=jnp.float32)
            r = rinv[l, j][:, 0:1]
            xr = f32(xs[l, j]) * r
            delta = (df + r * (a - xr * jnp.mean(a * xr, axis=-1, keepdims=True))).astype(jnp.bfloat16)
        return delta

    def backward(j, carry):
        @pl.when(last)
        def _():
            rows_in(down_cot, cot, j, 0).wait()

        @pl.when(jnp.logical_not(last))
        def _():
            bx_wait(j).wait_recv()

        if FIRST_PAIR < 8:

            @pl.when(jnp.logical_and(pair, jnp.logical_not(first)))
            def _():
                do[j] = backward_layers(j, 3, 0)
                bx(j).start()

        if FIRST_PAIR > 0:

            @pl.when(jnp.logical_and(single, jnp.logical_not(first)))
            def _():
                do[j] = backward_layers(j, 1, 0)
                bx(j).start()

        @pl.when(first)
        def _():
            rows = pl.ds(pl.multiple_of(j * MB_ROWS, MB_ROWS), MB_ROWS)
            delta = backward_layers(j, 1 if FIRST_PAIR > 0 else 3, 1)
            grad = (f32(delta) * sl[0, j]).astype(jnp.bfloat16)
            for q in range(4):
                ds[0, q, rows, :] = grad[:, q * WIDE : (q + 1) * WIDE]

        @pl.when(first)
        def _():
            share_all_u(j)

        return carry

    def share_all_u(j):
        def one(l, carry):
            for_owners(l, lambda t, cc: share_u(l, j, t, cc).start())
            return carry

        lax.fori_loop(0, layers, one, 0)

    lax.fori_loop(0, slots, backward, 0)

    @pl.when(jnp.logical_not(first))
    def _():
        lax.fori_loop(0, slots, lambda j, carry: (share_all_u(j), carry)[1], 0)

    @pl.when(last)
    def _():
        lax.fori_loop(0, layers, share_all_h, 0)

    def gy(p, k, t, cc):
        to_y = (y + k) % 4
        return send(
            gs.at[p, to_y, t, cc], gr.at[p, quarter, k], g_s.at[p, k, 2 * t + cc], g_r.at[p, quarter, k],
            at(2 * xh + t, to_y, z, cc),
        )

    def for_sums(p, act):
        for k in (2, 1, 3, 0):
            for t in range(2):
                for cc in range(2):
                    if k == 0:

                        @pl.when(2 * t + cc != quarter)
                        def _(k=k, t=t, cc=cc):
                            act(p, k, t, cc)

                    else:
                        act(p, k, t, cc)

    def sum_wait(p, k, q):
        return send(gr.at[p, q, k], gr.at[p, q, k], g_s.at[p, k, q], g_r.at[p, q, k], sibling)

    def collect(p):
        l = 2 * p + xh
        acc[...] = jnp.zeros_like(acc)

        def all_h(j, carry):
            hx[p, j, me8] = hs[l, mb_rows(j), :]
            dx[p, j, me8] = ds[l, quarter, mb_rows(j), :]
            for ax in range(4):
                block = hx.at[p, j, 2 * ax + other]
                send(block, block, h_s.at[0, 0], h_r.at[p, j, 2 * ax + other], sibling).wait_recv()
            return carry

        def one(j, carry):
            for src in range(8):

                @pl.when(src != me8)
                def _(src=src):
                    block = dx.at[p, j, src]
                    send(block, block, u_s.at[0, 0], u_r.at[p, j, src], sibling).wait_recv()

            acc[...] += lax.dot_general(
                hx[p, j].reshape(8 * MB_ROWS, D),
                dx[p, j].reshape(8 * MB_ROWS, WIDE),
                (((0,), (0,)), ((), ())),
                preferred_element_type=jnp.float32,
            )
            return carry

        lax.fori_loop(0, slots, all_h, 0)
        lax.fori_loop(0, slots, one, 0)
        gs[p] = acc[...].astype(jnp.bfloat16).reshape(4, 2, 2, 64, WIDE)
        for_sums(p, lambda p, k, t, cc: gy(p, k, t, cc).start())
        gr[p, quarter, 0] = gs[p, y, xl, c]

    def add_up(p, out):
        for q in range(4):
            for k in K:
                sum_wait(p, k, q).wait_recv()

            @pl.when(q != quarter)
            def _(q=q):
                sum_wait(p, 0, q).wait_recv()

            out[:, q * WIDE : (q + 1) * WIDE] = f32(gr[p, q, 0]) + f32(gr[p, q, 1]) + f32(gr[p, q, 2]) + f32(gr[p, q, 3])

    def zr():
        return send(zsend, zres, zr_s, zr_r, zpartner)

    if FIRST_PAIR < 8:

        @pl.when(pair)
        def _():
            hand_over(1 - own_p)
            hand_over(own_p)
            collect(1 - own_p)

    collect(own_p)
    if FIRST_PAIR < 8:

        @pl.when(pair)
        def _():
            add_up(1 - own_p, zsend)
            zr().start()

    if FIRST_PAIR < 8:

        @pl.when(pair)
        def _():
            zx().wait_send()

    @pl.when(last)
    def _():
        lax.fori_loop(0, planes, drain_gather, 0)

    def drain_relay(j, carry):
        @pl.when(jnp.logical_not(last))
        def _():
            fx(j).wait_send()

        @pl.when(jnp.logical_not(first))
        def _():
            bx(j).wait_send()

        return carry

    lax.fori_loop(0, slots, drain_relay, 0)

    def drain_layers(l, carry):
        def drain_rows(j, carry):
            for t in range(2):
                share_h(l, j, t).wait_send()
            for_owners(l, lambda t, cc: share_u(l, j, t, cc).wait_send())
            return carry

        return lax.fori_loop(0, slots, drain_rows, carry)

    lax.fori_loop(0, layers, drain_layers, 0)

    def drain_hand(p, carry):
        def one(j, carry):
            for k in K:
                hand_h(p, j, k).wait_send()
            return carry

        return lax.fori_loop(0, slots, one, carry)

    lax.fori_loop(0, planes, drain_hand, 0)

    def drain_sums(p, carry):
        for_sums(p, lambda p, k, t, cc: gy(p, k, t, cc).wait_send())
        return carry

    add_up(own_p, gw_out.at[0])
    if FIRST_PAIR < 8:

        @pl.when(pair)
        def _():
            zr().wait_recv()
            gw_out[0] = gw_out[0] + zres[...]
            zr().wait_send()

    full = gw_out[0]
    per_row = jnp.sum(full * wv[...].astype(jnp.float32), axis=1, keepdims=True)
    gg_out[...] = jnp.sum(jnp.where(eye, per_row, 0.0), axis=0, keepdims=True)
    gw_out[0] = full * gain_col

    lax.fori_loop(0, planes, drain_sums, 0)


def shards(down_input, up_input, down_cot, up_cot, weight, gain):
    nl = 2 if FIRST_PAIR == 8 else 4
    np_ = nl // 2
    bf, f4 = jnp.bfloat16, jnp.float32
    dma = pltpu.SemaphoreType.DMA
    scratch = [
        pltpu.VMEM((64, D), bf),
        pltpu.VMEM((nl, 4, 2, 2, 64, D), bf),
        pltpu.VMEM((nl, D, D), bf),
        pltpu.VMEM((nl, 4 * MB_ROWS, D), bf),
        pltpu.VMEM((nl, 4, 4 * MB_ROWS, D // 4), bf),
        pltpu.VMEM((np_, 4, 8, MB_ROWS, D), bf),
        pltpu.VMEM((np_, 4, 8, MB_ROWS, D // 4), bf),
        pltpu.VMEM((D, D // 4), f4),
        pltpu.VMEM((np_, 4, 2, 2, 64, D // 4), bf),
        pltpu.VMEM((np_, 4, 4, 64, D // 4), bf),
        pltpu.VMEM((64, D), f4),
        pltpu.VMEM((64, D), f4),
        pltpu.VMEM((nl + 1, 4, MB_ROWS, D), bf),
        pltpu.VMEM((nl, 4, MB_ROWS, D), f4),
        pltpu.VMEM((nl, 4, MB_ROWS, 128), f4),
        pltpu.VMEM((4, MB_ROWS, D), bf),
        pltpu.VMEM((4, MB_ROWS, D), bf),
        dma, dma,
        dma((np_, 3)), dma((np_, 3)), dma((np_, 3)), dma((np_, 3)),
        dma((np_, 4, 2)), dma((np_, 4, 2)), dma((np_, 4, 2)), dma((np_, 4, 2)),
        dma((np_, 4, 2)), dma((np_, 4, 2)), dma((np_, 4, 2)), dma((np_, 4, 2)),
        dma((np_, 39)), dma((np_,)),
        dma((4,)), dma((4,)), dma((4,)), dma((4,)),
        dma((8, 2)), dma((np_, 4, 8)), dma((np_, 4, 3)), dma((8, 4)), dma((np_, 4, 8)),
        dma((np_, 4, 4)), dma((np_, 4, 4)),
        dma, dma,
        pltpu.SemaphoreType.REGULAR((2,)),
        dma, dma((4,)),
    ]
    vmem = pl.BlockSpec(memory_space=pltpu.VMEM)
    return pl.pallas_call(
        kernel,
        out_shape=(
            jax.ShapeDtypeStruct((1, 64, D), f4),
            jax.ShapeDtypeStruct((1, 64), f4),
        ),
        in_specs=[pl.BlockSpec(memory_space=pl.ANY)] * 5 + [vmem],
        out_specs=(vmem, vmem),
        scratch_shapes=scratch,
        compiler_params=pltpu.CompilerParams(
            collective_id=0, has_side_effects=True, vmem_limit_bytes=56 * 1024 * 1024
        ),
    )(down_input, up_input, down_cot, up_cot, weight, gain)


def solution(mesh):
    rows = P(None, "dp", None)
    return jax.shard_map(
        shards,
        mesh=mesh,
        in_specs=(rows, rows, rows, rows, P("section", "dp", None), P("section", "dp")),
        out_specs=(P("section", "dp", None), P("section", "dp")),
        check_vma=False,
    )
```

```python
import functools
import math

import jax
import jax.numpy as jnp
from jax import lax
from jax.experimental import pallas as pl
from jax.experimental.pallas import tpu as pltpu
from jax.sharding import PartitionSpec as P

EPSILON = 1e-05
CUBIC = 0.044715
SLOPE = math.sqrt(2.0 / math.pi)
MESH = pl.DeviceIdType.MESH
FIRST_PAIR = 2
D = 1024
HALF = D // 2
MB_ROWS = 32


def kernel(
    down_in, up_in, down_cot, up_cot, w_in, g_in, gw_out, gg_out,
    wv, w, wt, hs, ds, hx, dx, acc, gs, gr, zres, zsend, xs, sl, rinv, do, cot,
    zx_s, zx_r, a1_s, a1_r, b1_s, b1_r, a2_s, a2_r, b2_s, b2_r, a3_s, a3_r, b3_s, b3_r, d_s, d_r,
    fx_s, fx_r, bx_s, bx_r, h_s, h_r, hf_s, u_s, u_r, g_s, g_r, zr_s, zr_r, above, w_sem, in_sem,
):
    sec, dp = lax.axis_index("section"), lax.axis_index("dp")
    z, xh = sec // 2, sec % 2
    y, xl, c = dp // 4, (dp // 2) % 2, dp % 2
    x = xh * 2 + xl
    other = 1 - c

    def at(ax, ay, az, ac):
        return (az * 2 + ax // 2, ay * 4 + (ax % 2) * 2 + ac)

    def xdev(k):
        return at((x + k) % 4, y, z, c)

    def ydev(k):
        return at(x, (y + k) % 4, z, c)

    def zdev(k):
        return at(x, y, (z + 8 + k) % 8, other)

    sibling = at(x, y, z, other)
    pair = z >= FIRST_PAIR
    single = z < FIRST_PAIR
    ispair = pair.astype(jnp.int32) if FIRST_PAIR < 8 else 0
    odd = (z % 2) * ispair
    planes = 1 + ispair
    layers = 2 * planes
    slots = 4 // planes
    own_p = odd
    own_l = 2 * own_p + xh
    zpartner = at(x, y, z + 1 - 2 * (z % 2), c)

    load_w = pltpu.make_async_copy(w_in.at[0], wv, w_sem)
    load_w.start()
    barrier = pltpu.get_barrier_semaphore()
    peers = [sibling] + [xdev(k) for k in (1, 2, 3)] + [ydev(k) for k in (1, 2, 3)]
    peers += [at((x + k) % 4, y, z, other) for k in (1, 2, 3)]
    peers += [at(x, (y + k) % 4, z, other) for k in (1, 2, 3)]
    beside = x + 1 - 2 * xl
    peers += [at(beside, (y + k) % 4, z, ac) for k in (1, 2, 3) for ac in (0, 1)]
    for peer in peers:
        pl.semaphore_signal(barrier, inc=1, device_id=peer, device_id_type=MESH)
    for k in (1, 2):

        @pl.when(z + k < 8)
        def _(k=k):
            pl.semaphore_signal(barrier, inc=1, device_id=zdev(k), device_id_type=MESH)

    if FIRST_PAIR < 8:

        @pl.when(pair)
        def _():
            pl.semaphore_signal(barrier, inc=1, device_id=zpartner, device_id_type=MESH)

    def wait_above():
        for k in (1, 2):

            @pl.when(z + k < 8)
            def _(k=k):
                pl.semaphore_wait(above.at[k - 1], 1)

    def send(src, dst, ss, rs, to):
        return pltpu.make_async_remote_copy(
            src_ref=src, dst_ref=dst, send_sem=ss, recv_sem=rs, device_id=to, device_id_type=MESH
        )

    eye = lax.broadcasted_iota(jnp.int32, (64, 64), 0) == lax.broadcasted_iota(jnp.int32, (64, 64), 1)
    gain_col = jnp.sum(jnp.where(eye, g_in[...].astype(jnp.float32), 0.0), axis=1, keepdims=True)
    load_w.wait()
    w[own_l, y, xl, c] = (wv[...].astype(jnp.float32) * gain_col).astype(jnp.bfloat16)
    pl.semaphore_wait(barrier, len(peers) + jnp.minimum(z, 2) + ispair)
    for k in (1, 2):

        @pl.when(z >= k)
        def _(k=k):
            pl.semaphore_signal(above.at[k - 1], inc=1, device_id=zdev(-k), device_id_type=MESH)


    A, B, ALL = pl.ds(0, HALF), pl.ds(HALF, HALF), pl.ds(0, D)

    def blk(p, bx, by, cols):
        return w.at[2 * p + bx // 2, by, bx % 2, c, :, cols]

    def zx():
        ref = w.at[own_l, y, xl, c]
        return send(ref, ref, zx_s, zx_r, zpartner)

    def zx_other():
        ref = w.at[2 * (1 - own_p) + xh, y, xl, c]
        return send(ref, ref, zx_s, zx_r, zpartner)

    def a1(p, k):
        ref = blk(p, x, y, A)
        return send(ref, ref, a1_s.at[p, k - 1], a1_r.at[p, k - 1], xdev(k))

    def b1(p, k):
        ref = blk(p, x, y, B)
        return send(ref, ref, b1_s.at[p, k - 1], b1_r.at[p, k - 1], ydev(k))

    def a2(p, src, k):
        ref = blk(p, (x - src + 4) % 4, y, A)
        return send(ref, ref, a2_s.at[p, src, k // 2], a2_r.at[p, src, k // 2], ydev(k))

    def b2(p, src, k):
        ref = blk(p, x, (y - src + 4) % 4, B)
        return send(ref, ref, b2_s.at[p, src, k // 2], b2_r.at[p, src, k // 2], xdev(k))

    def half_blk(p, bx, by, cols, k):
        return w.at[2 * p + bx // 2, by, bx % 2, c, pl.ds(32 * (k // 2), 32), cols]

    def a3(p, src, k):
        ref = half_blk(p, (x - src + 4) % 4, (y - k + 4) % 4, A, k)
        return send(ref, ref, a3_s.at[p, src, k // 2], a3_r.at[p, src, k // 2], ydev(k))

    def b3(p, src, k):
        ref = half_blk(p, (x - k + 4) % 4, (y - src + 4) % 4, B, k)
        return send(ref, ref, b3_s.at[p, src, k // 2], b3_r.at[p, src, k // 2], xdev(k))

    def a3_wait(p, src, k):
        ref = half_blk(p, (x - src + 4) % 4, (y + 2) % 4, A, k)
        return send(ref, ref, a3_s.at[p, src, k // 2], a3_r.at[p, src, k // 2], sibling)

    def b3_wait(p, src, k):
        ref = half_blk(p, (x + 2) % 4, (y - src + 4) % 4, B, k)
        return send(ref, ref, b3_s.at[p, src, k // 2], b3_r.at[p, src, k // 2], sibling)

    def d_a2(p, src, k):
        ref = blk(p, (x - src + 4) % 4, (y - k + 4) % 4, A)
        return send(ref, ref, d_s.at[p, 7 + 2 * src + k // 2], d_r.at[p], sibling)

    def d_b2(p, src, k):
        ref = blk(p, (x - k + 4) % 4, (y - src + 4) % 4, B)
        return send(ref, ref, d_s.at[p, 15 + 2 * src + k // 2], d_r.at[p], sibling)

    def d_a3(p, src, k):
        ref = half_blk(p, (x - src + 4) % 4, (y + 2) % 4, A, k)
        return send(ref, ref, d_s.at[p, 23 + 2 * src + k // 2], d_r.at[p], sibling)

    def d_b3(p, src, k):
        ref = half_blk(p, (x + 2) % 4, (y - src + 4) % 4, B, k)
        return send(ref, ref, d_s.at[p, 31 + 2 * src + k // 2], d_r.at[p], sibling)

    def a2_wait(p, src, k):
        ref = blk(p, (x - src + 4) % 4, (y - k + 4) % 4, A)
        return send(ref, ref, a2_s.at[p, src, k // 2], a2_r.at[p, src, k // 2], sibling)

    def b2_wait(p, src, k):
        ref = blk(p, (x - k + 4) % 4, (y - src + 4) % 4, B)
        return send(ref, ref, b2_s.at[p, src, k // 2], b2_r.at[p, src, k // 2], sibling)

    def d_own(p):
        ref = blk(p, x, y, ALL)
        return send(ref, ref, d_s.at[p, 0], d_r.at[p], sibling)

    def d_a1(p, k):
        ref = blk(p, (x - k + 4) % 4, y, A)
        return send(ref, ref, d_s.at[p, k], d_r.at[p], sibling)

    def d_b1(p, k):
        ref = blk(p, x, (y - k + 4) % 4, B)
        return send(ref, ref, d_s.at[p, 3 + k], d_r.at[p], sibling)

    def d_wait(p):
        ref = w.at[pl.ds(2 * p, 2), :, :, other]
        return send(ref, ref, d_s.at[p, 0], d_r.at[p], sibling)

    K, N = (1, 2, 3), (1, 3)
    if FIRST_PAIR < 8:

        @pl.when(pair)
        def _():
            zx().start()

    def gather_start(i, carry):
        p = (own_p + i) % planes

        @pl.when(i > 0)
        def _():
            zx_other().wait_recv()

        d_own(p).start()
        for k in (1, 3):
            a1(p, k).start()
            b1(p, k).start()
        a1(p, 2).start()
        b1(p, 2).start()
        for k in N:
            a2(p, 0, k).start()
            b2(p, 0, k).start()
        return carry

    def onward(p, src):
        a1(p, src).wait_recv()
        for k in N:
            a2(p, src, k).start()
        d_a1(p, src).start()
        b1(p, src).wait_recv()
        for k in N:
            b2(p, src, k).start()
        d_b1(p, src).start()

    def arrived(p, src):
        for k in N:
            a2_wait(p, src, k).wait_recv()
            a3(p, src, k).start()
            d_a2(p, src, k).start()
            b2_wait(p, src, k).wait_recv()
            b3(p, src, k).start()
            d_b2(p, src, k).start()

    def far_side(p, src):
        for k in N:
            a3_wait(p, src, k).wait_recv()
            d_a3(p, src, k).start()
            b3_wait(p, src, k).wait_recv()
            d_b3(p, src, k).start()

    def gather_mid(i, carry):
        p = (own_p + i) % planes
        for src in (1, 3, 2):
            onward(p, src)
        arrived(p, 0)
        return carry

    def gather_end(i, carry):
        p = (own_p + i) % planes
        arrived(p, 1)
        arrived(p, 3)
        far_side(p, 0)
        arrived(p, 2)
        far_side(p, 1)
        far_side(p, 3)
        far_side(p, 2)
        return carry

    def gather_wait(i, carry):
        d_wait((own_p + i) % planes).wait_recv()
        return carry

    lax.fori_loop(0, planes, gather_start, 0)

    first = z < (2 if FIRST_PAIR == 0 else 1)
    last = z >= (7 if FIRST_PAIR == 8 else 6)

    def rows_in(ref, dst, slot, j):
        rows = pl.ds(pl.multiple_of((j % 2) * MB_ROWS, MB_ROWS), MB_ROWS)
        return pltpu.make_async_copy(ref.at[j // 2, rows, :], dst.at[slot], in_sem.at[slot])

    def load_rows(dst, down, up):
        def one(slot, carry):
            j = slot * planes + odd
            for ref, cond in ((down, xh == 0), (up, xh == 1)):

                @pl.when(cond)
                def _(ref=ref):
                    rows_in(ref, dst, slot, j).start()

            return carry

        lax.fori_loop(0, slots, one, 0)

    @pl.when(first)
    def _():
        load_rows(xs.at[0], down_in, up_in)

    @pl.when(last)
    def _():
        load_rows(cot, down_cot, up_cot)

    lax.fori_loop(0, planes, gather_mid, 0)
    lax.fori_loop(0, planes, gather_end, 0)
    lax.fori_loop(0, planes, gather_wait, 0)

    if FIRST_PAIR == 8:

        def f_route(j):
            return zdev(1), j

        def b_route(j):
            return zdev(-1), j

    else:
        to_pair = (z == FIRST_PAIR - 1).astype(jnp.int32)
        from_pair = ((z // 2) * 2 == FIRST_PAIR).astype(jnp.int32)

        def f_route(j):
            step = ispair * 2 + (1 - ispair) * (1 + to_pair * (j % 2))
            slot = j - to_pair * (j - j // 2)
            return zdev(step), slot

        def b_route(j):
            step = ispair * (2 + from_pair * (odd - 1)) + (1 - ispair)
            slot = j + from_pair * (j + odd)
            return zdev(-step), slot

    def fx(j):
        to, slot = f_route(j)
        return send(xs.at[layers, j], xs.at[0, slot], fx_s.at[j], fx_r.at[slot], to)

    def fx_wait(j):
        return send(xs.at[layers, j], xs.at[0, j], fx_s.at[j], fx_r.at[j], sibling)

    def bx(j):
        to, slot = b_route(j)
        return send(do.at[j], cot.at[slot], bx_s.at[j], bx_r.at[slot], to)

    def bx_wait(j):
        return send(do.at[j], cot.at[j], bx_s.at[j], bx_r.at[j], sibling)

    me8 = x * 2 + c

    quarter = 2 * xl + c
    WIDE = D // 4

    def mb_rows(j):
        return pl.ds(pl.multiple_of(j * MB_ROWS, MB_ROWS), MB_ROWS)

    def share_h(l, j, t):
        to_x = 2 * (l % 2) + t
        near = (to_x == x).astype(jnp.int32)
        core = c + near * (1 - 2 * c)
        return send(
            hs.at[l, mb_rows(j), :], hx.at[l // 2, j, me8], h_s.at[l * slots + j, t], h_r.at[l // 2, j, me8],
            at(to_x, y, z, core),
        )

    def hand_h(p, j, k):
        src = ((x + k) % 4) * 2 + c
        ref = hx.at[p, j, src]
        return send(ref, ref, hf_s.at[p, j, k - 1], h_r.at[p, j, src], sibling)

    def hand_over(p):
        def one(j, carry):
            for k in K:
                hand_h(p, j, k).wait_recv()
                hand_h(p, j, k).start()
            return carry

        lax.fori_loop(0, slots, one, 0)

    def share_u(l, j, t, cc):
        return send(
            ds.at[l, 2 * t + cc, mb_rows(j), :], dx.at[l // 2, j, me8], u_s.at[l * slots + j, 2 * t + cc],
            u_r.at[l // 2, j, me8], at(2 * (l % 2) + t, y, z, cc),
        )

    def for_owners(l, act):
        for t in range(2):
            for cc in range(2):

                @pl.when(jnp.logical_or(2 * (l % 2) + t != x, cc != c))
                def _(t=t, cc=cc):
                    act(t, cc)

    def f32(v):
        return v.astype(jnp.float32)

    def forward_layers(j, count):
        rows = pl.ds(pl.multiple_of(j * MB_ROWS, MB_ROWS), MB_ROWS)
        xf = f32(xs[0, j])
        for l in range(count):
            r = lax.rsqrt(jnp.mean(xf * xf, axis=-1, keepdims=True) + EPSILON)
            normed = (xf * r).astype(jnp.bfloat16)
            u = jnp.dot(normed, w[l].reshape(D, D), preferred_element_type=jnp.float32)
            t = jnp.tanh(SLOPE * (u + CUBIC * (u * u) * u))
            nxt = (xf + 0.5 * u * (1.0 + t)).astype(jnp.bfloat16)
            xs[l + 1, j] = nxt
            xf = f32(nxt)
            sl[l, j] = u
            rinv[l, j] = jnp.broadcast_to(r, (MB_ROWS, 128))
            hs[l, rows, :] = normed

    def forward(j, carry):
        @pl.when(first)
        def _():
            rows_in(down_in, xs.at[0], j, 0).wait()

        @pl.when(jnp.logical_not(first))
        def _():
            fx_wait(j).wait_recv()

        if FIRST_PAIR > 0:

            @pl.when(single)
            def _():
                forward_layers(j, 2)

        if FIRST_PAIR < 8:

            @pl.when(pair)
            def _():
                forward_layers(j, 4)

        @pl.when(jnp.logical_not(last))
        def _():
            fx(j).start()

        return carry

    def slope(u):
        u2 = u * u
        t = jnp.tanh(SLOPE * (u + CUBIC * u2 * u))
        return 0.5 * (1.0 + t) + 0.5 * u * (1.0 - t * t) * SLOPE * (1.0 + 3.0 * CUBIC * u2)

    def slopes(l, carry):
        def one(j, carry):
            sl[l, j] = slope(sl[l, j])
            return carry

        return lax.fori_loop(0, slots, one, carry)

    def turn(l, carry):
        wt[l] = w[l].reshape(D, D).T
        return carry

    def share_all_h(l, carry):
        def one(j, carry):
            for t in range(2):
                share_h(l, j, t).start()
            return carry

        return lax.fori_loop(0, slots, one, carry)

    def drain_gather(i, carry):
        p = (own_p + i) % planes
        for k in K:
            a1(p, k).wait_send()
            b1(p, k).wait_send()
            d_a1(p, k).wait_send()
            d_b1(p, k).wait_send()
        for src in range(4):
            for k in N:
                for copy in (a2, b2, a3, b3, d_a2, d_b2, d_a3, d_b3):
                    copy(p, src, k).wait_send()
        d_own(p).wait_send()
        return carry

    @pl.when(last)
    def _():
        lax.fori_loop(0, layers, turn, 0)

    wait_above()
    lax.fori_loop(0, slots, forward, 0)

    @pl.when(jnp.logical_not(last))
    def _():
        lax.fori_loop(0, layers, share_all_h, 0)
        lax.fori_loop(0, layers, turn, 0)

    @pl.when(jnp.logical_not(last))
    def _():
        lax.fori_loop(0, layers, slopes, 0)
        lax.fori_loop(0, planes, drain_gather, 0)

    if FIRST_PAIR > 0:

        @pl.when(single)
        def _():
            hand_over(0)

    def backward_layers(j, top, bottom, fresh=False):
        rows = pl.ds(pl.multiple_of(j * MB_ROWS, MB_ROWS), MB_ROWS)
        delta = cot[j]
        for l in range(top, bottom - 1, -1):
            df = f32(delta)
            grad = (df * (slope(sl[l, j]) if fresh else sl[l, j])).astype(jnp.bfloat16)
            for q in range(4):
                ds[l, q, rows, :] = grad[:, q * WIDE : (q + 1) * WIDE]
            a = jnp.dot(grad, wt[l], preferred_element_type=jnp.float32)
            r = rinv[l, j][:, 0:1]
            xr = f32(xs[l, j]) * r
            delta = (df + r * (a - xr * jnp.mean(a * xr, axis=-1, keepdims=True))).astype(jnp.bfloat16)
        return delta

    def backward(j, carry):
        @pl.when(last)
        def _():
            rows_in(down_cot, cot, j, 0).wait()

        @pl.when(jnp.logical_not(last))
        def _():
            bx_wait(j).wait_recv()

        if FIRST_PAIR < 8:

            @pl.when(last)
            def _():
                do[j] = backward_layers(j, 3, 0, fresh=True)

            @pl.when(jnp.logical_and(pair, jnp.logical_not(jnp.logical_or(first, last))))
            def _():
                do[j] = backward_layers(j, 3, 0)

            @pl.when(pair)
            def _():
                bx(j).start()

        if FIRST_PAIR > 0:

            @pl.when(jnp.logical_and(single, jnp.logical_not(first)))
            def _():
                do[j] = backward_layers(j, 1, 0)
                bx(j).start()

        @pl.when(first)
        def _():
            rows = pl.ds(pl.multiple_of(j * MB_ROWS, MB_ROWS), MB_ROWS)
            delta = backward_layers(j, 1 if FIRST_PAIR > 0 else 3, 1)
            grad = (f32(delta) * sl[0, j]).astype(jnp.bfloat16)
            for q in range(4):
                ds[0, q, rows, :] = grad[:, q * WIDE : (q + 1) * WIDE]

        @pl.when(first)
        def _():
            share_all_u(j)

        return carry

    def share_all_u(j):
        def one(l, carry):
            for_owners(l, lambda t, cc: share_u(l, j, t, cc).start())
            return carry

        lax.fori_loop(0, layers, one, 0)

    lax.fori_loop(0, slots, backward, 0)

    @pl.when(jnp.logical_not(first))
    def _():
        lax.fori_loop(0, slots, lambda j, carry: (share_all_u(j), carry)[1], 0)

    @pl.when(last)
    def _():
        lax.fori_loop(0, layers, share_all_h, 0)

    def gy(p, k, t, cc):
        to_y = (y + k) % 4
        return send(
            gs.at[p, to_y, t, cc], gr.at[p, quarter, k], g_s.at[p, k, 2 * t + cc], g_r.at[p, quarter, k],
            at(2 * xh + t, to_y, z, cc),
        )

    def for_sums(p, act):
        for k in (2, 1, 3, 0):
            for t in range(2):
                for cc in range(2):
                    if k == 0:

                        @pl.when(2 * t + cc != quarter)
                        def _(k=k, t=t, cc=cc):
                            act(p, k, t, cc)

                    else:
                        act(p, k, t, cc)

    def sum_wait(p, k, q):
        return send(gr.at[p, q, k], gr.at[p, q, k], g_s.at[p, k, q], g_r.at[p, q, k], sibling)

    def collect(p):
        l = 2 * p + xh
        acc[...] = jnp.zeros_like(acc)

        def all_h(j, carry):
            hx[p, j, me8] = hs[l, mb_rows(j), :]
            dx[p, j, me8] = ds[l, quarter, mb_rows(j), :]
            for ax in range(4):
                block = hx.at[p, j, 2 * ax + other]
                send(block, block, h_s.at[0, 0], h_r.at[p, j, 2 * ax + other], sibling).wait_recv()
            return carry

        def one(j, carry):
            for src in range(8):

                @pl.when(src != me8)
                def _(src=src):
                    block = dx.at[p, j, src]
                    send(block, block, u_s.at[0, 0], u_r.at[p, j, src], sibling).wait_recv()

            acc[...] += lax.dot_general(
                hx[p, j].reshape(8 * MB_ROWS, D),
                dx[p, j].reshape(8 * MB_ROWS, WIDE),
                (((0,), (0,)), ((), ())),
                preferred_element_type=jnp.float32,
            )
            return carry

        lax.fori_loop(0, slots, all_h, 0)
        lax.fori_loop(0, slots, one, 0)
        gs[p] = acc[...].astype(jnp.bfloat16).reshape(4, 2, 2, 64, WIDE)
        for_sums(p, lambda p, k, t, cc: gy(p, k, t, cc).start())
        gr[p, quarter, 0] = gs[p, y, xl, c]

    def add_up(p, out):
        for q in range(4):
            for k in K:
                sum_wait(p, k, q).wait_recv()

            @pl.when(q != quarter)
            def _(q=q):
                sum_wait(p, 0, q).wait_recv()

            out[:, q * WIDE : (q + 1) * WIDE] = f32(gr[p, q, 0]) + f32(gr[p, q, 1]) + f32(gr[p, q, 2]) + f32(gr[p, q, 3])

    def zr():
        return send(zsend, zres, zr_s, zr_r, zpartner)

    if FIRST_PAIR < 8:

        @pl.when(pair)
        def _():
            hand_over(1 - own_p)
            hand_over(own_p)
            collect(1 - own_p)

    collect(own_p)
    if FIRST_PAIR < 8:

        @pl.when(pair)
        def _():
            add_up(1 - own_p, zsend)
            zr().start()

    if FIRST_PAIR < 8:

        @pl.when(pair)
        def _():
            zx().wait_send()

    @pl.when(last)
    def _():
        lax.fori_loop(0, planes, drain_gather, 0)

    def drain_relay(j, carry):
        @pl.when(jnp.logical_not(last))
        def _():
            fx(j).wait_send()

        @pl.when(jnp.logical_not(first))
        def _():
            bx(j).wait_send()

        return carry

    lax.fori_loop(0, slots, drain_relay, 0)

    def drain_layers(l, carry):
        def drain_rows(j, carry):
            for t in range(2):
                share_h(l, j, t).wait_send()
            for_owners(l, lambda t, cc: share_u(l, j, t, cc).wait_send())
            return carry

        return lax.fori_loop(0, slots, drain_rows, carry)

    lax.fori_loop(0, layers, drain_layers, 0)

    def drain_hand(p, carry):
        def one(j, carry):
            for k in K:
                hand_h(p, j, k).wait_send()
            return carry

        return lax.fori_loop(0, slots, one, carry)

    lax.fori_loop(0, planes, drain_hand, 0)

    def drain_sums(p, carry):
        for_sums(p, lambda p, k, t, cc: gy(p, k, t, cc).wait_send())
        return carry

    add_up(own_p, gw_out.at[0])
    if FIRST_PAIR < 8:

        @pl.when(pair)
        def _():
            zr().wait_recv()
            gw_out[0] = gw_out[0] + zres[...]
            zr().wait_send()

    full = gw_out[0]
    per_row = jnp.sum(full * wv[...].astype(jnp.float32), axis=1, keepdims=True)
    gg_out[...] = jnp.sum(jnp.where(eye, per_row, 0.0), axis=0, keepdims=True)
    gw_out[0] = full * gain_col

    lax.fori_loop(0, planes, drain_sums, 0)


def shards(down_input, up_input, down_cot, up_cot, weight, gain):
    nl = 2 if FIRST_PAIR == 8 else 4
    np_ = nl // 2
    bf, f4 = jnp.bfloat16, jnp.float32
    dma = pltpu.SemaphoreType.DMA
    scratch = [
        pltpu.VMEM((64, D), bf),
        pltpu.VMEM((nl, 4, 2, 2, 64, D), bf),
        pltpu.VMEM((nl, D, D), bf),
        pltpu.VMEM((nl, 4 * MB_ROWS, D), bf),
        pltpu.VMEM((nl, 4, 4 * MB_ROWS, D // 4), bf),
        pltpu.VMEM((np_, 4, 8, MB_ROWS, D), bf),
        pltpu.VMEM((np_, 4, 8, MB_ROWS, D // 4), bf),
        pltpu.VMEM((D, D // 4), f4),
        pltpu.VMEM((np_, 4, 2, 2, 64, D // 4), bf),
        pltpu.VMEM((np_, 4, 4, 64, D // 4), bf),
        pltpu.VMEM((64, D), f4),
        pltpu.VMEM((64, D), f4),
        pltpu.VMEM((nl + 1, 4, MB_ROWS, D), bf),
        pltpu.VMEM((nl, 4, MB_ROWS, D), f4),
        pltpu.VMEM((nl, 4, MB_ROWS, 128), f4),
        pltpu.VMEM((4, MB_ROWS, D), bf),
        pltpu.VMEM((4, MB_ROWS, D), bf),
        dma, dma,
        dma((np_, 3)), dma((np_, 3)), dma((np_, 3)), dma((np_, 3)),
        dma((np_, 4, 2)), dma((np_, 4, 2)), dma((np_, 4, 2)), dma((np_, 4, 2)),
        dma((np_, 4, 2)), dma((np_, 4, 2)), dma((np_, 4, 2)), dma((np_, 4, 2)),
        dma((np_, 39)), dma((np_,)),
        dma((4,)), dma((4,)), dma((4,)), dma((4,)),
        dma((8, 2)), dma((np_, 4, 8)), dma((np_, 4, 3)), dma((8, 4)), dma((np_, 4, 8)),
        dma((np_, 4, 4)), dma((np_, 4, 4)),
        dma, dma,
        pltpu.SemaphoreType.REGULAR((2,)),
        dma, dma((4,)),
    ]
    vmem = pl.BlockSpec(memory_space=pltpu.VMEM)
    return pl.pallas_call(
        kernel,
        out_shape=(
            jax.ShapeDtypeStruct((1, 64, D), f4),
            jax.ShapeDtypeStruct((1, 64), f4),
        ),
        in_specs=[pl.BlockSpec(memory_space=pl.ANY)] * 5 + [vmem],
        out_specs=(vmem, vmem),
        scratch_shapes=scratch,
        compiler_params=pltpu.CompilerParams(
            collective_id=0, has_side_effects=True, vmem_limit_bytes=56 * 1024 * 1024
        ),
    )(down_input, up_input, down_cot, up_cot, weight, gain)


def solution(mesh):
    rows = P(None, "dp", None)
    return jax.shard_map(
        shards,
        mesh=mesh,
        in_specs=(rows, rows, rows, rows, P("section", "dp", None), P("section", "dp")),
        out_specs=(P("section", "dp", None), P("section", "dp")),
        check_vma=False,
    )
```

```python
import functools
import math

import jax
import jax.numpy as jnp
from jax import lax
from jax.experimental import pallas as pl
from jax.experimental.pallas import tpu as pltpu
from jax.sharding import PartitionSpec as P

EPSILON = 1e-05
CUBIC = 0.044715
SLOPE = math.sqrt(2.0 / math.pi)
MESH = pl.DeviceIdType.MESH
FIRST_PAIR = 2
D = 1024
HALF = D // 2
MB_ROWS = 32


def kernel(
    down_in, up_in, down_cot, up_cot, w_in, g_in, gw_out, gg_out,
    wv, w, wt, hs, ds, hx, dx, acc, gs, gr, zres, zsend, xs, sl, rinv, do, cot,
    zx_s, zx_r, a1_s, a1_r, b1_s, b1_r, a2_s, a2_r, b2_s, b2_r, a3_s, a3_r, b3_s, b3_r, d_s, d_r,
    fx_s, fx_r, bx_s, bx_r, h_s, h_r, hf_s, u_s, u_r, g_s, g_r, zr_s, zr_r, above, w_sem, in_sem,
):
    sec, dp = lax.axis_index("section"), lax.axis_index("dp")
    z, xh = sec // 2, sec % 2
    y, xl, c = dp // 4, (dp // 2) % 2, dp % 2
    x = xh * 2 + xl
    other = 1 - c

    def at(ax, ay, az, ac):
        return (az * 2 + ax // 2, ay * 4 + (ax % 2) * 2 + ac)

    def xdev(k):
        return at((x + k) % 4, y, z, c)

    def ydev(k):
        return at(x, (y + k) % 4, z, c)

    def zdev(k, core):
        return at(x, y, (z + 8 + k) % 8, core)

    sibling = at(x, y, z, other)
    pair = z >= FIRST_PAIR
    single = z < FIRST_PAIR
    ispair = pair.astype(jnp.int32) if FIRST_PAIR < 8 else 0
    odd = (z % 2) * ispair
    planes = 1 + ispair
    layers = 2 * planes
    slots = 4 // planes
    own_p = odd
    own_l = 2 * own_p + xh
    zpartner = at(x, y, z + 1 - 2 * (z % 2), c)

    load_w = pltpu.make_async_copy(w_in.at[0], wv, w_sem)
    load_w.start()
    barrier = pltpu.get_barrier_semaphore()
    peers = [sibling] + [xdev(k) for k in (1, 2, 3)] + [ydev(k) for k in (1, 2, 3)]
    peers += [at((x + k) % 4, y, z, other) for k in (1, 2, 3)]
    peers += [at(x, (y + k) % 4, z, other) for k in (1, 2, 3)]
    beside = x + 1 - 2 * xl
    peers += [at(beside, (y + k) % 4, z, ac) for k in (1, 2, 3) for ac in (0, 1)]
    for peer in peers:
        pl.semaphore_signal(barrier, inc=1, device_id=peer, device_id_type=MESH)
    for k in (1, 2):

        @pl.when(z + k < 8)
        def _(k=k):
            for core in (c, other):
                pl.semaphore_signal(barrier, inc=1, device_id=zdev(k, core), device_id_type=MESH)

    if FIRST_PAIR < 8:

        @pl.when(pair)
        def _():
            pl.semaphore_signal(barrier, inc=1, device_id=zpartner, device_id_type=MESH)

    def wait_above():
        for k in (1, 2):

            @pl.when(z + k < 8)
            def _(k=k):
                pl.semaphore_wait(above.at[k - 1], 2)

    def send(src, dst, ss, rs, to):
        return pltpu.make_async_remote_copy(
            src_ref=src, dst_ref=dst, send_sem=ss, recv_sem=rs, device_id=to, device_id_type=MESH
        )

    eye = lax.broadcasted_iota(jnp.int32, (64, 64), 0) == lax.broadcasted_iota(jnp.int32, (64, 64), 1)
    gain_col = jnp.sum(jnp.where(eye, g_in[...].astype(jnp.float32), 0.0), axis=1, keepdims=True)
    load_w.wait()
    w[own_l, y, xl, c] = (wv[...].astype(jnp.float32) * gain_col).astype(jnp.bfloat16)
    pl.semaphore_wait(barrier, len(peers) + 2 * jnp.minimum(z, 2) + ispair)
    for k in (1, 2):

        @pl.when(z >= k)
        def _(k=k):
            for core in (c, other):
                pl.semaphore_signal(above.at[k - 1], inc=1, device_id=zdev(-k, core), device_id_type=MESH)


    A, B, ALL = pl.ds(0, HALF), pl.ds(HALF, HALF), pl.ds(0, D)

    def blk(p, bx, by, cols):
        return w.at[2 * p + bx // 2, by, bx % 2, c, :, cols]

    def zx():
        ref = w.at[own_l, y, xl, c]
        return send(ref, ref, zx_s, zx_r, zpartner)

    def zx_other():
        ref = w.at[2 * (1 - own_p) + xh, y, xl, c]
        return send(ref, ref, zx_s, zx_r, zpartner)

    def a1(p, k):
        ref = blk(p, x, y, A)
        return send(ref, ref, a1_s.at[p, k - 1], a1_r.at[p, k - 1], xdev(k))

    def b1(p, k):
        ref = blk(p, x, y, B)
        return send(ref, ref, b1_s.at[p, k - 1], b1_r.at[p, k - 1], ydev(k))

    def a2(p, src, k):
        ref = blk(p, (x - src + 4) % 4, y, A)
        return send(ref, ref, a2_s.at[p, src, k // 2], a2_r.at[p, src, k // 2], ydev(k))

    def b2(p, src, k):
        ref = blk(p, x, (y - src + 4) % 4, B)
        return send(ref, ref, b2_s.at[p, src, k // 2], b2_r.at[p, src, k // 2], xdev(k))

    def half_blk(p, bx, by, cols, k):
        return w.at[2 * p + bx // 2, by, bx % 2, c, pl.ds(32 * (k // 2), 32), cols]

    def a3(p, src, k):
        ref = half_blk(p, (x - src + 4) % 4, (y - k + 4) % 4, A, k)
        return send(ref, ref, a3_s.at[p, src, k // 2], a3_r.at[p, src, k // 2], ydev(k))

    def b3(p, src, k):
        ref = half_blk(p, (x - k + 4) % 4, (y - src + 4) % 4, B, k)
        return send(ref, ref, b3_s.at[p, src, k // 2], b3_r.at[p, src, k // 2], xdev(k))

    def a3_wait(p, src, k):
        ref = half_blk(p, (x - src + 4) % 4, (y + 2) % 4, A, k)
        return send(ref, ref, a3_s.at[p, src, k // 2], a3_r.at[p, src, k // 2], sibling)

    def b3_wait(p, src, k):
        ref = half_blk(p, (x + 2) % 4, (y - src + 4) % 4, B, k)
        return send(ref, ref, b3_s.at[p, src, k // 2], b3_r.at[p, src, k // 2], sibling)

    def d_a2(p, src, k):
        ref = blk(p, (x - src + 4) % 4, (y - k + 4) % 4, A)
        return send(ref, ref, d_s.at[p, 7 + 2 * src + k // 2], d_r.at[p], sibling)

    def d_b2(p, src, k):
        ref = blk(p, (x - k + 4) % 4, (y - src + 4) % 4, B)
        return send(ref, ref, d_s.at[p, 15 + 2 * src + k // 2], d_r.at[p], sibling)

    def d_a3(p, src, k):
        ref = half_blk(p, (x - src + 4) % 4, (y + 2) % 4, A, k)
        return send(ref, ref, d_s.at[p, 23 + 2 * src + k // 2], d_r.at[p], sibling)

    def d_b3(p, src, k):
        ref = half_blk(p, (x + 2) % 4, (y - src + 4) % 4, B, k)
        return send(ref, ref, d_s.at[p, 31 + 2 * src + k // 2], d_r.at[p], sibling)

    def a2_wait(p, src, k):
        ref = blk(p, (x - src + 4) % 4, (y - k + 4) % 4, A)
        return send(ref, ref, a2_s.at[p, src, k // 2], a2_r.at[p, src, k // 2], sibling)

    def b2_wait(p, src, k):
        ref = blk(p, (x - k + 4) % 4, (y - src + 4) % 4, B)
        return send(ref, ref, b2_s.at[p, src, k // 2], b2_r.at[p, src, k // 2], sibling)

    def d_own(p):
        ref = blk(p, x, y, ALL)
        return send(ref, ref, d_s.at[p, 0], d_r.at[p], sibling)

    def d_a1(p, k):
        ref = blk(p, (x - k + 4) % 4, y, A)
        return send(ref, ref, d_s.at[p, k], d_r.at[p], sibling)

    def d_b1(p, k):
        ref = blk(p, x, (y - k + 4) % 4, B)
        return send(ref, ref, d_s.at[p, 3 + k], d_r.at[p], sibling)

    def d_wait(p):
        ref = w.at[pl.ds(2 * p, 2), :, :, other]
        return send(ref, ref, d_s.at[p, 0], d_r.at[p], sibling)

    K, N = (1, 2, 3), (1, 3)
    if FIRST_PAIR < 8:

        @pl.when(pair)
        def _():
            zx().start()

    def gather_start(i, carry):
        p = (own_p + i) % planes

        @pl.when(i > 0)
        def _():
            zx_other().wait_recv()

        d_own(p).start()
        for k in (1, 3):
            a1(p, k).start()
            b1(p, k).start()
        a1(p, 2).start()
        b1(p, 2).start()
        for k in N:
            a2(p, 0, k).start()
            b2(p, 0, k).start()
        return carry

    def onward(p, src):
        a1(p, src).wait_recv()
        for k in N:
            a2(p, src, k).start()
        d_a1(p, src).start()
        b1(p, src).wait_recv()
        for k in N:
            b2(p, src, k).start()
        d_b1(p, src).start()

    def arrived(p, src):
        for k in N:
            a2_wait(p, src, k).wait_recv()
            a3(p, src, k).start()
            d_a2(p, src, k).start()
            b2_wait(p, src, k).wait_recv()
            b3(p, src, k).start()
            d_b2(p, src, k).start()

    def far_side(p, src):
        for k in N:
            a3_wait(p, src, k).wait_recv()
            d_a3(p, src, k).start()
            b3_wait(p, src, k).wait_recv()
            d_b3(p, src, k).start()

    def gather_mid(i, carry):
        p = (own_p + i) % planes
        for src in (1, 3, 2):
            onward(p, src)
        arrived(p, 0)
        return carry

    def gather_end(i, carry):
        p = (own_p + i) % planes
        arrived(p, 1)
        arrived(p, 3)
        far_side(p, 0)
        arrived(p, 2)
        far_side(p, 1)
        far_side(p, 3)
        far_side(p, 2)
        return carry

    def gather_wait(i, carry):
        d_wait((own_p + i) % planes).wait_recv()
        return carry

    lax.fori_loop(0, planes, gather_start, 0)

    first = z < (2 if FIRST_PAIR == 0 else 1)
    last = z >= (7 if FIRST_PAIR == 8 else 6)

    def rows_in(ref, dst, slot, j):
        rows = pl.ds(pl.multiple_of((j % 2) * MB_ROWS, MB_ROWS), MB_ROWS)
        return pltpu.make_async_copy(ref.at[j // 2, rows, :], dst.at[slot], in_sem.at[slot])

    def load_rows(dst, down, up):
        def one(slot, carry):
            j = slot * planes + odd
            for ref, cond in ((down, xh == 0), (up, xh == 1)):

                @pl.when(cond)
                def _(ref=ref):
                    rows_in(ref, dst, slot, j).start()

            return carry

        lax.fori_loop(0, slots, one, 0)

    @pl.when(first)
    def _():
        load_rows(xs.at[0], down_in, up_in)

    @pl.when(last)
    def _():
        load_rows(cot, down_cot, up_cot)

    lax.fori_loop(0, planes, gather_mid, 0)
    lax.fori_loop(0, planes, gather_end, 0)
    lax.fori_loop(0, planes, gather_wait, 0)

    def changes(*planes_below):
        hit = sum((z == low).astype(jnp.int32) for low in planes_below)
        return c + hit * (1 - 2 * c)

    up_core = changes(0, 2, 3)
    down_core = changes(1, 4, 5)
    to_pair = (z == FIRST_PAIR - 1).astype(jnp.int32)
    from_pair = ((z // 2) * 2 == FIRST_PAIR).astype(jnp.int32)

    def f_route(j):
        step = ispair * 2 + (1 - ispair) * (1 + to_pair * (j % 2))
        slot = j - to_pair * (j - j // 2)
        return zdev(step, up_core), slot

    def b_route(j):
        step = ispair * (2 + from_pair * (odd - 1)) + (1 - ispair)
        slot = j + from_pair * (j + odd)
        return zdev(-step, down_core), slot

    def fx(j):
        to, slot = f_route(j)
        return send(xs.at[layers, j], xs.at[0, slot], fx_s.at[j], fx_r.at[slot], to)

    def fx_wait(j):
        return send(xs.at[layers, j], xs.at[0, j], fx_s.at[j], fx_r.at[j], sibling)

    def bx(j):
        to, slot = b_route(j)
        return send(do.at[j], cot.at[slot], bx_s.at[j], bx_r.at[slot], to)

    def bx_wait(j):
        return send(do.at[j], cot.at[j], bx_s.at[j], bx_r.at[j], sibling)

    me8 = x * 2 + c

    quarter = 2 * xl + c
    WIDE = D // 4

    def mb_rows(j):
        return pl.ds(pl.multiple_of(j * MB_ROWS, MB_ROWS), MB_ROWS)

    def share_h(l, j, t):
        to_x = 2 * (l % 2) + t
        near = (to_x == x).astype(jnp.int32)
        core = c + near * (1 - 2 * c)
        return send(
            hs.at[l, mb_rows(j), :], hx.at[l // 2, j, me8], h_s.at[l * slots + j, t], h_r.at[l // 2, j, me8],
            at(to_x, y, z, core),
        )

    def hand_h(p, j, k):
        src = ((x + k) % 4) * 2 + c
        ref = hx.at[p, j, src]
        return send(ref, ref, hf_s.at[p, j, k - 1], h_r.at[p, j, src], sibling)

    def hand_over(p):
        def one(j, carry):
            for k in K:
                hand_h(p, j, k).wait_recv()
                hand_h(p, j, k).start()
            return carry

        lax.fori_loop(0, slots, one, 0)

    def share_u(l, j, t, cc):
        return send(
            ds.at[l, 2 * t + cc, mb_rows(j), :], dx.at[l // 2, j, me8], u_s.at[l * slots + j, 2 * t + cc],
            u_r.at[l // 2, j, me8], at(2 * (l % 2) + t, y, z, cc),
        )

    def for_owners(l, act):
        for t in range(2):
            for cc in range(2):

                @pl.when(jnp.logical_or(2 * (l % 2) + t != x, cc != c))
                def _(t=t, cc=cc):
                    act(t, cc)

    def f32(v):
        return v.astype(jnp.float32)

    def forward_layers(j, count):
        rows = pl.ds(pl.multiple_of(j * MB_ROWS, MB_ROWS), MB_ROWS)
        xf = f32(xs[0, j])
        for l in range(count):
            r = lax.rsqrt(jnp.mean(xf * xf, axis=-1, keepdims=True) + EPSILON)
            normed = (xf * r).astype(jnp.bfloat16)
            u = jnp.dot(normed, w[l].reshape(D, D), preferred_element_type=jnp.float32)
            t = jnp.tanh(SLOPE * (u + CUBIC * (u * u) * u))
            nxt = (xf + 0.5 * u * (1.0 + t)).astype(jnp.bfloat16)
            xs[l + 1, j] = nxt
            xf = f32(nxt)
            sl[l, j] = u
            rinv[l, j] = jnp.broadcast_to(r, (MB_ROWS, 128))
            hs[l, rows, :] = normed

    def forward(j, carry):
        @pl.when(first)
        def _():
            rows_in(down_in, xs.at[0], j, 0).wait()

        @pl.when(jnp.logical_not(first))
        def _():
            fx_wait(j).wait_recv()

        if FIRST_PAIR > 0:

            @pl.when(single)
            def _():
                forward_layers(j, 2)

        if FIRST_PAIR < 8:

            @pl.when(pair)
            def _():
                forward_layers(j, 4)

        @pl.when(jnp.logical_not(last))
        def _():
            fx(j).start()

        return carry

    def slope(u):
        u2 = u * u
        t = jnp.tanh(SLOPE * (u + CUBIC * u2 * u))
        return 0.5 * (1.0 + t) + 0.5 * u * (1.0 - t * t) * SLOPE * (1.0 + 3.0 * CUBIC * u2)

    def slopes(l, carry):
        def one(j, carry):
            sl[l, j] = slope(sl[l, j])
            return carry

        return lax.fori_loop(0, slots, one, carry)

    def turn(l, carry):
        wt[l] = w[l].reshape(D, D).T
        return carry

    def share_all_h(l, carry):
        def one(j, carry):
            for t in range(2):
                share_h(l, j, t).start()
            return carry

        return lax.fori_loop(0, slots, one, carry)

    def drain_gather(i, carry):
        p = (own_p + i) % planes
        for k in K:
            a1(p, k).wait_send()
            b1(p, k).wait_send()
            d_a1(p, k).wait_send()
            d_b1(p, k).wait_send()
        for src in range(4):
            for k in N:
                for copy in (a2, b2, a3, b3, d_a2, d_b2, d_a3, d_b3):
                    copy(p, src, k).wait_send()
        d_own(p).wait_send()
        return carry

    @pl.when(last)
    def _():
        lax.fori_loop(0, layers, turn, 0)

    wait_above()
    lax.fori_loop(0, slots, forward, 0)

    @pl.when(jnp.logical_not(last))
    def _():
        lax.fori_loop(0, layers, share_all_h, 0)
        lax.fori_loop(0, layers, turn, 0)

    @pl.when(jnp.logical_not(last))
    def _():
        lax.fori_loop(0, layers, slopes, 0)
        lax.fori_loop(0, planes, drain_gather, 0)

    if FIRST_PAIR > 0:

        @pl.when(single)
        def _():
            hand_over(0)

    def backward_layers(j, top, bottom, fresh=False):
        rows = pl.ds(pl.multiple_of(j * MB_ROWS, MB_ROWS), MB_ROWS)
        delta = cot[j]
        for l in range(top, bottom - 1, -1):
            df = f32(delta)
            grad = (df * (slope(sl[l, j]) if fresh else sl[l, j])).astype(jnp.bfloat16)
            for q in range(4):
                ds[l, q, rows, :] = grad[:, q * WIDE : (q + 1) * WIDE]
            a = jnp.dot(grad, wt[l], preferred_element_type=jnp.float32)
            r = rinv[l, j][:, 0:1]
            xr = f32(xs[l, j]) * r
            delta = (df + r * (a - xr * jnp.mean(a * xr, axis=-1, keepdims=True))).astype(jnp.bfloat16)
        return delta

    def backward(j, carry):
        @pl.when(last)
        def _():
            rows_in(down_cot, cot, j, 0).wait()

        @pl.when(jnp.logical_not(last))
        def _():
            bx_wait(j).wait_recv()

        if FIRST_PAIR < 8:

            @pl.when(last)
            def _():
                do[j] = backward_layers(j, 3, 0, fresh=True)

            @pl.when(jnp.logical_and(pair, jnp.logical_not(jnp.logical_or(first, last))))
            def _():
                do[j] = backward_layers(j, 3, 0)

            @pl.when(pair)
            def _():
                bx(j).start()

        if FIRST_PAIR > 0:

            @pl.when(jnp.logical_and(single, jnp.logical_not(first)))
            def _():
                do[j] = backward_layers(j, 1, 0)
                bx(j).start()

        @pl.when(first)
        def _():
            rows = pl.ds(pl.multiple_of(j * MB_ROWS, MB_ROWS), MB_ROWS)
            delta = backward_layers(j, 1 if FIRST_PAIR > 0 else 3, 1)
            grad = (f32(delta) * sl[0, j]).astype(jnp.bfloat16)
            for q in range(4):
                ds[0, q, rows, :] = grad[:, q * WIDE : (q + 1) * WIDE]

        @pl.when(first)
        def _():
            share_all_u(j)

        return carry

    def share_all_u(j):
        def one(l, carry):
            for_owners(l, lambda t, cc: share_u(l, j, t, cc).start())
            return carry

        lax.fori_loop(0, layers, one, 0)

    lax.fori_loop(0, slots, backward, 0)

    @pl.when(jnp.logical_not(first))
    def _():
        lax.fori_loop(0, slots, lambda j, carry: (share_all_u(j), carry)[1], 0)

    @pl.when(last)
    def _():
        lax.fori_loop(0, layers, share_all_h, 0)

    def gy(p, k, t, cc):
        to_y = (y + k) % 4
        return send(
            gs.at[p, to_y, t, cc], gr.at[p, quarter, k], g_s.at[p, k, 2 * t + cc], g_r.at[p, quarter, k],
            at(2 * xh + t, to_y, z, cc),
        )

    def for_sums(p, act):
        for k in (2, 1, 3, 0):
            for t in range(2):
                for cc in range(2):
                    if k == 0:

                        @pl.when(2 * t + cc != quarter)
                        def _(k=k, t=t, cc=cc):
                            act(p, k, t, cc)

                    else:
                        act(p, k, t, cc)

    def sum_wait(p, k, q):
        return send(gr.at[p, q, k], gr.at[p, q, k], g_s.at[p, k, q], g_r.at[p, q, k], sibling)

    def collect(p):
        l = 2 * p + xh
        acc[...] = jnp.zeros_like(acc)

        def all_h(j, carry):
            hx[p, j, me8] = hs[l, mb_rows(j), :]
            dx[p, j, me8] = ds[l, quarter, mb_rows(j), :]
            for ax in range(4):
                block = hx.at[p, j, 2 * ax + other]
                send(block, block, h_s.at[0, 0], h_r.at[p, j, 2 * ax + other], sibling).wait_recv()
            return carry

        def one(j, carry):
            for src in range(8):

                @pl.when(src != me8)
                def _(src=src):
                    block = dx.at[p, j, src]
                    send(block, block, u_s.at[0, 0], u_r.at[p, j, src], sibling).wait_recv()

            acc[...] += lax.dot_general(
                hx[p, j].reshape(8 * MB_ROWS, D),
                dx[p, j].reshape(8 * MB_ROWS, WIDE),
                (((0,), (0,)), ((), ())),
                preferred_element_type=jnp.float32,
            )
            return carry

        lax.fori_loop(0, slots, all_h, 0)
        lax.fori_loop(0, slots, one, 0)
        gs[p] = acc[...].astype(jnp.bfloat16).reshape(4, 2, 2, 64, WIDE)
        for_sums(p, lambda p, k, t, cc: gy(p, k, t, cc).start())
        gr[p, quarter, 0] = gs[p, y, xl, c]

    def add_up(p, out):
        for q in range(4):
            for k in K:
                sum_wait(p, k, q).wait_recv()

            @pl.when(q != quarter)
            def _(q=q):
                sum_wait(p, 0, q).wait_recv()

            out[:, q * WIDE : (q + 1) * WIDE] = f32(gr[p, q, 0]) + f32(gr[p, q, 1]) + f32(gr[p, q, 2]) + f32(gr[p, q, 3])

    def zr():
        return send(zsend, zres, zr_s, zr_r, zpartner)

    if FIRST_PAIR < 8:

        @pl.when(pair)
        def _():
            hand_over(1 - own_p)
            hand_over(own_p)
            collect(1 - own_p)

    collect(own_p)
    if FIRST_PAIR < 8:

        @pl.when(pair)
        def _():
            add_up(1 - own_p, zsend)
            zr().start()

    if FIRST_PAIR < 8:

        @pl.when(pair)
        def _():
            zx().wait_send()

    @pl.when(last)
    def _():
        lax.fori_loop(0, planes, drain_gather, 0)

    def drain_relay(j, carry):
        @pl.when(jnp.logical_not(last))
        def _():
            fx(j).wait_send()

        @pl.when(jnp.logical_not(first))
        def _():
            bx(j).wait_send()

        return carry

    lax.fori_loop(0, slots, drain_relay, 0)

    def drain_layers(l, carry):
        def drain_rows(j, carry):
            for t in range(2):
                share_h(l, j, t).wait_send()
            for_owners(l, lambda t, cc: share_u(l, j, t, cc).wait_send())
            return carry

        return lax.fori_loop(0, slots, drain_rows, carry)

    lax.fori_loop(0, layers, drain_layers, 0)

    def drain_hand(p, carry):
        def one(j, carry):
            for k in K:
                hand_h(p, j, k).wait_send()
            return carry

        return lax.fori_loop(0, slots, one, carry)

    lax.fori_loop(0, planes, drain_hand, 0)

    def drain_sums(p, carry):
        for_sums(p, lambda p, k, t, cc: gy(p, k, t, cc).wait_send())
        return carry

    add_up(own_p, gw_out.at[0])
    if FIRST_PAIR < 8:

        @pl.when(pair)
        def _():
            zr().wait_recv()
            gw_out[0] = gw_out[0] + zres[...]
            zr().wait_send()

    full = gw_out[0]
    per_row = jnp.sum(full * wv[...].astype(jnp.float32), axis=1, keepdims=True)
    gg_out[...] = jnp.sum(jnp.where(eye, per_row, 0.0), axis=0, keepdims=True)
    gw_out[0] = full * gain_col

    lax.fori_loop(0, planes, drain_sums, 0)


def shards(down_input, up_input, down_cot, up_cot, weight, gain):
    nl = 2 if FIRST_PAIR == 8 else 4
    np_ = nl // 2
    bf, f4 = jnp.bfloat16, jnp.float32
    dma = pltpu.SemaphoreType.DMA
    scratch = [
        pltpu.VMEM((64, D), bf),
        pltpu.VMEM((nl, 4, 2, 2, 64, D), bf),
        pltpu.VMEM((nl, D, D), bf),
        pltpu.VMEM((nl, 4 * MB_ROWS, D), bf),
        pltpu.VMEM((nl, 4, 4 * MB_ROWS, D // 4), bf),
        pltpu.VMEM((np_, 4, 8, MB_ROWS, D), bf),
        pltpu.VMEM((np_, 4, 8, MB_ROWS, D // 4), bf),
        pltpu.VMEM((D, D // 4), f4),
        pltpu.VMEM((np_, 4, 2, 2, 64, D // 4), bf),
        pltpu.VMEM((np_, 4, 4, 64, D // 4), bf),
        pltpu.VMEM((64, D), f4),
        pltpu.VMEM((64, D), f4),
        pltpu.VMEM((nl + 1, 4, MB_ROWS, D), bf),
        pltpu.VMEM((nl, 4, MB_ROWS, D), f4),
        pltpu.VMEM((nl, 4, MB_ROWS, 128), f4),
        pltpu.VMEM((4, MB_ROWS, D), bf),
        pltpu.VMEM((4, MB_ROWS, D), bf),
        dma, dma,
        dma((np_, 3)), dma((np_, 3)), dma((np_, 3)), dma((np_, 3)),
        dma((np_, 4, 2)), dma((np_, 4, 2)), dma((np_, 4, 2)), dma((np_, 4, 2)),
        dma((np_, 4, 2)), dma((np_, 4, 2)), dma((np_, 4, 2)), dma((np_, 4, 2)),
        dma((np_, 39)), dma((np_,)),
        dma((4,)), dma((4,)), dma((4,)), dma((4,)),
        dma((8, 2)), dma((np_, 4, 8)), dma((np_, 4, 3)), dma((8, 4)), dma((np_, 4, 8)),
        dma((np_, 4, 4)), dma((np_, 4, 4)),
        dma, dma,
        pltpu.SemaphoreType.REGULAR((2,)),
        dma, dma((4,)),
    ]
    vmem = pl.BlockSpec(memory_space=pltpu.VMEM)
    return pl.pallas_call(
        kernel,
        out_shape=(
            jax.ShapeDtypeStruct((1, 64, D), f4),
            jax.ShapeDtypeStruct((1, 64), f4),
        ),
        in_specs=[pl.BlockSpec(memory_space=pl.ANY)] * 5 + [vmem],
        out_specs=(vmem, vmem),
        scratch_shapes=scratch,
        compiler_params=pltpu.CompilerParams(
            collective_id=0, has_side_effects=True, vmem_limit_bytes=56 * 1024 * 1024
        ),
    )(down_input, up_input, down_cot, up_cot, weight, gain)


def solution(mesh):
    rows = P(None, "dp", None)
    return jax.shard_map(
        shards,
        mesh=mesh,
        in_specs=(rows, rows, rows, rows, P("section", "dp", None), P("section", "dp")),
        out_specs=(P("section", "dp", None), P("section", "dp")),
        check_vma=False,
    )
```

```python
import functools
import math

import jax
import jax.numpy as jnp
from jax import lax
from jax.experimental import pallas as pl
from jax.experimental.pallas import tpu as pltpu
from jax.sharding import PartitionSpec as P

EPSILON = 1e-05
CUBIC = 0.044715
SLOPE = math.sqrt(2.0 / math.pi)
MESH = pl.DeviceIdType.MESH
FIRST_PAIR = 2
D = 1024
HALF = D // 2
MB_ROWS = 32


def kernel(
    down_in, up_in, down_cot, up_cot, w_in, g_in, gw_out, gg_out,
    wv, w, wt, hs, ds, hx, dx, acc, gs, gr, zres, zsend, xs, sl, rinv, do, cot,
    zx_s, zx_r, a1_s, a1_r, b1_s, b1_r, a2_s, a2_r, b2_s, b2_r, a3_s, a3_r, b3_s, b3_r, d_s, d_r,
    fx_s, fx_r, bx_s, bx_r, h_s, h_r, hf_s, u_s, u_r, g_s, g_r, zr_s, zr_r, above, w_sem, in_sem,
):
    sec, dp = lax.axis_index("section"), lax.axis_index("dp")
    z, xh = sec // 2, sec % 2
    y, xl, c = dp // 4, (dp // 2) % 2, dp % 2
    x = xh * 2 + xl
    other = 1 - c

    def at(ax, ay, az, ac):
        return (az * 2 + ax // 2, ay * 4 + (ax % 2) * 2 + ac)

    def xdev(k):
        return at((x + k) % 4, y, z, c)

    def ydev(k):
        return at(x, (y + k) % 4, z, c)

    def zdev(k, core):
        return at(x, y, (z + 8 + k) % 8, core)

    sibling = at(x, y, z, other)
    pair = z >= FIRST_PAIR
    single = z < FIRST_PAIR
    ispair = pair.astype(jnp.int32) if FIRST_PAIR < 8 else 0
    odd = (z % 2) * ispair
    planes = 1 + ispair
    layers = 2 * planes
    slots = 4 // planes
    own_p = odd
    own_l = 2 * own_p + xh
    zpartner = at(x, y, z + 1 - 2 * (z % 2), c)

    load_w = pltpu.make_async_copy(w_in.at[0], wv, w_sem)
    load_w.start()
    barrier = pltpu.get_barrier_semaphore()
    peers = [sibling] + [xdev(k) for k in (1, 2, 3)] + [ydev(k) for k in (1, 2, 3)]
    peers += [at((x + k) % 4, y, z, other) for k in (1, 2, 3)]
    peers += [at(x, (y + k) % 4, z, other) for k in (1, 2, 3)]
    beside = x + 1 - 2 * xl
    peers += [at(beside, (y + k) % 4, z, ac) for k in (1, 2, 3) for ac in (0, 1)]
    for peer in peers:
        pl.semaphore_signal(barrier, inc=1, device_id=peer, device_id_type=MESH)
    for k in (1, 2):

        @pl.when(z + k < 8)
        def _(k=k):
            for core in (c, other):
                pl.semaphore_signal(barrier, inc=1, device_id=zdev(k, core), device_id_type=MESH)

    if FIRST_PAIR < 8:

        @pl.when(pair)
        def _():
            pl.semaphore_signal(barrier, inc=1, device_id=zpartner, device_id_type=MESH)

    def wait_above():
        for k in (1, 2):

            @pl.when(z + k < 8)
            def _(k=k):
                pl.semaphore_wait(above.at[k - 1], 2)

    def send(src, dst, ss, rs, to):
        return pltpu.make_async_remote_copy(
            src_ref=src, dst_ref=dst, send_sem=ss, recv_sem=rs, device_id=to, device_id_type=MESH
        )

    eye = lax.broadcasted_iota(jnp.int32, (64, 64), 0) == lax.broadcasted_iota(jnp.int32, (64, 64), 1)
    gain_col = jnp.sum(jnp.where(eye, g_in[...].astype(jnp.float32), 0.0), axis=1, keepdims=True)
    load_w.wait()
    w[own_l, y, xl, c] = (wv[...].astype(jnp.float32) * gain_col).astype(jnp.bfloat16)
    pl.semaphore_wait(barrier, len(peers) + 2 * jnp.minimum(z, 2) + ispair)
    for k in (1, 2):

        @pl.when(z >= k)
        def _(k=k):
            for core in (c, other):
                pl.semaphore_signal(above.at[k - 1], inc=1, device_id=zdev(-k, core), device_id_type=MESH)


    A, B, ALL = pl.ds(0, HALF), pl.ds(HALF, HALF), pl.ds(0, D)

    def blk(p, bx, by, cols):
        return w.at[2 * p + bx // 2, by, bx % 2, c, :, cols]

    def zx():
        ref = w.at[own_l, y, xl, c]
        return send(ref, ref, zx_s, zx_r, zpartner)

    def zx_other():
        ref = w.at[2 * (1 - own_p) + xh, y, xl, c]
        return send(ref, ref, zx_s, zx_r, zpartner)

    def a1(p, k):
        ref = blk(p, x, y, A)
        return send(ref, ref, a1_s.at[p, k - 1], a1_r.at[p, k - 1], xdev(k))

    def b1(p, k):
        ref = blk(p, x, y, B)
        return send(ref, ref, b1_s.at[p, k - 1], b1_r.at[p, k - 1], ydev(k))

    def a2(p, src, k):
        ref = blk(p, (x - src + 4) % 4, y, A)
        return send(ref, ref, a2_s.at[p, src, k // 2], a2_r.at[p, src, k // 2], ydev(k))

    def b2(p, src, k):
        ref = blk(p, x, (y - src + 4) % 4, B)
        return send(ref, ref, b2_s.at[p, src, k // 2], b2_r.at[p, src, k // 2], xdev(k))

    def half_blk(p, bx, by, cols, k):
        return w.at[2 * p + bx // 2, by, bx % 2, c, pl.ds(32 * (k // 2), 32), cols]

    def a3(p, src, k):
        ref = half_blk(p, (x - src + 4) % 4, (y - k + 4) % 4, A, k)
        return send(ref, ref, a3_s.at[p, src, k // 2], a3_r.at[p, src, k // 2], ydev(k))

    def b3(p, src, k):
        ref = half_blk(p, (x - k + 4) % 4, (y - src + 4) % 4, B, k)
        return send(ref, ref, b3_s.at[p, src, k // 2], b3_r.at[p, src, k // 2], xdev(k))

    def a3_wait(p, src, k):
        ref = half_blk(p, (x - src + 4) % 4, (y + 2) % 4, A, k)
        return send(ref, ref, a3_s.at[p, src, k // 2], a3_r.at[p, src, k // 2], sibling)

    def b3_wait(p, src, k):
        ref = half_blk(p, (x + 2) % 4, (y - src + 4) % 4, B, k)
        return send(ref, ref, b3_s.at[p, src, k // 2], b3_r.at[p, src, k // 2], sibling)

    def d_a2(p, src, k):
        ref = blk(p, (x - src + 4) % 4, (y - k + 4) % 4, A)
        return send(ref, ref, d_s.at[p, 7 + 2 * src + k // 2], d_r.at[p], sibling)

    def d_b2(p, src, k):
        ref = blk(p, (x - k + 4) % 4, (y - src + 4) % 4, B)
        return send(ref, ref, d_s.at[p, 15 + 2 * src + k // 2], d_r.at[p], sibling)

    def d_a3(p, src, k):
        ref = half_blk(p, (x - src + 4) % 4, (y + 2) % 4, A, k)
        return send(ref, ref, d_s.at[p, 23 + 2 * src + k // 2], d_r.at[p], sibling)

    def d_b3(p, src, k):
        ref = half_blk(p, (x + 2) % 4, (y - src + 4) % 4, B, k)
        return send(ref, ref, d_s.at[p, 31 + 2 * src + k // 2], d_r.at[p], sibling)

    def a2_wait(p, src, k):
        ref = blk(p, (x - src + 4) % 4, (y - k + 4) % 4, A)
        return send(ref, ref, a2_s.at[p, src, k // 2], a2_r.at[p, src, k // 2], sibling)

    def b2_wait(p, src, k):
        ref = blk(p, (x - k + 4) % 4, (y - src + 4) % 4, B)
        return send(ref, ref, b2_s.at[p, src, k // 2], b2_r.at[p, src, k // 2], sibling)

    def d_own(p):
        ref = blk(p, x, y, ALL)
        return send(ref, ref, d_s.at[p, 0], d_r.at[p], sibling)

    def d_a1(p, k):
        ref = blk(p, (x - k + 4) % 4, y, A)
        return send(ref, ref, d_s.at[p, k], d_r.at[p], sibling)

    def d_b1(p, k):
        ref = blk(p, x, (y - k + 4) % 4, B)
        return send(ref, ref, d_s.at[p, 3 + k], d_r.at[p], sibling)

    def d_wait(p):
        ref = w.at[pl.ds(2 * p, 2), :, :, other]
        return send(ref, ref, d_s.at[p, 0], d_r.at[p], sibling)

    K, N = (1, 2, 3), (1, 3)
    if FIRST_PAIR < 8:

        @pl.when(pair)
        def _():
            zx().start()

    def gather_start(i, carry):
        p = (own_p + i) % planes

        @pl.when(i > 0)
        def _():
            zx_other().wait_recv()

        d_own(p).start()
        for k in (1, 3):
            a1(p, k).start()
            b1(p, k).start()
        a1(p, 2).start()
        b1(p, 2).start()
        for k in N:
            a2(p, 0, k).start()
            b2(p, 0, k).start()
        return carry

    def onward(p, src):
        a1(p, src).wait_recv()
        for k in N:
            a2(p, src, k).start()
        d_a1(p, src).start()
        b1(p, src).wait_recv()
        for k in N:
            b2(p, src, k).start()
        d_b1(p, src).start()

    def arrived(p, src):
        for k in N:
            a2_wait(p, src, k).wait_recv()
            a3(p, src, k).start()
            d_a2(p, src, k).start()
            b2_wait(p, src, k).wait_recv()
            b3(p, src, k).start()
            d_b2(p, src, k).start()

    def far_side(p, src):
        for k in N:
            a3_wait(p, src, k).wait_recv()
            d_a3(p, src, k).start()
            b3_wait(p, src, k).wait_recv()
            d_b3(p, src, k).start()

    def gather_mid(i, carry):
        p = (own_p + i) % planes
        for src in (1, 3, 2):
            onward(p, src)
        arrived(p, 0)
        return carry

    def gather_end(i, carry):
        p = (own_p + i) % planes
        arrived(p, 1)
        arrived(p, 3)
        far_side(p, 0)
        arrived(p, 2)
        far_side(p, 1)
        far_side(p, 3)
        far_side(p, 2)
        return carry

    def gather_wait(i, carry):
        d_wait((own_p + i) % planes).wait_recv()
        return carry

    lax.fori_loop(0, planes, gather_start, 0)

    first = z < (2 if FIRST_PAIR == 0 else 1)
    last = z >= (7 if FIRST_PAIR == 8 else 6)

    def rows_in(ref, dst, slot, j):
        rows = pl.ds(pl.multiple_of((j % 2) * MB_ROWS, MB_ROWS), MB_ROWS)
        return pltpu.make_async_copy(ref.at[j // 2, rows, :], dst.at[slot], in_sem.at[slot])

    def load_rows(dst, down, up):
        def one(slot, carry):
            j = slot * planes + odd
            for ref, cond in ((down, xh == 0), (up, xh == 1)):

                @pl.when(cond)
                def _(ref=ref):
                    rows_in(ref, dst, slot, j).start()

            return carry

        lax.fori_loop(0, slots, one, 0)

    @pl.when(first)
    def _():
        load_rows(xs.at[0], down_in, up_in)

    @pl.when(last)
    def _():
        load_rows(cot, down_cot, up_cot)

    lax.fori_loop(0, planes, gather_mid, 0)
    lax.fori_loop(0, planes, gather_end, 0)
    lax.fori_loop(0, planes, gather_wait, 0)

    def changes(*planes_below):
        hit = sum((z == low).astype(jnp.int32) for low in planes_below)
        return c + hit * (1 - 2 * c)

    up_core = changes(0, 2, 3)
    down_core = changes(1, 4, 5)
    to_pair = (z == FIRST_PAIR - 1).astype(jnp.int32)
    from_pair = ((z // 2) * 2 == FIRST_PAIR).astype(jnp.int32)

    def f_route(j):
        step = ispair * 2 + (1 - ispair) * (1 + to_pair * (j % 2))
        slot = j - to_pair * (j - j // 2)
        return zdev(step, up_core), slot

    def b_route(j):
        step = ispair * (2 + from_pair * (odd - 1)) + (1 - ispair)
        slot = j + from_pair * (j + odd)
        return zdev(-step, down_core), slot

    def fx(j):
        to, slot = f_route(j)
        return send(xs.at[layers, j], xs.at[0, slot], fx_s.at[j], fx_r.at[slot], to)

    def fx_wait(j):
        return send(xs.at[layers, j], xs.at[0, j], fx_s.at[j], fx_r.at[j], sibling)

    def bx(j):
        to, slot = b_route(j)
        return send(do.at[j], cot.at[slot], bx_s.at[j], bx_r.at[slot], to)

    def bx_wait(j):
        return send(do.at[j], cot.at[j], bx_s.at[j], bx_r.at[j], sibling)

    me8 = x * 2 + c

    quarter = 2 * xl + c
    WIDE = D // 4

    def mb_rows(j):
        return pl.ds(pl.multiple_of(j * MB_ROWS, MB_ROWS), MB_ROWS)

    def share_h(l, j, t):
        to_x = 2 * (l % 2) + t
        near = (to_x == x).astype(jnp.int32)
        core = c + near * (1 - 2 * c)
        return send(
            hs.at[l, mb_rows(j), :], hx.at[l // 2, j, me8], h_s.at[l * slots + j, t], h_r.at[l // 2, j, me8],
            at(to_x, y, z, core),
        )

    def hand_h(p, j, k):
        src = ((x + k) % 4) * 2 + c
        ref = hx.at[p, j, src]
        return send(ref, ref, hf_s.at[p, j, k - 1], h_r.at[p, j, src], sibling)

    def hand_over(p):
        def one(j, carry):
            for k in K:
                hand_h(p, j, k).wait_recv()
                hand_h(p, j, k).start()
            return carry

        lax.fori_loop(0, slots, one, 0)

    def share_u(l, j, t, cc):
        return send(
            ds.at[l, 2 * t + cc, mb_rows(j), :], dx.at[l // 2, j, me8], u_s.at[l * slots + j, 2 * t + cc],
            u_r.at[l // 2, j, me8], at(2 * (l % 2) + t, y, z, cc),
        )

    def for_owners(l, act):
        for t in range(2):
            for cc in range(2):

                @pl.when(jnp.logical_or(2 * (l % 2) + t != x, cc != c))
                def _(t=t, cc=cc):
                    act(t, cc)

    def f32(v):
        return v.astype(jnp.float32)

    def forward_layers(j, count):
        rows = pl.ds(pl.multiple_of(j * MB_ROWS, MB_ROWS), MB_ROWS)
        xf = f32(xs[0, j])
        for l in range(count):
            r = lax.rsqrt(jnp.mean(xf * xf, axis=-1, keepdims=True) + EPSILON)
            normed = (xf * r).astype(jnp.bfloat16)
            u = jnp.dot(normed, w[l].reshape(D, D), preferred_element_type=jnp.float32)
            t = jnp.tanh(SLOPE * (u + CUBIC * (u * u) * u))
            nxt = (xf + 0.5 * u * (1.0 + t)).astype(jnp.bfloat16)
            xs[l + 1, j] = nxt
            xf = f32(nxt)
            sl[l, j] = u
            rinv[l, j] = jnp.broadcast_to(r, (MB_ROWS, 128))
            hs[l, rows, :] = normed

    def forward(j, carry):
        @pl.when(first)
        def _():
            rows_in(down_in, xs.at[0], j, 0).wait()

        @pl.when(jnp.logical_not(first))
        def _():
            fx_wait(j).wait_recv()

        if FIRST_PAIR > 0:

            @pl.when(single)
            def _():
                forward_layers(j, 2)

        if FIRST_PAIR < 8:

            @pl.when(pair)
            def _():
                forward_layers(j, 4)

        fx(j).start()
        return carry

    def slope(u):
        u2 = u * u
        t = jnp.tanh(SLOPE * (u + CUBIC * u2 * u))
        return 0.5 * (1.0 + t) + 0.5 * u * (1.0 - t * t) * SLOPE * (1.0 + 3.0 * CUBIC * u2)

    def slopes(l, carry):
        def one(j, carry):
            sl[l, j] = slope(sl[l, j])
            return carry

        return lax.fori_loop(0, slots, one, carry)

    def turn(l, carry):
        wt[l] = w[l].reshape(D, D).T
        return carry

    def share_all_h(l, carry):
        def one(j, carry):
            for t in range(2):
                share_h(l, j, t).start()
            return carry

        return lax.fori_loop(0, slots, one, carry)

    def drain_gather(i, carry):
        p = (own_p + i) % planes
        for k in K:
            a1(p, k).wait_send()
            b1(p, k).wait_send()
            d_a1(p, k).wait_send()
            d_b1(p, k).wait_send()
        for src in range(4):
            for k in N:
                for copy in (a2, b2, a3, b3, d_a2, d_b2, d_a3, d_b3):
                    copy(p, src, k).wait_send()
        d_own(p).wait_send()
        return carry

    @pl.when(last)
    def _():
        lax.fori_loop(0, layers, turn, 0)

    wait_above()
    @pl.when(jnp.logical_not(last))
    def _():
        lax.fori_loop(0, slots, forward, 0)

    @pl.when(jnp.logical_not(last))
    def _():
        lax.fori_loop(0, layers, share_all_h, 0)
        lax.fori_loop(0, layers, turn, 0)

    @pl.when(jnp.logical_not(last))
    def _():
        lax.fori_loop(0, layers, slopes, 0)
        lax.fori_loop(0, planes, drain_gather, 0)

    if FIRST_PAIR > 0:

        @pl.when(single)
        def _():
            hand_over(0)

    def backward_layers(j, top, bottom, fresh=False):
        rows = pl.ds(pl.multiple_of(j * MB_ROWS, MB_ROWS), MB_ROWS)
        delta = cot[j]
        for l in range(top, bottom - 1, -1):
            df = f32(delta)
            grad = (df * (slope(sl[l, j]) if fresh else sl[l, j])).astype(jnp.bfloat16)
            for q in range(4):
                ds[l, q, rows, :] = grad[:, q * WIDE : (q + 1) * WIDE]
            a = jnp.dot(grad, wt[l], preferred_element_type=jnp.float32)
            r = rinv[l, j][:, 0:1]
            xr = f32(xs[l, j]) * r
            delta = (df + r * (a - xr * jnp.mean(a * xr, axis=-1, keepdims=True))).astype(jnp.bfloat16)
        return delta

    def backward(j, carry):
        bx_wait(j).wait_recv()

        if FIRST_PAIR < 8:

            @pl.when(jnp.logical_and(pair, jnp.logical_not(first)))
            def _():
                do[j] = backward_layers(j, 3, 0)
                bx(j).start()

        if FIRST_PAIR > 0:

            @pl.when(jnp.logical_and(single, jnp.logical_not(first)))
            def _():
                do[j] = backward_layers(j, 1, 0)
                bx(j).start()

        @pl.when(first)
        def _():
            rows = pl.ds(pl.multiple_of(j * MB_ROWS, MB_ROWS), MB_ROWS)
            delta = backward_layers(j, 1 if FIRST_PAIR > 0 else 3, 1)
            grad = (f32(delta) * sl[0, j]).astype(jnp.bfloat16)
            for q in range(4):
                ds[0, q, rows, :] = grad[:, q * WIDE : (q + 1) * WIDE]

        @pl.when(first)
        def _():
            share_all_u(j)

        return carry

    def share_all_u(j):
        def one(l, carry):
            for_owners(l, lambda t, cc: share_u(l, j, t, cc).start())
            return carry

        lax.fori_loop(0, layers, one, 0)

    @pl.when(jnp.logical_not(last))
    def _():
        lax.fori_loop(0, slots, backward, 0)

    def turn_round(j, carry):
        fx_wait(j).wait_recv()
        forward_layers(j, 4)
        rows_in(down_cot, cot, j, 0).wait()
        do[j] = backward_layers(j, 3, 0, fresh=True)
        bx(j).start()
        return carry

    @pl.when(last)
    def _():
        lax.fori_loop(0, slots, turn_round, 0)

    @pl.when(jnp.logical_not(first))
    def _():
        lax.fori_loop(0, slots, lambda j, carry: (share_all_u(j), carry)[1], 0)

    @pl.when(last)
    def _():
        lax.fori_loop(0, layers, share_all_h, 0)

    def gy(p, k, t, cc):
        to_y = (y + k) % 4
        return send(
            gs.at[p, to_y, t, cc], gr.at[p, quarter, k], g_s.at[p, k, 2 * t + cc], g_r.at[p, quarter, k],
            at(2 * xh + t, to_y, z, cc),
        )

    def for_sums(p, act):
        for k in (2, 1, 3, 0):
            for t in range(2):
                for cc in range(2):
                    if k == 0:

                        @pl.when(2 * t + cc != quarter)
                        def _(k=k, t=t, cc=cc):
                            act(p, k, t, cc)

                    else:
                        act(p, k, t, cc)

    def sum_wait(p, k, q):
        return send(gr.at[p, q, k], gr.at[p, q, k], g_s.at[p, k, q], g_r.at[p, q, k], sibling)

    def collect(p):
        l = 2 * p + xh
        acc[...] = jnp.zeros_like(acc)

        def all_h(j, carry):
            hx[p, j, me8] = hs[l, mb_rows(j), :]
            dx[p, j, me8] = ds[l, quarter, mb_rows(j), :]
            for ax in range(4):
                block = hx.at[p, j, 2 * ax + other]
                send(block, block, h_s.at[0, 0], h_r.at[p, j, 2 * ax + other], sibling).wait_recv()
            return carry

        def one(j, carry):
            for src in range(8):

                @pl.when(src != me8)
                def _(src=src):
                    block = dx.at[p, j, src]
                    send(block, block, u_s.at[0, 0], u_r.at[p, j, src], sibling).wait_recv()

            acc[...] += lax.dot_general(
                hx[p, j].reshape(8 * MB_ROWS, D),
                dx[p, j].reshape(8 * MB_ROWS, WIDE),
                (((0,), (0,)), ((), ())),
                preferred_element_type=jnp.float32,
            )
            return carry

        lax.fori_loop(0, slots, all_h, 0)
        lax.fori_loop(0, slots, one, 0)
        gs[p] = acc[...].astype(jnp.bfloat16).reshape(4, 2, 2, 64, WIDE)
        for_sums(p, lambda p, k, t, cc: gy(p, k, t, cc).start())
        gr[p, quarter, 0] = gs[p, y, xl, c]

    def add_up(p, out):
        for q in range(4):
            for k in K:
                sum_wait(p, k, q).wait_recv()

            @pl.when(q != quarter)
            def _(q=q):
                sum_wait(p, 0, q).wait_recv()

            out[:, q * WIDE : (q + 1) * WIDE] = f32(gr[p, q, 0]) + f32(gr[p, q, 1]) + f32(gr[p, q, 2]) + f32(gr[p, q, 3])

    def zr():
        return send(zsend, zres, zr_s, zr_r, zpartner)

    if FIRST_PAIR < 8:

        @pl.when(pair)
        def _():
            hand_over(1 - own_p)
            hand_over(own_p)
            collect(1 - own_p)

    collect(own_p)
    if FIRST_PAIR < 8:

        @pl.when(pair)
        def _():
            add_up(1 - own_p, zsend)
            zr().start()

    if FIRST_PAIR < 8:

        @pl.when(pair)
        def _():
            zx().wait_send()

    @pl.when(last)
    def _():
        lax.fori_loop(0, planes, drain_gather, 0)

    def drain_relay(j, carry):
        @pl.when(jnp.logical_not(last))
        def _():
            fx(j).wait_send()

        @pl.when(jnp.logical_not(first))
        def _():
            bx(j).wait_send()

        return carry

    lax.fori_loop(0, slots, drain_relay, 0)

    def drain_layers(l, carry):
        def drain_rows(j, carry):
            for t in range(2):
                share_h(l, j, t).wait_send()
            for_owners(l, lambda t, cc: share_u(l, j, t, cc).wait_send())
            return carry

        return lax.fori_loop(0, slots, drain_rows, carry)

    lax.fori_loop(0, layers, drain_layers, 0)

    def drain_hand(p, carry):
        def one(j, carry):
            for k in K:
                hand_h(p, j, k).wait_send()
            return carry

        return lax.fori_loop(0, slots, one, carry)

    lax.fori_loop(0, planes, drain_hand, 0)

    def drain_sums(p, carry):
        for_sums(p, lambda p, k, t, cc: gy(p, k, t, cc).wait_send())
        return carry

    add_up(own_p, gw_out.at[0])
    if FIRST_PAIR < 8:

        @pl.when(pair)
        def _():
            zr().wait_recv()
            gw_out[0] = gw_out[0] + zres[...]
            zr().wait_send()

    full = gw_out[0]
    per_row = jnp.sum(full * wv[...].astype(jnp.float32), axis=1, keepdims=True)
    gg_out[...] = jnp.sum(jnp.where(eye, per_row, 0.0), axis=0, keepdims=True)
    gw_out[0] = full * gain_col

    lax.fori_loop(0, planes, drain_sums, 0)


def shards(down_input, up_input, down_cot, up_cot, weight, gain):
    nl = 2 if FIRST_PAIR == 8 else 4
    np_ = nl // 2
    bf, f4 = jnp.bfloat16, jnp.float32
    dma = pltpu.SemaphoreType.DMA
    scratch = [
        pltpu.VMEM((64, D), bf),
        pltpu.VMEM((nl, 4, 2, 2, 64, D), bf),
        pltpu.VMEM((nl, D, D), bf),
        pltpu.VMEM((nl, 4 * MB_ROWS, D), bf),
        pltpu.VMEM((nl, 4, 4 * MB_ROWS, D // 4), bf),
        pltpu.VMEM((np_, 4, 8, MB_ROWS, D), bf),
        pltpu.VMEM((np_, 4, 8, MB_ROWS, D // 4), bf),
        pltpu.VMEM((D, D // 4), f4),
        pltpu.VMEM((np_, 4, 2, 2, 64, D // 4), bf),
        pltpu.VMEM((np_, 4, 4, 64, D // 4), bf),
        pltpu.VMEM((64, D), f4),
        pltpu.VMEM((64, D), f4),
        pltpu.VMEM((nl + 1, 4, MB_ROWS, D), bf),
        pltpu.VMEM((nl, 4, MB_ROWS, D), f4),
        pltpu.VMEM((nl, 4, MB_ROWS, 128), f4),
        pltpu.VMEM((4, MB_ROWS, D), bf),
        pltpu.VMEM((4, MB_ROWS, D), bf),
        dma, dma,
        dma((np_, 3)), dma((np_, 3)), dma((np_, 3)), dma((np_, 3)),
        dma((np_, 4, 2)), dma((np_, 4, 2)), dma((np_, 4, 2)), dma((np_, 4, 2)),
        dma((np_, 4, 2)), dma((np_, 4, 2)), dma((np_, 4, 2)), dma((np_, 4, 2)),
        dma((np_, 39)), dma((np_,)),
        dma((4,)), dma((4,)), dma((4,)), dma((4,)),
        dma((8, 2)), dma((np_, 4, 8)), dma((np_, 4, 3)), dma((8, 4)), dma((np_, 4, 8)),
        dma((np_, 4, 4)), dma((np_, 4, 4)),
        dma, dma,
        pltpu.SemaphoreType.REGULAR((2,)),
        dma, dma((4,)),
    ]
    vmem = pl.BlockSpec(memory_space=pltpu.VMEM)
    return pl.pallas_call(
        kernel,
        out_shape=(
            jax.ShapeDtypeStruct((1, 64, D), f4),
            jax.ShapeDtypeStruct((1, 64), f4),
        ),
        in_specs=[pl.BlockSpec(memory_space=pl.ANY)] * 5 + [vmem],
        out_specs=(vmem, vmem),
        scratch_shapes=scratch,
        compiler_params=pltpu.CompilerParams(
            collective_id=0, has_side_effects=True, vmem_limit_bytes=56 * 1024 * 1024
        ),
    )(down_input, up_input, down_cot, up_cot, weight, gain)


def solution(mesh):
    rows = P(None, "dp", None)
    return jax.shard_map(
        shards,
        mesh=mesh,
        in_specs=(rows, rows, rows, rows, P("section", "dp", None), P("section", "dp")),
        out_specs=(P("section", "dp", None), P("section", "dp")),
        check_vma=False,
    )
```
